32 devices in a mesh: groups: 2 (over y), slab: 4 (over z), tilt: 2 (over x), rep: 2 (over core).
Axes of the slice: x: 2, y: 2, z: 4, core: 2. Of those that a mesh axis runs over, the one named last changes fastest.
Arguments:
- object_slab: bfloat16 [4, 2, 4, 512, 512], P(('groups', 'tilt'), None, None, 'slab'), parts along dimension 0, may hold values from -4 to 4
- probe_field: bfloat16 [2, 128, 128], replicated, may hold values from -6 to 6
- phases: float32 [128], replicated, may hold values from -3.140625 to 3.140625
- cotangent: bfloat16 [4, 32, 2, 128, 128], P(('groups', 'tilt'), ('slab', 'rep')), parts along dimension 0, may hold values from -6 to 6
- positions: int32 [4, 32], P(('groups', 'tilt'), ('slab', 'rep')), parts along dimension 0, may hold values from 0 to 384
- pair_index: int32 [3, 4, 4, 4, 16], P(None, ('groups', 'tilt'), 'slab'), parts along dimension 1, may hold values from 0 to 127, as said below
- pair_counts: int32 [4, 4, 4], P(('groups', 'tilt'), 'slab'), parts along dimension 0, may hold values from 0 to 16, as said below
- row_interp: float32 [8, 16, 16], replicated, may hold values from -0.75 to 0.75
- col_interp: float32 [8, 128, 128], replicated, may hold values from -0.5 to 0.5
Outputs:
- volume_grad: float32 [512, 2, 16, 128], P(('groups', 'slab', 'tilt', 'rep')), parts along dimension 0
The draws below stay inside these ranges and needn't reach their ends.
There are 2 independent parts, one for each index of `groups`. The reference program is written for one: setup_inputs(seed, part) draws one part's arguments, and reference() takes and returns one part's arrays. A program takes and returns all parts, laid end to end along the dimension named above; an argument that names none is the same for every part. Nothing has to cross between parts.
Inputs may be any that keep to these rules, and one draw needn't show every extreme that they name: `pair_index`: component 0 lies below 128, component 1 below 64, component 2 below 8. `pair_counts`: in each angle each source slab has exactly 16 live slots towards one destination slab at most one slab away, 12 to 16 towards every other slab at most three away, and none towards slabs more than three away.
All inputs are finite; a program needn't handle non-finite values.
Results may differ from the reference program's by a relative error of at most 0.015.
Values sent between devices are 32-bit elements; how exact they have to be, the bound alone decides.
No kernel may reach another device: no remote copies, remote signals or barrier semaphores. Data moves between devices by JAX's collectives and lax.ppermute only.
A program may use at most 64 MiB of HBM per device.

```python
import math
import jax
import jax.numpy as jnp
from jax import lax

M = 128
NSL = 4
WCOL = 512
BR = 16
BC = 128
NW = 8
CAP = 16
VB_DEV = 64
SLABS = 4
ANG = 2
ROWS = 512
BAND_WIN = 8
WIN = 32
BLK_BAND = 128
VBLK = 256


def draw_pair_index(key, part):
    key = jax.random.fold_in(key, 11)
    keys = jax.random.split(key, 4)
    shape_full = (ANG, SLABS, SLABS, CAP)
    source_ids = jax.random.randint(keys[0], shape_full, 0, BLK_BAND)
    volume_ids = jax.random.randint(keys[1], shape_full, 0, VB_DEV)
    tile_ids = jax.random.randint(keys[2], shape_full, 0, NW)
    flat_ids = source_ids.reshape(ANG, -1)
    chosen = jax.random.randint(keys[3], (ANG, 1), 0, flat_ids.shape[1])
    spots = jnp.arange(flat_ids.shape[1], dtype=jnp.int32)[None, :]
    flat_ids = jnp.where(spots == chosen, BLK_BAND - 1, flat_ids)
    source_ids = flat_ids.reshape(shape_full)
    return jnp.stack([source_ids, volume_ids, tile_ids]).astype(jnp.int32)


def draw_pair_counts(key, part):
    key = jax.random.fold_in(key, 23)
    keys = jax.random.split(key, 2)
    source_ids = jnp.arange(SLABS, dtype=jnp.int32)[:, None]
    target_ids = jnp.arange(SLABS, dtype=jnp.int32)[None, :]
    nearby = jnp.abs(target_ids - source_ids) <= 3
    counts_base = jax.random.randint(keys[0], (ANG, SLABS, SLABS), 3 * CAP // 4, CAP + 1)
    shifts = jax.random.randint(keys[1], (ANG, SLABS), -1, 2)
    full_target = jnp.clip(source_ids[None, :, 0] + shifts, 0, SLABS - 1)
    counts_all = jnp.where(nearby[None], counts_base, 0)
    counts_all = jnp.where(target_ids[None] == full_target[:, :, None], CAP, counts_all)
    return counts_all.astype(jnp.int32)


def set_ends(array, stream_key, smallest, top_value):
    extent = array.shape
    spot = [jax.random.randint(jax.random.fold_in(stream_key, axis), (), 0, extent[axis]) for axis in range(len(extent))]
    array = array.at[tuple(spot)].set(smallest)
    longest = extent.index(max(extent))
    spot[longest] = (spot[longest] + 1) % extent[longest]
    return array.at[tuple(spot)].set(top_value)


def block_levels(key, extent, pieces, low, top_value):
    loudness, own = 1.0, jax.random.fold_in(key, 6)
    for axis_at, parts in pieces:
        steps = jnp.exp(jax.random.uniform(jax.random.fold_in(own, axis_at), (parts,), jnp.float32, low / len(pieces), top_value / len(pieces)))
        loudness = loudness * jnp.repeat(steps, extent[axis_at] // parts).reshape([-1 if axis == axis_at else 1 for axis in range(len(extent))])
    return loudness


def centred(stream_key, extent, scale, limit, cuts=(), held_as=jnp.bfloat16):
    drawn = scale * jax.random.normal(stream_key, extent, jnp.float32)
    if cuts:
        drawn = drawn * block_levels(stream_key, extent, cuts, -0.22, 0.18)
    return jnp.clip(drawn, -limit, limit).astype(held_as)


def setup_inputs(seed: int = 0, part: int = 0) -> dict:
    seeds = jax.random.split(jax.random.key(seed), 10)
    part_keys = jax.random.split(jax.random.fold_in(seeds[9], part), 10)
    return {
        "object_slab": centred(part_keys[0], (ANG, 2, NSL, ROWS, WCOL), 0.6, 4.0, ((0, 2), (3, 4))),
        "probe_field": centred(seeds[1], (2, M, M), 1.0, 6.0),
        "phases": jnp.clip(jax.random.uniform(seeds[2], (M,), jnp.float32, -3.140625, 3.140625), -3.140625, 3.140625),
        "cotangent": centred(part_keys[3], (ANG, WIN, 2, M, M), 1.0, 6.0, ((0, 2), (1, 8))),
        "positions": set_ends(jax.random.randint(part_keys[4], (ANG, WIN), 0, WCOL - M + 1), jax.random.fold_in(part_keys[4], 1), 0, WCOL - M).astype(jnp.int32),
        "pair_index": draw_pair_index(jax.random.fold_in(jax.random.fold_in(seeds[9], part), 71), part),
        "pair_counts": draw_pair_counts(jax.random.fold_in(jax.random.fold_in(seeds[9], part), 71), part),
        "row_interp": centred(seeds[7], (NW, BR, BR), (4 * BR) ** -0.5, 0.75, (), jnp.float32),
        "col_interp": centred(seeds[8], (NW, BC, BC), BC ** -0.5, 0.5, (), jnp.float32),
    }


def propagators(phases):
    length = phases.shape[0]
    frequency = jnp.arange(length, dtype=jnp.int32)
    products = (frequency[:, None] * frequency[None, :]) % length
    angle_table = products.astype(jnp.float32) * (2.0 * math.pi / length) + phases[:, None]
    kernel_re = jnp.mean(jnp.cos(angle_table), axis=0)
    kernel_im = jnp.mean(jnp.sin(angle_table), axis=0)
    offset = (frequency[:, None] - frequency[None, :]) % length
    real_part = jnp.take(kernel_re, offset).astype(jnp.bfloat16)
    imag_part = jnp.take(kernel_im, offset).astype(jnp.bfloat16)
    forward = jnp.stack([jnp.stack([real_part, -imag_part]), jnp.stack([imag_part, real_part])])
    adjoint = jnp.stack([jnp.stack([real_part.T, imag_part.T]), jnp.stack([-imag_part.T, real_part.T])])
    return forward, adjoint


def apply_left(matrix, source):
    return jnp.einsum("oimk,ikn->omn", matrix.astype(jnp.float32), source.astype(jnp.float32), precision=lax.Precision.HIGHEST)


def apply_right(source, matrix):
    return jnp.einsum("imk,iokn->omn", source.astype(jnp.float32), matrix.astype(jnp.float32), precision=lax.Precision.HIGHEST)


def complex_product(left_field, right_field):
    return jnp.stack([left_field[0] * right_field[0] - left_field[1] * right_field[1], left_field[0] * right_field[1] + left_field[1] * right_field[0]])


def conj_product(left_field, right_field):
    return jnp.stack([left_field[0] * right_field[0] + left_field[1] * right_field[1], left_field[0] * right_field[1] - left_field[1] * right_field[0]])


def window_gradient(window, incoming, probe_field, forward, adjoint):
    slices = window.shape[1]
    field_now = probe_field
    fields_kept = []
    for slice_index in range(slices):
        fields_kept.append(field_now.astype(jnp.float32))
        if slice_index + 1 < slices:
            passed = complex_product(window[:, slice_index].astype(jnp.float32), fields_kept[slice_index]).astype(jnp.bfloat16)
            partial_value = apply_left(forward, passed).astype(jnp.bfloat16)
            field_now = apply_right(partial_value, adjoint).astype(jnp.bfloat16)
    gradients = [None] * slices
    back_field = incoming
    for slice_index in reversed(range(slices)):
        back_wide = back_field.astype(jnp.float32)
        gradients[slice_index] = conj_product(fields_kept[slice_index], back_wide)
        if slice_index > 0:
            turned = conj_product(window[:, slice_index].astype(jnp.float32), back_wide).astype(jnp.bfloat16)
            partial_value = apply_left(adjoint, turned).astype(jnp.bfloat16)
            back_field = apply_right(partial_value, forward).astype(jnp.bfloat16)
    return jnp.stack(gradients, axis=1)


def band_gradient(object_band, cotangent, positions, probe_field, forward, adjoint):
    window_size = probe_field.shape[-1]

    def cut_window(column):
        return lax.dynamic_slice_in_dim(object_band, column, window_size, 3)

    windows = jax.vmap(cut_window)(positions.astype(jnp.int32))
    updates = jax.vmap(lambda window, incoming: window_gradient(window, incoming, probe_field, forward, adjoint))(windows, cotangent)
    initial = jnp.zeros(object_band.shape, jnp.float32)

    def accumulate(counter, running):
        column = positions[counter].astype(jnp.int32)
        current = lax.dynamic_slice_in_dim(running, column, window_size, 3)
        return lax.dynamic_update_slice_in_dim(running, current + updates[counter], column, 3)

    return lax.fori_loop(0, positions.shape[0], accumulate, initial)


def band_blocks(band_grad, block_rows, block_cols):
    parts_count, slices, rows_total, cols_total = band_grad.shape
    shaped = band_grad.reshape(parts_count, slices, rows_total // block_rows, block_rows, cols_total // block_cols, block_cols)
    shaped = shaped.transpose(1, 2, 4, 0, 3, 5)
    return shaped.reshape(-1, parts_count, block_rows, block_cols)


def interpolate(blocks, weights, row_interp, col_interp):
    row_sel = jnp.take(row_interp, weights, axis=0)
    col_sel = jnp.take(col_interp, weights, axis=0)
    inner_term = jnp.einsum("icqk,ikl->icql", blocks, col_sel, precision=lax.Precision.HIGHEST)
    return jnp.einsum("ipq,icql->icpl", row_sel, inner_term, precision=lax.Precision.HIGHEST)


def reference(object_slab, probe_field, phases, cotangent, positions, pair_index, pair_counts, row_interp, col_interp):
    forward, adjoint = propagators(phases)
    block_rows = row_interp.shape[-1]
    block_cols = col_interp.shape[-1]

    def one_angle(volume, packed):
        obj_angle, cot_angle, pos_angle, index_angle, count_angle = packed
        obj_bands = obj_angle.reshape(2, NSL, SLABS, M, WCOL).transpose(2, 0, 1, 3, 4)

        def one_band(band_pack):
            return band_gradient(band_pack[0], band_pack[1], band_pack[2], probe_field, forward, adjoint)

        band_grads = lax.map(one_band, (obj_bands, cot_angle.reshape(SLABS, BAND_WIN, 2, M, M), pos_angle.reshape(SLABS, BAND_WIN)))

        def one_source(volume_now, source_pack):
            band_grad, chosen, counts = source_pack
            blocks = band_blocks(band_grad, block_rows, block_cols)
            picked = jnp.take(blocks, chosen[0].reshape(-1).astype(jnp.int32), axis=0)
            mixed_blocks = interpolate(picked, chosen[2].reshape(-1).astype(jnp.int32), row_interp, col_interp)
            slot_ids = jnp.arange(CAP, dtype=jnp.int32)
            is_live = (slot_ids[None, :] < counts[:, None]).astype(jnp.float32).reshape(-1)
            target = (jnp.arange(SLABS, dtype=jnp.int32)[:, None] * VB_DEV + chosen[1]).reshape(-1).astype(jnp.int32)
            volume_now = volume_now.at[target].add(mixed_blocks * is_live[:, None, None, None])
            return volume_now, None

        volume, unused = lax.scan(one_source, volume, (band_grads, index_angle.transpose(1, 0, 2, 3), count_angle))
        return volume, None

    initial = jnp.zeros((VBLK, 2, block_rows, block_cols), jnp.float32)
    volume, unused = lax.scan(one_angle, initial, (object_slab, cotangent, positions, pair_index.transpose(1, 0, 2, 3, 4), pair_counts))
    return volume
```

```python
import functools
import math

import jax
import jax.numpy as jnp
import numpy as np
from jax import lax
from jax.experimental import pallas as pl
from jax.experimental.pallas import tpu as pltpu
from jax.sharding import PartitionSpec as P

VB_DEV = 64
REACH = 3
HIGH = lax.Precision.HIGHEST
SMEM = pltpu.SMEM
VMEM = pltpu.VMEM


def dot(left, right, precision=None):
    return jnp.dot(left, right, precision=precision, preferred_element_type=jnp.float32)


def slab_shifts(peers):
    if peers <= 2 * REACH + 1:
        return tuple(range(peers))
    return (0,) + tuple(s for k in range(1, REACH + 1) for s in (k, peers - k))


def angle_table(length):
    grid = np.arange(length)
    angles = (grid[:, None] * grid[None, :] % length) * (2.0 * math.pi / length)
    return np.concatenate([np.cos(angles), np.sin(angles)], axis=1).astype(np.float32)


def propagator_blocks(phases, table):
    length = phases.shape[-1]
    row = lax.broadcasted_iota(jnp.int32, (8, length), 0)
    waves = jnp.where(row == 0, jnp.cos(phases), jnp.sin(phases))
    sums = dot(waves, table, HIGH) * (1.0 / length)
    cc, cs = sums[0:1, :length], sums[0:1, length:]
    sc, ss = sums[1:2, :length], sums[1:2, length:]

    def circulant(line):
        wide = jnp.broadcast_to(line, (length, length))
        return pltpu.roll(wide, 0, 1, stride=1, stride_axis=0)

    kr, ki = circulant(cc + ss), circulant(sc - cs)
    krt, kit = circulant(cc - ss), circulant(sc + cs)
    whole = jnp.concatenate(
        [jnp.concatenate([kr, -ki], 1), jnp.concatenate([ki, kr], 1)], 0
    ).astype(jnp.bfloat16)
    turned = jnp.concatenate(
        [jnp.concatenate([krt, kit], 1), jnp.concatenate([-kit, krt], 1)], 0
    ).astype(jnp.bfloat16)
    return whole, turned


def frame_kernel(
    shifts,
    pos_ref,
    index_ref,
    count_ref,
    obj_ref,
    probe_ref,
    cot_ref,
    phase_ref,
    table_ref,
    mine_ref,
    other_ref,
    *rest,
):
    details, band, window = rest[:-2], rest[-2], rest[-1]
    me, core = lax.axis_index("slab"), lax.axis_index("rep")
    peers = lax.axis_size("slab")
    capacity = index_ref.shape[-1]
    for k, shift in enumerate(shifts):
        dest = lax.rem(me + shift, peers)
        live = count_ref[0, 0, dest]
        for slot in range(capacity):
            details[k][0, slot] = jnp.where(slot < live, index_ref[1, 0, 0, dest, slot], VB_DEV)
            details[k][1, slot] = index_ref[2, 0, 0, dest, slot]

    whole, turned = propagator_blocks(phase_ref[...], table_ref[...])
    size = probe_ref.shape[-1]
    _, _, slices, rows, cols = obj_ref.shape
    count = cot_ref.shape[1]
    wide = count * size
    group = 2 if count % 2 == 0 else 1
    f32, bf16 = jnp.float32, jnp.bfloat16

    col_down = lax.broadcasted_iota(jnp.int32, (cols, size), 0)
    lane = lax.broadcasted_iota(jnp.int32, (cols, size), 1)
    cut = jnp.concatenate(
        [(col_down == lane + pos_ref[0, w]).astype(bf16) for w in range(count)], 1
    )
    lane_down = lax.broadcasted_iota(jnp.int32, (size, cols), 0)
    col = lax.broadcasted_iota(jnp.int32, (size, cols), 1)
    paste = jnp.concatenate(
        [(col == lane_down + pos_ref[0, w]).astype(bf16) for w in range(count)], 0
    )

    for s in range(slices):
        source = jnp.concatenate([obj_ref[0, 0, s], obj_ref[0, 1, s]], 0)
        window[s] = dot(source, cut).astype(bf16)

    def tile(s, c, w):
        return window[s, c * rows : (c + 1) * rows, w * size : (w + 1) * size].astype(f32)

    def propagate(fields, first, second):
        result = []
        for g in range(0, count, group):
            stack = jnp.concatenate(
                [jnp.concatenate([fields[w][c] for w in range(g, g + group)], 1) for c in (0, 1)], 0
            )
            part = dot(first, stack).astype(bf16)
            turned_part = jnp.concatenate(
                [
                    jnp.concatenate(
                        [
                            part[c * size : (c + 1) * size, k * size : (k + 1) * size]
                            for c in (0, 1)
                        ],
                        1,
                    )
                    for k in range(group)
                ],
                0,
            )
            done = dot(turned_part, second).astype(bf16)
            for k in range(group):
                result.append(
                    tuple(
                        done[k * size : (k + 1) * size, c * size : (c + 1) * size] for c in (0, 1)
                    )
                )
        return result

    now = [(probe_ref[0], probe_ref[1])] * count
    kept = []
    for s in range(slices):
        kept.append(now)
        if s + 1 < slices:
            passed = []
            for w in range(count):
                o_re, o_im = tile(s, 0, w), tile(s, 1, w)
                p_re, p_im = now[w][0].astype(f32), now[w][1].astype(f32)
                passed.append(
                    (
                        (o_re * p_re - o_im * p_im).astype(bf16),
                        (o_re * p_im + o_im * p_re).astype(bf16),
                    )
                )
            now = propagate(passed, whole, turned)

    block_rows, block_cols = mine_ref.shape[-2:]
    across = cols // block_cols
    back = [(cot_ref[0, w, 0], cot_ref[0, w, 1]) for w in range(count)]
    for s in reversed(range(slices)):
        grads, rhos = [], []
        for w in range(count):
            c_re, c_im = back[w][0].astype(f32), back[w][1].astype(f32)
            p_re, p_im = kept[s][w][0].astype(f32), kept[s][w][1].astype(f32)
            grads.append(
                (
                    (p_re * c_re + p_im * c_im).astype(bf16),
                    (p_re * c_im - p_im * c_re).astype(bf16),
                )
            )
            if s > 0:
                o_re, o_im = tile(s, 0, w), tile(s, 1, w)
                rhos.append(
                    (
                        (o_re * c_re + o_im * c_im).astype(bf16),
                        (o_re * c_im - o_im * c_re).astype(bf16),
                    )
                )
        if s > 0:
            back = propagate(rhos, turned, whole)
        stack = jnp.concatenate(
            [jnp.concatenate([grads[w][c] for w in range(count)], 1) for c in (0, 1)], 0
        )
        spread = dot(stack, paste)
        for c in (0, 1):
            for i in range(rows // block_rows):
                top = c * rows + i * block_rows
                for j in range(across):
                    band[c, (s * (rows // block_rows) + i) * across + j] = spread[
                        top : top + block_rows, j * block_cols : (j + 1) * block_cols
                    ]

    for k, shift in enumerate(shifts):
        dest = lax.rem(me + shift, peers)
        for slot in range(capacity):
            block = index_ref[0, 0, 0, dest, slot]
            mine_ref[k * capacity + slot] = band[core, block]
            other_ref[k * capacity + slot] = band[1 - core, block]


def place_kernel(sources, owners, *refs):
    details, blocks = refs[:sources], refs[sources : 2 * sources]
    row_ref, col_ref = refs[2 * sources : 2 * sources + 2]
    outs = refs[2 * sources + 2 : -2]
    volume, col_bf = refs[-2:]
    f32, bf16 = jnp.float32, jnp.bfloat16
    tiles, block_rows, _ = row_ref.shape
    capacity = blocks[0].shape[0]
    wide = capacity * block_rows
    volume[...] = jnp.zeros_like(volume)
    col_bf[...] = col_ref[...].astype(bf16)
    down = lax.broadcasted_iota(jnp.int32, (block_rows, wide), 0)
    along = lax.broadcasted_iota(jnp.int32, (block_rows, wide), 1)
    repeat = (lax.rem(along, block_rows) == down).astype(bf16)
    row_wide = dot(row_ref[...].reshape(tiles * block_rows, block_rows).astype(bf16), repeat)
    row_scr = row_wide.reshape(tiles, block_rows, wide)
    strip = lax.div(along, block_rows)
    for p in range(sources):
        inner, rows = [], []
        for slot in range(capacity):
            t = details[p][1, slot]
            inner.append(dot(blocks[p][slot].astype(bf16), col_bf[t]).astype(bf16))
            picked = row_scr[0]
            for u in range(1, tiles):
                picked = jnp.where(t == u, row_scr[u], picked)
            rows.append(jnp.where(strip == slot, picked, 0.0).astype(bf16))
        mixed = dot(jnp.concatenate(rows, 0), jnp.concatenate(inner, 0))
        for slot in range(capacity):
            v = details[p][0, slot]
            volume[v] = volume[v] + mixed[slot * block_rows : (slot + 1) * block_rows]
    tilt, core = lax.axis_index("tilt"), lax.axis_index("rep")
    tilts, cores = lax.axis_size("tilt"), lax.axis_size("rep")
    each = VB_DEV // (tilts * cores)
    for out, (dt, dr) in zip(outs, owners):
        owner = lax.rem(tilt + dt, tilts) * cores + lax.rem(core + dr, cores)
        out[...] = volume[pl.ds(owner * each, each)]


def sum_kernel(owners, *refs):
    out_ref = refs[-1]
    core, cores = lax.axis_index("rep"), lax.axis_size("rep")
    for dr in range(cores):
        total = None
        for ref, (_, other) in zip(refs, owners):
            if other == dr:
                total = ref[...] if total is None else total + ref[...]
        out_ref[:, lax.rem(core + dr, cores)] = total


def on_device(
    object_slab,
    probe_field,
    phases,
    cotangent,
    positions,
    pair_index,
    pair_counts,
    row_interp,
    col_interp,
):
    peers = lax.axis_size("slab")
    tilts, cores = lax.axis_size("tilt"), lax.axis_size("rep")
    shifts = slab_shifts(peers)
    capacity = pair_index.shape[-1]
    block_rows, block_cols = row_interp.shape[-1], col_interp.shape[-1]
    _, _, slices, rows, cols = object_slab.shape
    windows, size = cotangent.shape[1], cotangent.shape[-1]
    f32 = jnp.float32
    smem, vmem = pl.BlockSpec(memory_space=SMEM), pl.BlockSpec(memory_space=VMEM)
    block_set = jax.ShapeDtypeStruct((len(shifts) * capacity, block_rows, block_cols), f32)
    detail = jax.ShapeDtypeStruct((2, capacity), jnp.int32)
    big = pltpu.CompilerParams(vmem_limit_bytes=40 * 1024 * 1024)

    mine, other, *details = pl.pallas_call(
        functools.partial(frame_kernel, shifts),
        out_shape=[block_set, block_set] + [detail] * len(shifts),
        in_specs=[smem] * 3 + [vmem] * 5,
        out_specs=[vmem, vmem] + [smem] * len(shifts),
        scratch_shapes=[
            pltpu.VMEM(
                (2, slices * (rows // block_rows) * (cols // block_cols), block_rows, block_cols),
                f32,
            ),
            pltpu.VMEM((slices, 2 * rows, windows * size), jnp.bfloat16),
        ],
        compiler_params=big,
        name="frame",
    )(
        positions,
        pair_index,
        pair_counts,
        object_slab,
        probe_field,
        cotangent,
        phases.reshape(1, -1),
        jnp.asarray(angle_table(size)),
    )

    swap = [(r, (r + 1) % cores) for r in range(cores)]
    got = lax.ppermute(other, "rep", swap)
    blocks, arrived_details = [], []
    for k, shift in enumerate(shifts):
        piece = slice(k * capacity, (k + 1) * capacity)
        summed = mine[piece] + got[piece]
        info = details[k]
        if shift:
            ring = [(p, (p + shift) % peers) for p in range(peers)]
            info = lax.ppermute(info, "slab", ring)
            summed = lax.ppermute(summed, "slab", ring)
        blocks.append(summed)
        arrived_details.append(info)

    owners = [(dt, dr) for dt in range(tilts) for dr in range(cores)]
    each = VB_DEV // len(owners)
    share = jax.ShapeDtypeStruct((each, block_rows, block_cols), f32)
    sources = len(shifts)
    parts = pl.pallas_call(
        functools.partial(place_kernel, sources, owners),
        out_shape=[share] * len(owners),
        in_specs=[smem] * sources + [vmem] * (sources + 2),
        out_specs=[vmem] * len(owners),
        scratch_shapes=[
            pltpu.VMEM((VB_DEV + 1, block_rows, block_cols), f32),
            pltpu.VMEM(col_interp.shape, jnp.bfloat16),
        ],
        compiler_params=big,
        name="place",
    )(*arrived_details, *blocks, row_interp, col_interp)

    arrived = []
    for part, (dt, dr) in zip(parts, owners):
        if dt or dr:
            route = [
                (t * cores + r, (t + dt) % tilts * cores + (r + dr) % cores)
                for t in range(tilts)
                for r in range(cores)
            ]
            part = lax.ppermute(part, ("tilt", "rep"), route)
        arrived.append(part)
    return pl.pallas_call(
        functools.partial(sum_kernel, owners),
        out_shape=jax.ShapeDtypeStruct((each, cores, block_rows, block_cols), f32),
        in_specs=[vmem] * len(owners),
        out_specs=vmem,
        name="total",
    )(*arrived)


def solution(mesh):
    in_specs = (
        P(("groups", "tilt"), None, None, "slab", None),
        P(),
        P(),
        P(("groups", "tilt"), ("slab", "rep"), None, None, None),
        P(("groups", "tilt"), ("slab", "rep")),
        P(None, ("groups", "tilt"), "slab", None, None),
        P(("groups", "tilt"), "slab", None),
        P(),
        P(),
    )
    out_specs = P(("groups", "slab", "tilt", "rep"), None, None, None)
    return jax.shard_map(
        on_device, mesh=mesh, in_specs=in_specs, out_specs=out_specs, check_vma=False
    )
```

```python
import functools
import math

import jax
import jax.numpy as jnp
import numpy as np
from jax import lax
from jax.experimental import pallas as pl
from jax.experimental.pallas import tpu as pltpu
from jax.sharding import PartitionSpec as P

VB_DEV = 64
REACH = 3
CHUNKS = 2
CHUNK_ROWS = 8
HIGH = lax.Precision.HIGHEST
SMEM = pltpu.SMEM
VMEM = pltpu.VMEM


def dot(left, right, precision=None):
    return jnp.dot(left, right, precision=precision, preferred_element_type=jnp.float32)


def slab_shifts(peers):
    if peers <= 2 * REACH + 1:
        return tuple(range(peers))
    return (0,) + tuple(s for k in range(1, REACH + 1) for s in (k, peers - k))


def angle_table(length):
    grid = np.arange(length)
    angles = (grid[:, None] * grid[None, :] % length) * (2.0 * math.pi / length)
    return np.concatenate([np.cos(angles), np.sin(angles)], axis=1).astype(np.float32)


def propagator_blocks(phases, table):
    length = phases.shape[-1]
    row = lax.broadcasted_iota(jnp.int32, (8, length), 0)
    waves = jnp.where(row == 0, jnp.cos(phases), jnp.sin(phases))
    sums = dot(waves, table, HIGH) * (1.0 / length)
    cc, cs = sums[0:1, :length], sums[0:1, length:]
    sc, ss = sums[1:2, :length], sums[1:2, length:]

    def circulant(line):
        wide = jnp.broadcast_to(line, (length, length))
        return pltpu.roll(wide, 0, 1, stride=1, stride_axis=0)

    kr, ki = circulant(cc + ss), circulant(sc - cs)
    krt, kit = circulant(cc - ss), circulant(sc + cs)
    whole = jnp.concatenate(
        [jnp.concatenate([kr, -ki], 1), jnp.concatenate([ki, kr], 1)], 0
    ).astype(jnp.bfloat16)
    turned = jnp.concatenate(
        [jnp.concatenate([krt, kit], 1), jnp.concatenate([-kit, krt], 1)], 0
    ).astype(jnp.bfloat16)
    return whole, turned


def frame_kernel(
    shifts,
    pos_hbm,
    index_hbm,
    count_hbm,
    phase_hbm,
    table_hbm,
    obj_hbm,
    probe_hbm,
    cot_hbm,
    row_hbm,
    col_hbm,
    *rest,
):
    mine, other = rest[: CHUNKS * len(shifts)], rest[CHUNKS * len(shifts)]
    scratch = rest[CHUNKS * len(shifts) + 1 :]
    pos_ref, index_ref, count_ref = scratch[0:3]
    phase_ref, table_ref, obj_ref, probe_ref, cot_ref, row_ref, col_ref = scratch[3:10]
    sems, band, window, col_bf = scratch[10:]
    slices = obj_ref.shape[2]
    copies = [
        pltpu.make_async_copy(src, dst, sems.at[i])
        for i, (src, dst) in enumerate(
            [
                (phase_hbm, phase_ref),
                (table_hbm, table_ref),
                (pos_hbm, pos_ref),
                (probe_hbm, probe_ref),
                (index_hbm, index_ref),
                (count_hbm, count_ref),
                (row_hbm, row_ref),
            ]
        )
    ]
    got_phase, got_table, got_pos, got_probe, got_index, got_count, got_row = copies
    got_obj = [
        pltpu.make_async_copy(obj_hbm.at[0, :, s], obj_ref.at[0, :, s], sems.at[len(copies) + s])
        for s in range(slices)
    ]
    got_cot = pltpu.make_async_copy(cot_hbm, cot_ref, sems.at[len(copies) + slices])
    got_col = pltpu.make_async_copy(col_hbm, col_ref, sems.at[len(copies) + slices + 1])
    for copy in (got_phase, got_table, got_pos, *got_obj, got_probe, got_cot):
        copy.start()
    for copy in (got_index, got_count, got_row, got_col):
        copy.start()

    me, core = lax.axis_index("slab"), lax.axis_index("rep")
    peers = lax.axis_size("slab")
    capacity = index_ref.shape[-1]
    size = probe_ref.shape[-1]
    rows, cols = obj_ref.shape[3:]
    count = cot_ref.shape[1]
    group = 2 if count % 2 == 0 else 1
    f32, bf16 = jnp.float32, jnp.bfloat16

    got_phase.wait()
    got_table.wait()
    whole, turned = propagator_blocks(phase_ref[...], table_ref[...])

    got_pos.wait()
    col_down = lax.broadcasted_iota(jnp.int32, (cols, size), 0)
    lane = lax.broadcasted_iota(jnp.int32, (cols, size), 1)
    cut = jnp.concatenate(
        [(col_down == lane + pos_ref[0, w]).astype(bf16) for w in range(count)], 1
    )
    lane_down = lax.broadcasted_iota(jnp.int32, (size, cols), 0)
    col = lax.broadcasted_iota(jnp.int32, (size, cols), 1)
    paste = jnp.concatenate(
        [(col == lane_down + pos_ref[0, w]).astype(bf16) for w in range(count)], 0
    )

    for s in range(slices):
        got_obj[s].wait()
        source = jnp.concatenate([obj_ref[0, 0, s], obj_ref[0, 1, s]], 0)
        window[s] = dot(source, cut).astype(bf16)

    def tile(s, c, w):
        return window[s, c * rows : (c + 1) * rows, w * size : (w + 1) * size].astype(f32)

    def propagate(fields, first, second):
        result = []
        for g in range(0, count, group):
            stack = jnp.concatenate(
                [jnp.concatenate([fields[w][c] for w in range(g, g + group)], 1) for c in (0, 1)], 0
            )
            part = dot(first, stack).astype(bf16)
            turned_part = jnp.concatenate(
                [
                    jnp.concatenate(
                        [
                            part[c * size : (c + 1) * size, k * size : (k + 1) * size]
                            for c in (0, 1)
                        ],
                        1,
                    )
                    for k in range(group)
                ],
                0,
            )
            done = dot(turned_part, second).astype(bf16)
            for k in range(group):
                result.append(
                    tuple(
                        done[k * size : (k + 1) * size, c * size : (c + 1) * size] for c in (0, 1)
                    )
                )
        return result

    got_probe.wait()
    now = [(probe_ref[0], probe_ref[1])] * count
    kept = []
    for s in range(slices):
        kept.append(now)
        if s + 1 < slices:
            passed = []
            for w in range(count):
                o_re, o_im = tile(s, 0, w), tile(s, 1, w)
                p_re, p_im = now[w][0].astype(f32), now[w][1].astype(f32)
                passed.append(
                    (
                        (o_re * p_re - o_im * p_im).astype(bf16),
                        (o_re * p_im + o_im * p_re).astype(bf16),
                    )
                )
            now = propagate(passed, whole, turned)

    block_rows, block_cols = row_ref.shape[-1], col_ref.shape[-1]
    across = cols // block_cols
    got_cot.wait()
    back = [(cot_ref[0, w, 0], cot_ref[0, w, 1]) for w in range(count)]
    for s in reversed(range(slices)):
        grads, rhos = [], []
        for w in range(count):
            c_re, c_im = back[w][0].astype(f32), back[w][1].astype(f32)
            p_re, p_im = kept[s][w][0].astype(f32), kept[s][w][1].astype(f32)
            grads.append(
                (
                    (p_re * c_re + p_im * c_im).astype(bf16),
                    (p_re * c_im - p_im * c_re).astype(bf16),
                )
            )
            if s > 0:
                o_re, o_im = tile(s, 0, w), tile(s, 1, w)
                rhos.append(
                    (
                        (o_re * c_re + o_im * c_im).astype(bf16),
                        (o_re * c_im - o_im * c_re).astype(bf16),
                    )
                )
        if s > 0:
            back = propagate(rhos, turned, whole)
        stack = jnp.concatenate(
            [jnp.concatenate([grads[w][c] for w in range(count)], 1) for c in (0, 1)], 0
        )
        spread = dot(stack, paste).astype(bf16)
        for c in (0, 1):
            for i in range(rows // block_rows):
                top = c * rows + i * block_rows
                for j in range(across):
                    band[c, (s * (rows // block_rows) + i) * across + j] = spread[
                        top : top + block_rows, j * block_cols : (j + 1) * block_cols
                    ]

    got_row.wait()
    got_col.wait()
    got_index.wait()
    got_count.wait()
    tiles = row_ref.shape[0]
    wide = capacity * block_rows
    col_bf[...] = col_ref[...].astype(bf16)
    down = lax.broadcasted_iota(jnp.int32, (block_rows, wide), 0)
    along = lax.broadcasted_iota(jnp.int32, (block_rows, wide), 1)
    repeat = (lax.rem(along, block_rows) == down).astype(bf16)
    row_wide = dot(row_ref[...].reshape(tiles * block_rows, block_rows).astype(bf16), repeat)
    row_wide = row_wide.reshape(tiles, block_rows, wide)
    strip = lax.div(along, block_rows)
    half = block_rows // CHUNKS
    mark_down = lax.broadcasted_iota(jnp.int32, (half, capacity * half), 0)
    mark_along = lax.broadcasted_iota(jnp.int32, (half, capacity * half), 1)
    mark_slot = jnp.where(lax.rem(mark_along, half) == mark_down, lax.div(mark_along, half), -1)
    starts = np.cumsum([0] + [ref.shape[0] for ref in mine])
    for k, shift in enumerate(shifts):
        dest = lax.rem(me + shift, peers)
        live = count_ref[0, 0, dest]
        inner, picks = [], []
        marks = jnp.full(mark_slot.shape, VB_DEV, jnp.int32)
        for slot in range(capacity):
            block = index_ref[0, 0, 0, dest, slot]
            target = index_ref[1, 0, 0, dest, slot]
            t = index_ref[2, 0, 0, dest, slot]
            target = jnp.where(slot < live, target, VB_DEV)
            marks = jnp.where(mark_slot == slot, target, marks)
            pair = jnp.concatenate([band[core, block], band[1 - core, block]], 0)
            mixed = dot(pair, col_bf[t]).astype(bf16)
            inner.append(jnp.concatenate([mixed[:block_rows], mixed[block_rows:]], 1))
            picked = row_wide[0]
            for u in range(1, tiles):
                picked = jnp.where(t == u, row_wide[u], picked)
            picks.append(jnp.where(strip == slot, picked, 0.0).astype(bf16))
        result = dot(jnp.concatenate(picks, 0), jnp.concatenate(inner, 0))
        for h in range(CHUNKS):
            for slot in range(capacity):
                top = slot * block_rows + h * half
                place = slice(slot * half, (slot + 1) * half)
                mine[h * len(shifts) + k][place] = result[top : top + half, :block_cols]
                begin = starts[h * len(shifts) + k] + slot * half
                other[begin : begin + half] = result[top : top + half, block_cols:]
        tail = capacity * half
        mine[k][tail : tail + half] = marks.astype(f32)
        begin = starts[k] + tail
        other[begin : begin + half] = jnp.zeros(marks.shape, f32)


def place_kernel(sources, owners, first, *refs):
    tilt, core = lax.axis_index("tilt"), lax.axis_index("rep")
    tilts, cores = lax.axis_size("tilt"), lax.axis_size("rep")
    each = VB_DEV // (tilts * cores)
    blocks = refs[:sources]
    half, lanes = CHUNK_ROWS, blocks[0].shape[-1]
    size = each * half
    if first:
        outs, mark_ref = refs[sources:-1], refs[-1]
        for k, block in enumerate(blocks):
            mark_ref[k] = block[lanes:]
    else:
        mark_ref, rest = refs[sources], refs[sources + 1 :]
        before, outs, done = rest[: len(owners)], rest[len(owners) : -1], rest[-1]
        for dr in range(cores):
            parts = [ref[...] for ref, (dt, r) in zip(before, owners) if r == dr]
            if dr:
                outs[dr][:size] = parts.pop(0)
            done[dr] = functools.reduce(jnp.add, parts, jnp.zeros((size, lanes), jnp.float32))
    data = jnp.concatenate([block[:lanes].astype(jnp.bfloat16) for block in blocks], 0)
    volume = lax.broadcasted_iota(jnp.int32, (each, half, lanes), 0).astype(jnp.float32)
    for out, (dt, dr) in zip(outs, owners):
        owner = lax.rem(tilt + dt, tilts) * cores + lax.rem(core + dr, cores)
        base = (owner * each).astype(jnp.float32)
        hot = []
        for k in range(sources):
            mark = mark_ref[k] - base
            hit = jnp.where(volume == mark[None], 1.0, 0.0)
            hot.append(hit.reshape(size, lanes).astype(jnp.bfloat16))
        begin = out.shape[0] - size
        out[begin : begin + size] = dot(jnp.concatenate(hot, 1), data)


def sum_kernel(owners, done_ref, *refs):
    parts, out_ref = refs[:-1], refs[-1]
    core, cores = lax.axis_index("rep"), lax.axis_size("rep")
    each, cols = out_ref.shape[0], out_ref.shape[-1]
    size = each * CHUNK_ROWS
    for dr in range(cores):
        at = lax.rem(core + dr, cores)
        early, late = done_ref[dr], None
        for ref, (dt, r) in zip(parts, owners):
            if r == dr:
                if dr and not dt:
                    early = early + ref[:size]
                value = ref[ref.shape[0] - size :]
                late = value if late is None else late + value
        for h, value in enumerate([early, late]):
            rows = pl.ds(h * CHUNK_ROWS, CHUNK_ROWS)
            out_ref[:, at, rows] = value.reshape(each, CHUNK_ROWS, cols)


def on_device(
    object_slab,
    probe_field,
    phases,
    cotangent,
    positions,
    pair_index,
    pair_counts,
    row_interp,
    col_interp,
):
    peers = lax.axis_size("slab")
    tilts, cores = lax.axis_size("tilt"), lax.axis_size("rep")
    shifts = slab_shifts(peers)
    capacity = pair_index.shape[-1]
    block_rows, block_cols = row_interp.shape[-1], col_interp.shape[-1]
    _, _, slices, rows, cols = object_slab.shape
    windows, size = cotangent.shape[1], cotangent.shape[-1]
    f32, bf16 = jnp.float32, jnp.bfloat16
    hbm, vmem = pl.BlockSpec(memory_space=pltpu.HBM), pl.BlockSpec(memory_space=VMEM)
    limit = pltpu.CompilerParams(vmem_limit_bytes=40 * 1024 * 1024)
    sources = len(shifts)
    lanes = capacity * CHUNK_ROWS

    phase_line = phases.reshape(1, -1)
    table = jnp.asarray(angle_table(size))
    frames = (slices * (rows // block_rows) * (cols // block_cols), block_rows, block_cols)
    marked = jax.ShapeDtypeStruct((lanes + CHUNK_ROWS, block_cols), f32)
    plain = jax.ShapeDtypeStruct((lanes, block_cols), f32)
    shapes = [marked] * sources + [plain] * (sources * (CHUNKS - 1))
    fetched = [
        (phase_line, VMEM),
        (table, VMEM),
        (object_slab, VMEM),
        (probe_field, VMEM),
        (cotangent, VMEM),
        (row_interp, VMEM),
        (col_interp, VMEM),
    ]
    scalars = [positions, pair_index, pair_counts]
    total = sum(shape.shape[0] for shape in shapes)
    *mine, other = pl.pallas_call(
        functools.partial(frame_kernel, shifts),
        out_shape=shapes + [jax.ShapeDtypeStruct((total, block_cols), f32)],
        in_specs=[hbm] * 10,
        out_specs=[vmem] * (len(shapes) + 1),
        scratch_shapes=[SMEM(x.shape, x.dtype) for x in scalars]
        + [space(x.shape, x.dtype) for x, space in fetched]
        + [
            pltpu.SemaphoreType.DMA((9 + slices,)),
            VMEM((2,) + frames, bf16),
            VMEM((slices, 2 * rows, windows * size), bf16),
            VMEM(col_interp.shape, bf16),
        ],
        compiler_params=limit,
        name="frame",
    )(*[pltpu.with_memory_space_constraint(x, pltpu.HBM) for x in scalars + [x for x, _ in fetched]])

    swap = [(r, (r + 1) % cores) for r in range(cores)]
    owners = [(dt, dr) for dt in range(tilts) for dr in range(cores)]
    each = VB_DEV // len(owners)
    share = jax.ShapeDtypeStruct((each * CHUNK_ROWS, block_cols), f32)
    got = lax.ppermute(other, "rep", swap)
    sent, start = [], 0
    for part in mine:
        sent.append(part + got[start : start + part.shape[0]])
        start += part.shape[0]

    mark = jax.ShapeDtypeStruct((sources, CHUNK_ROWS, block_cols), f32)
    double = jax.ShapeDtypeStruct((2 * each * CHUNK_ROWS, block_cols), f32)
    done = jax.ShapeDtypeStruct((cores, each * CHUNK_ROWS, block_cols), f32)
    extra = []
    for h in range(CHUNKS):
        blocks = [None] * sources
        for k in reversed(range(sources)):
            block = sent[h * sources + k]
            if shifts[k]:
                ring = [(p, (p + shifts[k]) % peers) for p in range(peers)]
                block = lax.ppermute(block, "slab", ring)
            blocks[k] = block
        *parts, more = pl.pallas_call(
            functools.partial(place_kernel, sources, owners, h == 0),
            out_shape=[double if h and dr and not dt else share for dt, dr in owners]
            + [done if h else mark],
            in_specs=[vmem] * (sources + len(extra)),
            out_specs=[vmem] * (len(owners) + 1),
            compiler_params=limit,
            name="place",
        )(*blocks, *extra)
        for i, (dt, dr) in enumerate(owners):
            if dt or (dr and h):
                route = [
                    (t * cores + r, (t + dt) % tilts * cores + (r + dr) % cores)
                    for t in range(tilts)
                    for r in range(cores)
                ]
                parts[i] = lax.ppermute(parts[i], ("tilt", "rep"), route)
        extra = [more, *parts]
    return pl.pallas_call(
        functools.partial(sum_kernel, owners),
        out_shape=jax.ShapeDtypeStruct((each, cores, block_rows, block_cols), f32),
        in_specs=[vmem] * len(extra),
        out_specs=vmem,
        compiler_params=limit,
        name="total",
    )(*extra)


def solution(mesh):
    in_specs = (
        P(("groups", "tilt"), None, None, "slab", None),
        P(),
        P(),
        P(("groups", "tilt"), ("slab", "rep"), None, None, None),
        P(("groups", "tilt"), ("slab", "rep")),
        P(None, ("groups", "tilt"), "slab", None, None),
        P(("groups", "tilt"), "slab", None),
        P(),
        P(),
    )
    out_specs = P(("groups", "slab", "tilt", "rep"), None, None, None)
    return jax.shard_map(
        on_device, mesh=mesh, in_specs=in_specs, out_specs=out_specs, check_vma=False
    )
```

```python
import functools
import math

import jax
import jax.numpy as jnp
import numpy as np
from jax import lax
from jax.experimental import pallas as pl
from jax.experimental.pallas import tpu as pltpu
from jax.sharding import PartitionSpec as P

VB_DEV = 64
REACH = 3
CHUNKS = 2
CHUNK_ROWS = 8
HIGH = lax.Precision.HIGHEST
SMEM = pltpu.SMEM
VMEM = pltpu.VMEM


def dot(left, right, precision=None):
    return jnp.dot(left, right, precision=precision, preferred_element_type=jnp.float32)


def slab_shifts(peers):
    if peers <= 2 * REACH + 1:
        return tuple(range(peers))
    return (0,) + tuple(s for k in range(1, REACH + 1) for s in (k, peers - k))


def angle_table(length):
    grid = np.arange(length)
    angles = (grid[:, None] * grid[None, :] % length) * (2.0 * math.pi / length)
    return np.concatenate([np.cos(angles), np.sin(angles)], axis=1).astype(np.float32)


def propagator_blocks(phases, table):
    length = phases.shape[-1]
    row = lax.broadcasted_iota(jnp.int32, (8, length), 0)
    waves = jnp.where(row == 0, jnp.cos(phases), jnp.sin(phases))
    sums = dot(waves, table, HIGH) * (1.0 / length)
    cc, cs = sums[0:1, :length], sums[0:1, length:]
    sc, ss = sums[1:2, :length], sums[1:2, length:]

    def circulant(line):
        wide = jnp.broadcast_to(line, (length, length))
        return pltpu.roll(wide, 0, 1, stride=1, stride_axis=0)

    kr, ki = circulant(cc + ss), circulant(sc - cs)
    krt, kit = circulant(cc - ss), circulant(sc + cs)
    whole = jnp.concatenate(
        [jnp.concatenate([kr, -ki], 1), jnp.concatenate([ki, kr], 1)], 0
    ).astype(jnp.bfloat16)
    turned = jnp.concatenate(
        [jnp.concatenate([krt, kit], 1), jnp.concatenate([-kit, krt], 1)], 0
    ).astype(jnp.bfloat16)
    return whole, turned


def frame_kernel(
    shifts,
    pos_hbm,
    index_hbm,
    count_hbm,
    phase_hbm,
    table_hbm,
    obj_hbm,
    probe_hbm,
    cot_hbm,
    row_hbm,
    col_hbm,
    *rest,
):
    mine, other = rest[: CHUNKS * len(shifts)], rest[CHUNKS * len(shifts)]
    scratch = rest[CHUNKS * len(shifts) + 1 :]
    pos_ref, index_ref, count_ref = scratch[0:3]
    phase_ref, table_ref, obj_ref, probe_ref, cot_ref, row_ref, col_ref = scratch[3:10]
    sems, band, window, col_bf, row_scr = scratch[10:]
    slices = obj_ref.shape[2]
    copies = [
        pltpu.make_async_copy(src, dst, sems.at[i])
        for i, (src, dst) in enumerate(
            [
                (phase_hbm, phase_ref),
                (table_hbm, table_ref),
                (pos_hbm, pos_ref),
                (probe_hbm, probe_ref),
                (index_hbm, index_ref),
                (count_hbm, count_ref),
                (row_hbm, row_ref),
            ]
        )
    ]
    got_phase, got_table, got_pos, got_probe, got_index, got_count, got_row = copies
    got_obj = [
        pltpu.make_async_copy(obj_hbm.at[0, :, s], obj_ref.at[0, :, s], sems.at[len(copies) + s])
        for s in range(slices)
    ]
    got_cot = pltpu.make_async_copy(cot_hbm, cot_ref, sems.at[len(copies) + slices])
    got_col = pltpu.make_async_copy(col_hbm, col_ref, sems.at[len(copies) + slices + 1])
    order = [s for i in range((slices + 1) // 2) for s in sorted({i, slices - 1 - i})]
    for copy in (got_pos, got_phase, got_table, *[got_obj[s] for s in order], got_probe, got_cot):
        copy.start()
    for copy in (got_index, got_count, got_row, got_col):
        copy.start()

    me, core = lax.axis_index("slab"), lax.axis_index("rep")
    peers = lax.axis_size("slab")
    capacity = index_ref.shape[-1]
    size = probe_ref.shape[-1]
    rows, cols = obj_ref.shape[3:]
    count = cot_ref.shape[1]
    group = 2 if count % 2 == 0 else 1
    f32, bf16 = jnp.float32, jnp.bfloat16

    got_pos.wait()
    got_phase.wait()
    got_table.wait()
    col_down = lax.broadcasted_iota(jnp.int32, (cols, size), 0)
    lane = lax.broadcasted_iota(jnp.int32, (cols, size), 1)
    cut = jnp.concatenate(
        [(col_down == lane + pos_ref[0, w]).astype(bf16) for w in range(count)], 1
    )
    whole, turned = propagator_blocks(phase_ref[...], table_ref[...])

    for copy in got_obj:
        copy.wait()
    got_probe.wait()
    got_cot.wait()
    for s in order:
        source = jnp.concatenate([obj_ref[0, 0, s], obj_ref[0, 1, s]], 0)
        window[s] = dot(source, cut).astype(bf16)

    def tile(s, c, w):
        return window[s, c * rows : (c + 1) * rows, w * size : (w + 1) * size]

    def left(fields, matrix):
        parts = []
        for g in range(0, count, group):
            stack = jnp.concatenate(
                [jnp.concatenate([fields[w][c] for w in range(g, g + group)], 1) for c in (0, 1)], 0
            )
            parts.append(dot(matrix, stack).astype(bf16))
        return parts

    def right(parts, matrix):
        result = []
        for part in parts:
            stack = jnp.concatenate(
                [
                    jnp.concatenate(
                        [
                            part[c * size : (c + 1) * size, k * size : (k + 1) * size]
                            for c in (0, 1)
                        ],
                        1,
                    )
                    for k in range(group)
                ],
                0,
            )
            done = dot(stack, matrix).astype(bf16)
            for k in range(group):
                lines = done[k * size : (k + 1) * size]
                result.append((lines[:, :size], lines[:, size:]))
        return result

    def product(one, two, conjugate):
        a_re, a_im = one[0].astype(f32), one[1].astype(f32)
        b_re, b_im = two[0].astype(f32), two[1].astype(f32)
        if conjugate:
            a_im = -a_im
        return (
            (a_re * b_re - a_im * b_im).astype(bf16),
            (a_re * b_im + a_im * b_re).astype(bf16),
        )

    block_rows, block_cols = row_ref.shape[-1], col_ref.shape[-1]
    across = cols // block_cols
    psi, chi = {}, {}
    now = [(probe_ref[0], probe_ref[1])] * count
    back = [(cot_ref[0, w, 0], cot_ref[0, w, 1]) for w in range(count)]
    lane_down = lax.broadcasted_iota(jnp.int32, (size, cols), 0)
    col = lax.broadcasted_iota(jnp.int32, (size, cols), 1)
    paste = jnp.concatenate(
        [(col == lane_down + pos_ref[0, w]).astype(bf16) for w in range(count)], 0
    )
    for i in range(slices):
        s, e = i, slices - 1 - i
        psi[s], chi[e] = now, back
        if i + 1 < slices:
            here = [(tile(s, 0, w), tile(s, 1, w)) for w in range(count)]
            there = [(tile(e, 0, w), tile(e, 1, w)) for w in range(count)]
            passed = [product(here[w], now[w], False) for w in range(count)]
            rho = [product(there[w], back[w], True) for w in range(count)]
            now, back = left(passed, whole), left(rho, turned)
            now, back = right(now, turned), right(back, whole)
        for t in sorted({s, e}):
            if t not in psi or t not in chi or max(t, slices - 1 - t) != i:
                continue
            grads = [product(psi[t][w], chi[t][w], True) for w in range(count)]
            stack = jnp.concatenate(
                [jnp.concatenate([grads[w][c] for w in range(count)], 1) for c in (0, 1)], 0
            )
            spread = dot(stack, paste).astype(bf16)
            for c in (0, 1):
                for k in range(rows // block_rows):
                    top = c * rows + k * block_rows
                    for j in range(across):
                        band[c, (t * (rows // block_rows) + k) * across + j] = spread[
                            top : top + block_rows, j * block_cols : (j + 1) * block_cols
                        ]

    got_row.wait()
    got_col.wait()
    got_index.wait()
    got_count.wait()
    tiles = row_ref.shape[0]
    batch = 8
    wide = batch * block_rows
    col_bf[...] = col_ref[...].astype(bf16)
    down = lax.broadcasted_iota(jnp.int32, (block_rows, wide), 0)
    along = lax.broadcasted_iota(jnp.int32, (block_rows, wide), 1)
    repeat = (lax.rem(along, block_rows) == down).astype(bf16)
    row_wide = dot(row_ref[...].reshape(tiles * block_rows, block_rows).astype(bf16), repeat)
    row_scr[...] = row_wide.reshape(tiles, block_rows, wide)
    strip = lax.div(along, block_rows)
    half = block_rows // CHUNKS
    mark_down = lax.broadcasted_iota(jnp.int32, (half, capacity * half), 0)
    mark_along = lax.broadcasted_iota(jnp.int32, (half, capacity * half), 1)
    mark_slot = jnp.where(lax.rem(mark_along, half) == mark_down, lax.div(mark_along, half), -1)
    starts = np.cumsum([0] + [ref.shape[0] for ref in mine])
    for k, shift in enumerate(shifts):
        dest = lax.rem(me + shift, peers)
        live = count_ref[0, 0, dest]
        marks = jnp.full(mark_slot.shape, VB_DEV, jnp.int32)
        for first in range(0, capacity, batch):
            inner, picks = [], []
            for slot in range(first, first + batch, 2):
                pairs, factors = [], []
                for one in (slot, slot + 1):
                    block = index_ref[0, 0, 0, dest, one]
                    target = index_ref[1, 0, 0, dest, one]
                    t = index_ref[2, 0, 0, dest, one]
                    target = jnp.where(one < live, target, VB_DEV)
                    marks = jnp.where(mark_slot == one, target, marks)
                    pairs += [band[core, block], band[1 - core, block]]
                    factors.append(col_bf[t])
                    picked = jnp.where(strip == one - first, row_scr[t], 0.0)
                    picks.append(picked.astype(bf16))
                mixed = dot(jnp.concatenate(pairs, 0), jnp.concatenate(factors, 1)).astype(bf16)
                for n in (0, 1):
                    lanes = slice(n * block_cols, (n + 1) * block_cols)
                    top = 2 * n * block_rows
                    inner.append(
                        jnp.concatenate(
                            [
                                mixed[top : top + block_rows, lanes],
                                mixed[top + block_rows : top + 2 * block_rows, lanes],
                            ],
                            1,
                        )
                    )
            result = dot(jnp.concatenate(picks, 0), jnp.concatenate(inner, 0))
            for h in range(CHUNKS):
                for slot in range(first, first + batch):
                    top = (slot - first) * block_rows + h * half
                    place = slice(slot * half, (slot + 1) * half)
                    mine[h * len(shifts) + k][place] = result[top : top + half, :block_cols]
                    begin = starts[h * len(shifts) + k] + slot * half
                    other[begin : begin + half] = result[top : top + half, block_cols:]
        tail = capacity * half
        mine[k][tail : tail + half] = marks.astype(f32)
        begin = starts[k] + tail
        other[begin : begin + half] = jnp.zeros(marks.shape, f32)


def place_kernel(sources, owners, first, *refs):
    tilt, core = lax.axis_index("tilt"), lax.axis_index("rep")
    tilts, cores = lax.axis_size("tilt"), lax.axis_size("rep")
    each = VB_DEV // (tilts * cores)
    blocks = refs[sources - 1 :: -1]
    half, lanes = CHUNK_ROWS, blocks[0].shape[-1]
    size = each * half
    if first:
        outs, mark_ref = refs[sources:-1], refs[-1]
        for k, block in enumerate(blocks):
            mark_ref[k] = block[lanes:]
    else:
        mark_ref, rest = refs[sources], refs[sources + 1 :]
        before, outs, done = rest[: len(owners)], rest[len(owners) : -1], rest[-1]
        for dr in range(cores):
            parts = [ref[...] for ref, (dt, r) in zip(before, owners) if r == dr]
            if dr:
                outs[dr][:size] = parts.pop(0)
            done[dr] = functools.reduce(jnp.add, parts, jnp.zeros((size, lanes), jnp.float32))
    data = jnp.concatenate([block[:lanes].astype(jnp.bfloat16) for block in blocks], 0)
    volume = lax.broadcasted_iota(jnp.int32, (each, half, lanes), 0).astype(jnp.float32)
    for out, (dt, dr) in zip(outs, owners):
        owner = lax.rem(tilt + dt, tilts) * cores + lax.rem(core + dr, cores)
        base = (owner * each).astype(jnp.float32)
        hot = []
        for k in range(sources):
            mark = mark_ref[k] - base
            hit = jnp.where(volume == mark[None], 1.0, 0.0)
            hot.append(hit.reshape(size, lanes).astype(jnp.bfloat16))
        begin = out.shape[0] - size
        out[begin : begin + size] = dot(jnp.concatenate(hot, 1), data)


def sum_kernel(owners, done_ref, *refs):
    parts, out_ref = refs[:-1], refs[-1]
    core, cores = lax.axis_index("rep"), lax.axis_size("rep")
    each, cols = out_ref.shape[0], out_ref.shape[-1]
    size = each * CHUNK_ROWS
    for dr in range(cores):
        at = lax.rem(core + dr, cores)
        early, late = done_ref[dr], None
        for ref, (dt, r) in zip(parts, owners):
            if r == dr:
                if dr and not dt:
                    early = early + ref[:size]
                value = ref[ref.shape[0] - size :]
                late = value if late is None else late + value
        for h, value in enumerate([early, late]):
            rows = pl.ds(h * CHUNK_ROWS, CHUNK_ROWS)
            out_ref[:, at, rows] = value.reshape(each, CHUNK_ROWS, cols)


def on_device(
    object_slab,
    probe_field,
    phases,
    cotangent,
    positions,
    pair_index,
    pair_counts,
    row_interp,
    col_interp,
):
    peers = lax.axis_size("slab")
    tilts, cores = lax.axis_size("tilt"), lax.axis_size("rep")
    shifts = slab_shifts(peers)
    capacity = pair_index.shape[-1]
    block_rows, block_cols = row_interp.shape[-1], col_interp.shape[-1]
    _, _, slices, rows, cols = object_slab.shape
    windows, size = cotangent.shape[1], cotangent.shape[-1]
    f32, bf16 = jnp.float32, jnp.bfloat16
    hbm, vmem = pl.BlockSpec(memory_space=pltpu.HBM), pl.BlockSpec(memory_space=VMEM)
    limit = pltpu.CompilerParams(vmem_limit_bytes=40 * 1024 * 1024)
    sources = len(shifts)
    lanes = capacity * CHUNK_ROWS

    phase_line = phases.reshape(1, -1)
    table = jnp.asarray(angle_table(size))
    frames = (slices * (rows // block_rows) * (cols // block_cols), block_rows, block_cols)
    marked = jax.ShapeDtypeStruct((lanes + CHUNK_ROWS, block_cols), f32)
    plain = jax.ShapeDtypeStruct((lanes, block_cols), f32)
    shapes = [marked] * sources + [plain] * (sources * (CHUNKS - 1))
    fetched = [
        (phase_line, VMEM),
        (table, VMEM),
        (object_slab, VMEM),
        (probe_field, VMEM),
        (cotangent, VMEM),
        (row_interp, VMEM),
        (col_interp, VMEM),
    ]
    scalars = [positions, pair_index, pair_counts]
    total = sum(shape.shape[0] for shape in shapes)
    *mine, other = pl.pallas_call(
        functools.partial(frame_kernel, shifts),
        out_shape=shapes + [jax.ShapeDtypeStruct((total, block_cols), f32)],
        in_specs=[hbm] * 10,
        out_specs=[vmem] * (len(shapes) + 1),
        scratch_shapes=[SMEM(x.shape, x.dtype) for x in scalars]
        + [space(x.shape, x.dtype) for x, space in fetched]
        + [
            pltpu.SemaphoreType.DMA((9 + slices,)),
            VMEM((2,) + frames, bf16),
            VMEM((slices, 2 * rows, windows * size), bf16),
            VMEM(col_interp.shape, bf16),
            VMEM((row_interp.shape[0], block_rows, 8 * block_rows), f32),
        ],
        compiler_params=limit,
        name="frame",
    )(*[pltpu.with_memory_space_constraint(x, pltpu.HBM) for x in scalars + [x for x, _ in fetched]])

    swap = [(r, (r + 1) % cores) for r in range(cores)]
    owners = [(dt, dr) for dt in range(tilts) for dr in range(cores)]
    each = VB_DEV // len(owners)
    share = jax.ShapeDtypeStruct((each * CHUNK_ROWS, block_cols), f32)
    got = lax.ppermute(other, "rep", swap)
    sent, start = [], 0
    for part in mine:
        sent.append(part + got[start : start + part.shape[0]])
        start += part.shape[0]

    mark = jax.ShapeDtypeStruct((sources, CHUNK_ROWS, block_cols), f32)
    double = jax.ShapeDtypeStruct((2 * each * CHUNK_ROWS, block_cols), f32)
    done = jax.ShapeDtypeStruct((cores, each * CHUNK_ROWS, block_cols), f32)
    extra = []
    for h in range(CHUNKS):
        blocks = [None] * sources
        for k in reversed(range(sources)):
            block = sent[h * sources + k]
            if shifts[k]:
                ring = [(p, (p + shifts[k]) % peers) for p in range(peers)]
                block = lax.ppermute(block, "slab", ring)
            blocks[k] = block
        *parts, more = pl.pallas_call(
            functools.partial(place_kernel, sources, owners, h == 0),
            out_shape=[double if h and dr and not dt else share for dt, dr in owners]
            + [done if h else mark],
            in_specs=[vmem] * (sources + len(extra)),
            out_specs=[vmem] * (len(owners) + 1),
            compiler_params=limit,
            name="place",
        )(*blocks[::-1], *extra)
        for i, (dt, dr) in enumerate(owners):
            if dt or (dr and h):
                route = [
                    (t * cores + r, (t + dt) % tilts * cores + (r + dr) % cores)
                    for t in range(tilts)
                    for r in range(cores)
                ]
                parts[i] = lax.ppermute(parts[i], ("tilt", "rep"), route)
        extra = [more, *parts]
    return pl.pallas_call(
        functools.partial(sum_kernel, owners),
        out_shape=jax.ShapeDtypeStruct((each, cores, block_rows, block_cols), f32),
        in_specs=[vmem] * len(extra),
        out_specs=vmem,
        compiler_params=limit,
        name="total",
    )(*extra)


def solution(mesh):
    in_specs = (
        P(("groups", "tilt"), None, None, "slab", None),
        P(),
        P(),
        P(("groups", "tilt"), ("slab", "rep"), None, None, None),
        P(("groups", "tilt"), ("slab", "rep")),
        P(None, ("groups", "tilt"), "slab", None, None),
        P(("groups", "tilt"), "slab", None),
        P(),
        P(),
    )
    out_specs = P(("groups", "slab", "tilt", "rep"), None, None, None)
    return jax.shard_map(
        on_device, mesh=mesh, in_specs=in_specs, out_specs=out_specs, check_vma=False
    )
```

```python
import functools
import math

import jax
import jax.numpy as jnp
import numpy as np
from jax import lax
from jax.experimental import pallas as pl
from jax.experimental.pallas import tpu as pltpu
from jax.sharding import PartitionSpec as P

VB_DEV = 64
REACH = 3
CHUNKS = 2
CHUNK_ROWS = 8
HIGH = lax.Precision.HIGHEST
SMEM = pltpu.SMEM
VMEM = pltpu.VMEM


def dot(left, right, precision=None):
    return jnp.dot(left, right, precision=precision, preferred_element_type=jnp.float32)


def slab_steps(peers):
    if peers <= REACH + 1:
        return (0,) + tuple(sorted(range(1, peers), key=lambda k: (k < peers // 2, k)))
    return (0,) + tuple(s for k in range(1, REACH + 1) for s in (k, peers - k))


def partner(slab, step, peers):
    if peers <= REACH + 1 and peers & (peers - 1) == 0:
        return slab ^ step
    return (slab + step) % peers


def angle_table(length):
    grid = np.arange(length)
    angles = (grid[:, None] * grid[None, :] % length) * (2.0 * math.pi / length)
    return np.concatenate([np.cos(angles), np.sin(angles)], axis=1).astype(np.float32)


def propagator_blocks(phases, table):
    length = phases.shape[-1]
    row = lax.broadcasted_iota(jnp.int32, (8, length), 0)
    waves = jnp.where(row == 0, jnp.cos(phases), jnp.sin(phases))
    sums = dot(waves, table, HIGH) * (1.0 / length)
    cc, cs = sums[0:1, :length], sums[0:1, length:]
    sc, ss = sums[1:2, :length], sums[1:2, length:]

    def circulant(line):
        wide = jnp.broadcast_to(line, (length, length))
        return pltpu.roll(wide, 0, 1, stride=1, stride_axis=0)

    kr, ki = circulant(cc + ss), circulant(sc - cs)
    krt, kit = circulant(cc - ss), circulant(sc + cs)
    whole = jnp.concatenate(
        [jnp.concatenate([kr, -ki], 1), jnp.concatenate([ki, kr], 1)], 0
    ).astype(jnp.bfloat16)
    turned = jnp.concatenate(
        [jnp.concatenate([krt, kit], 1), jnp.concatenate([-kit, krt], 1)], 0
    ).astype(jnp.bfloat16)
    return whole, turned


def frame_kernel(
    shifts,
    pos_hbm,
    index_hbm,
    count_hbm,
    phase_hbm,
    table_hbm,
    obj_hbm,
    probe_hbm,
    cot_hbm,
    row_hbm,
    col_hbm,
    *rest,
):
    mine = rest[: CHUNKS * len(shifts)]
    other = rest[CHUNKS * len(shifts) :][:CHUNKS]
    scratch = rest[CHUNKS * (len(shifts) + 1) :]
    pos_ref, index_ref, count_ref = scratch[0:3]
    phase_ref, table_ref, obj_ref, probe_ref, cot_ref, row_ref, col_ref = scratch[3:10]
    sems, band, window, col_bf, row_scr = scratch[10:]
    slices = obj_ref.shape[2]
    copies = [
        pltpu.make_async_copy(src, dst, sems.at[i])
        for i, (src, dst) in enumerate(
            [
                (phase_hbm, phase_ref),
                (table_hbm, table_ref),
                (pos_hbm, pos_ref),
                (probe_hbm, probe_ref),
                (index_hbm, index_ref),
                (count_hbm, count_ref),
                (row_hbm, row_ref),
            ]
        )
    ]
    got_phase, got_table, got_pos, got_probe, got_index, got_count, got_row = copies
    got_obj = [
        pltpu.make_async_copy(obj_hbm.at[0, :, s], obj_ref.at[0, :, s], sems.at[len(copies) + s])
        for s in range(slices)
    ]
    got_cot = pltpu.make_async_copy(cot_hbm, cot_ref, sems.at[len(copies) + slices])
    got_col = pltpu.make_async_copy(col_hbm, col_ref, sems.at[len(copies) + slices + 1])
    order = [s for i in range((slices + 1) // 2) for s in sorted({i, slices - 1 - i})]
    for copy in (got_pos, got_phase, got_table, *[got_obj[s] for s in order], got_probe, got_cot):
        copy.start()
    for copy in (got_index, got_count, got_row, got_col):
        copy.start()

    me, core = lax.axis_index("slab"), lax.axis_index("rep")
    peers = lax.axis_size("slab")
    capacity = index_ref.shape[-1]
    size = probe_ref.shape[-1]
    rows, cols = obj_ref.shape[3:]
    count = cot_ref.shape[1]
    group = 2 if count % 2 == 0 else 1
    f32, bf16 = jnp.float32, jnp.bfloat16

    got_pos.wait()
    got_phase.wait()
    got_table.wait()
    col_down = lax.broadcasted_iota(jnp.int32, (cols, size), 0)
    lane = lax.broadcasted_iota(jnp.int32, (cols, size), 1)
    cut = jnp.concatenate(
        [(col_down == lane + pos_ref[0, w]).astype(bf16) for w in range(count)], 1
    )
    whole, turned = propagator_blocks(phase_ref[...], table_ref[...])

    for copy in got_obj:
        copy.wait()
    got_probe.wait()
    got_cot.wait()
    for s in order:
        source = jnp.concatenate([obj_ref[0, 0, s], obj_ref[0, 1, s]], 0)
        window[s] = dot(source, cut).astype(bf16)

    def tile(s, c, w):
        return window[s, c * rows : (c + 1) * rows, w * size : (w + 1) * size]

    def left(fields, matrix):
        parts = []
        for g in range(0, count, group):
            stack = jnp.concatenate(
                [jnp.concatenate([fields[w][c] for w in range(g, g + group)], 1) for c in (0, 1)], 0
            )
            parts.append(dot(matrix, stack).astype(bf16))
        return parts

    def right(parts, matrix):
        result = []
        for part in parts:
            stack = jnp.concatenate(
                [
                    jnp.concatenate(
                        [
                            part[c * size : (c + 1) * size, k * size : (k + 1) * size]
                            for c in (0, 1)
                        ],
                        1,
                    )
                    for k in range(group)
                ],
                0,
            )
            done = dot(stack, matrix).astype(bf16)
            for k in range(group):
                lines = done[k * size : (k + 1) * size]
                result.append((lines[:, :size], lines[:, size:]))
        return result

    def product(one, two, conjugate):
        a_re, a_im = one[0].astype(f32), one[1].astype(f32)
        b_re, b_im = two[0].astype(f32), two[1].astype(f32)
        if conjugate:
            a_im = -a_im
        return (
            (a_re * b_re - a_im * b_im).astype(bf16),
            (a_re * b_im + a_im * b_re).astype(bf16),
        )

    block_rows, block_cols = row_ref.shape[-1], col_ref.shape[-1]
    across = cols // block_cols
    psi, chi = {}, {}
    now = [(probe_ref[0], probe_ref[1])] * count
    back = [(cot_ref[0, w, 0], cot_ref[0, w, 1]) for w in range(count)]
    lane_down = lax.broadcasted_iota(jnp.int32, (size, cols), 0)
    col = lax.broadcasted_iota(jnp.int32, (size, cols), 1)
    paste = jnp.concatenate(
        [(col == lane_down + pos_ref[0, w]).astype(bf16) for w in range(count)], 0
    )
    for i in range(slices):
        s, e = i, slices - 1 - i
        psi[s], chi[e] = now, back
        if i + 1 < slices:
            here = [(tile(s, 0, w), tile(s, 1, w)) for w in range(count)]
            there = [(tile(e, 0, w), tile(e, 1, w)) for w in range(count)]
            passed = [product(here[w], now[w], False) for w in range(count)]
            rho = [product(there[w], back[w], True) for w in range(count)]
            now, back = left(passed, whole), left(rho, turned)
            now, back = right(now, turned), right(back, whole)
        for t in sorted({s, e}):
            if t not in psi or t not in chi or max(t, slices - 1 - t) != i:
                continue
            grads = [product(psi[t][w], chi[t][w], True) for w in range(count)]
            stack = jnp.concatenate(
                [jnp.concatenate([grads[w][c] for w in range(count)], 1) for c in (0, 1)], 0
            )
            spread = dot(stack, paste).astype(bf16)
            for c in (0, 1):
                for k in range(rows // block_rows):
                    top = c * rows + k * block_rows
                    for j in range(across):
                        band[c, (t * (rows // block_rows) + k) * across + j] = spread[
                            top : top + block_rows, j * block_cols : (j + 1) * block_cols
                        ]

    got_row.wait()
    got_col.wait()
    got_index.wait()
    got_count.wait()
    tiles = row_ref.shape[0]
    batch = 8
    wide = batch * block_rows
    col_bf[...] = col_ref[...].astype(bf16)
    down = lax.broadcasted_iota(jnp.int32, (block_rows, wide), 0)
    along = lax.broadcasted_iota(jnp.int32, (block_rows, wide), 1)
    repeat = (lax.rem(along, block_rows) == down).astype(bf16)
    row_wide = dot(row_ref[...].reshape(tiles * block_rows, block_rows).astype(bf16), repeat)
    row_scr[...] = row_wide.reshape(tiles, block_rows, wide)
    strip = lax.div(along, block_rows)
    half = block_rows // CHUNKS
    mark_down = lax.broadcasted_iota(jnp.int32, (half, capacity * half), 0)
    mark_along = lax.broadcasted_iota(jnp.int32, (half, capacity * half), 1)
    mark_slot = jnp.where(lax.rem(mark_along, half) == mark_down, lax.div(mark_along, half), -1)
    for k, shift in enumerate(shifts):
        dest = partner(me, shift, peers)
        live = count_ref[0, 0, dest]
        marks = jnp.full(mark_slot.shape, VB_DEV, jnp.int32)
        for first in range(0, capacity, batch):
            inner, picks = [], []
            for slot in range(first, first + batch, 2):
                pairs, factors = [], []
                for one in (slot, slot + 1):
                    block = index_ref[0, 0, 0, dest, one]
                    target = index_ref[1, 0, 0, dest, one]
                    t = index_ref[2, 0, 0, dest, one]
                    target = jnp.where(one < live, target, VB_DEV)
                    marks = jnp.where(mark_slot == one, target, marks)
                    pairs += [band[core, block], band[1 - core, block]]
                    factors.append(col_bf[t])
                    picked = jnp.where(strip == one - first, row_scr[t], 0.0)
                    picks.append(picked.astype(bf16))
                mixed = dot(jnp.concatenate(pairs, 0), jnp.concatenate(factors, 1)).astype(bf16)
                for n in (0, 1):
                    lanes = slice(n * block_cols, (n + 1) * block_cols)
                    top = 2 * n * block_rows
                    inner.append(
                        jnp.concatenate(
                            [
                                mixed[top : top + block_rows, lanes],
                                mixed[top + block_rows : top + 2 * block_rows, lanes],
                            ],
                            1,
                        )
                    )
            result = dot(jnp.concatenate(picks, 0), jnp.concatenate(inner, 0))
            for h in range(CHUNKS):
                for slot in range(first, first + batch):
                    top = (slot - first) * block_rows + h * half
                    place = slice(slot * half, (slot + 1) * half)
                    mine[h * len(shifts) + k][place] = result[top : top + half, :block_cols]
                    begin = k * mine[h * len(shifts)].shape[0] + slot * half
                    other[h][begin : begin + half] = result[top : top + half, block_cols:]
        tail = capacity * half
        mine[k][tail : tail + half] = marks.astype(f32)
        begin = k * mine[0].shape[0] + tail
        other[0][begin : begin + half] = jnp.zeros(marks.shape, f32)


def place_kernel(sources, owners, first, *refs):
    tilt, core = lax.axis_index("tilt"), lax.axis_index("rep")
    tilts, cores = lax.axis_size("tilt"), lax.axis_size("rep")
    each = VB_DEV // (tilts * cores)
    blocks = refs[sources - 1 :: -1]
    half, lanes = CHUNK_ROWS, blocks[0].shape[-1]
    size = each * half
    if first:
        outs, mark_ref = refs[sources:-1], refs[-1]
        for k, block in enumerate(blocks):
            mark_ref[k] = block[lanes:]
    else:
        mark_ref, rest = refs[sources], refs[sources + 1 :]
        before, outs, done = rest[: len(owners)], rest[len(owners) : -1], rest[-1]
        for dr in range(cores):
            parts = [ref[...] for ref, (dt, r) in zip(before, owners) if r == dr]
            if dr:
                outs[dr][:size] = parts.pop(0)
            done[dr] = functools.reduce(jnp.add, parts, jnp.zeros((size, lanes), jnp.float32))
    data = jnp.concatenate([block[:lanes].astype(jnp.bfloat16) for block in blocks], 0)
    volume = lax.broadcasted_iota(jnp.int32, (each, half, lanes), 0).astype(jnp.float32)
    for out, (dt, dr) in zip(outs, owners):
        owner = lax.rem(tilt + dt, tilts) * cores + lax.rem(core + dr, cores)
        base = (owner * each).astype(jnp.float32)
        hot = []
        for k in range(sources):
            mark = mark_ref[k] - base
            hit = jnp.where(volume == mark[None], 1.0, 0.0)
            hot.append(hit.reshape(size, lanes).astype(jnp.bfloat16))
        begin = out.shape[0] - size
        out[begin : begin + size] = dot(jnp.concatenate(hot, 1), data)


def sum_kernel(owners, done_ref, *refs):
    parts, out_ref = refs[:-1], refs[-1]
    core, cores = lax.axis_index("rep"), lax.axis_size("rep")
    each, cols = out_ref.shape[0], out_ref.shape[-1]
    size = each * CHUNK_ROWS
    for dr in range(cores):
        at = lax.rem(core + dr, cores)
        early, late = done_ref[dr], None
        for ref, (dt, r) in zip(parts, owners):
            if r == dr:
                if dr and not dt:
                    early = early + ref[:size]
                value = ref[ref.shape[0] - size :]
                late = value if late is None else late + value
        for h, value in enumerate([early, late]):
            rows = pl.ds(h * CHUNK_ROWS, CHUNK_ROWS)
            out_ref[:, at, rows] = value.reshape(each, CHUNK_ROWS, cols)


def on_device(
    object_slab,
    probe_field,
    phases,
    cotangent,
    positions,
    pair_index,
    pair_counts,
    row_interp,
    col_interp,
):
    peers = lax.axis_size("slab")
    tilts, cores = lax.axis_size("tilt"), lax.axis_size("rep")
    shifts = slab_steps(peers)
    capacity = pair_index.shape[-1]
    block_rows, block_cols = row_interp.shape[-1], col_interp.shape[-1]
    _, _, slices, rows, cols = object_slab.shape
    windows, size = cotangent.shape[1], cotangent.shape[-1]
    f32, bf16 = jnp.float32, jnp.bfloat16
    hbm, vmem = pl.BlockSpec(memory_space=pltpu.HBM), pl.BlockSpec(memory_space=VMEM)
    limit = pltpu.CompilerParams(vmem_limit_bytes=40 * 1024 * 1024)
    sources = len(shifts)
    lanes = capacity * CHUNK_ROWS

    phase_line = phases.reshape(1, -1)
    table = jnp.asarray(angle_table(size))
    frames = (slices * (rows // block_rows) * (cols // block_cols), block_rows, block_cols)
    marked = jax.ShapeDtypeStruct((lanes + CHUNK_ROWS, block_cols), f32)
    plain = jax.ShapeDtypeStruct((lanes, block_cols), f32)
    shapes = [marked] * sources + [plain] * (sources * (CHUNKS - 1))
    fetched = [
        (phase_line, VMEM),
        (table, VMEM),
        (object_slab, VMEM),
        (probe_field, VMEM),
        (cotangent, VMEM),
        (row_interp, VMEM),
        (col_interp, VMEM),
    ]
    scalars = [positions, pair_index, pair_counts]
    wholes = [
        jax.ShapeDtypeStruct((sources * shapes[h * sources].shape[0], block_cols), f32)
        for h in range(CHUNKS)
    ]
    held = pl.pallas_call(
        functools.partial(frame_kernel, shifts),
        out_shape=shapes + wholes,
        in_specs=[hbm] * 10,
        out_specs=[vmem] * (len(shapes) + CHUNKS),
        scratch_shapes=[SMEM(x.shape, x.dtype) for x in scalars]
        + [space(x.shape, x.dtype) for x, space in fetched]
        + [
            pltpu.SemaphoreType.DMA((9 + slices,)),
            VMEM((2,) + frames, bf16),
            VMEM((slices, 2 * rows, windows * size), bf16),
            VMEM(col_interp.shape, bf16),
            VMEM((row_interp.shape[0], block_rows, 8 * block_rows), f32),
        ],
        compiler_params=limit,
        name="frame",
    )(*[pltpu.with_memory_space_constraint(x, pltpu.HBM) for x in scalars + [x for x, _ in fetched]])

    swap = [(r, (r + 1) % cores) for r in range(cores)]
    mine, other = held[: len(shapes)], held[len(shapes) :]
    sent = []
    for h in range(CHUNKS):
        got = lax.ppermute(other[h], "rep", swap)
        for k in range(sources):
            part = mine[h * sources + k]
            tall = part.shape[0]
            sent.append(part + got[k * tall : (k + 1) * tall])

    owners = [(dt, dr) for dt in range(tilts) for dr in range(cores)]
    each = VB_DEV // len(owners)
    share = jax.ShapeDtypeStruct((each * CHUNK_ROWS, block_cols), f32)
    mark = jax.ShapeDtypeStruct((sources, CHUNK_ROWS, block_cols), f32)
    double = jax.ShapeDtypeStruct((2 * each * CHUNK_ROWS, block_cols), f32)
    done = jax.ShapeDtypeStruct((cores, each * CHUNK_ROWS, block_cols), f32)
    extra = []
    for h in range(CHUNKS):
        blocks = [None] * sources
        for k in reversed(range(sources)):
            block = sent[h * sources + k]
            if shifts[k]:
                ring = [(p, partner(p, shifts[k], peers)) for p in range(peers)]
                block = lax.ppermute(block, "slab", ring)
            blocks[k] = block
        *parts, more = pl.pallas_call(
            functools.partial(place_kernel, sources, owners, h == 0),
            out_shape=[double if h and dr and not dt else share for dt, dr in owners]
            + [done if h else mark],
            in_specs=[vmem] * (sources + len(extra)),
            out_specs=[vmem] * (len(owners) + 1),
            compiler_params=limit,
            name="place",
        )(*blocks[::-1], *extra)
        for i, (dt, dr) in enumerate(owners):
            if dt or (dr and h):
                route = [
                    (t * cores + r, (t + dt) % tilts * cores + (r + dr) % cores)
                    for t in range(tilts)
                    for r in range(cores)
                ]
                parts[i] = lax.ppermute(parts[i], ("tilt", "rep"), route)
        extra = [more, *parts]
    return pl.pallas_call(
        functools.partial(sum_kernel, owners),
        out_shape=jax.ShapeDtypeStruct((each, cores, block_rows, block_cols), f32),
        in_specs=[vmem] * len(extra),
        out_specs=vmem,
        compiler_params=limit,
        name="total",
    )(*extra)


def solution(mesh):
    in_specs = (
        P(("groups", "tilt"), None, None, "slab", None),
        P(),
        P(),
        P(("groups", "tilt"), ("slab", "rep"), None, None, None),
        P(("groups", "tilt"), ("slab", "rep")),
        P(None, ("groups", "tilt"), "slab", None, None),
        P(("groups", "tilt"), "slab", None),
        P(),
        P(),
    )
    out_specs = P(("groups", "slab", "tilt", "rep"), None, None, None)
    return jax.shard_map(
        on_device, mesh=mesh, in_specs=in_specs, out_specs=out_specs, check_vma=False
    )
```

```python
import functools
import math

import jax
import jax.numpy as jnp
import numpy as np
from jax import lax
from jax.experimental import pallas as pl
from jax.experimental.pallas import tpu as pltpu
from jax.sharding import PartitionSpec as P

VB_DEV = 64
CHUNKS = 2
CHUNK_ROWS = 8
HIGH = lax.Precision.HIGHEST
SMEM = pltpu.SMEM
VMEM = pltpu.VMEM


def dot(left, right, precision=None):
    return jnp.dot(left, right, precision=precision, preferred_element_type=jnp.float32)


def angle_table(length):
    grid = np.arange(length)
    angles = (grid[:, None] * grid[None, :] % length) * (2.0 * math.pi / length)
    return np.concatenate([np.cos(angles), np.sin(angles)], axis=1).astype(np.float32)


def propagator_blocks(phases, table):
    length = phases.shape[-1]
    row = lax.broadcasted_iota(jnp.int32, (8, length), 0)
    waves = jnp.where(row == 0, jnp.cos(phases), jnp.sin(phases))
    sums = dot(waves, table, HIGH) * (1.0 / length)
    cc, cs = sums[0:1, :length], sums[0:1, length:]
    sc, ss = sums[1:2, :length], sums[1:2, length:]

    def circulant(line):
        wide = jnp.broadcast_to(line, (length, length))
        return pltpu.roll(wide, 0, 1, stride=1, stride_axis=0)

    kr, ki = circulant(cc + ss), circulant(sc - cs)
    krt, kit = circulant(cc - ss), circulant(sc + cs)
    whole = jnp.concatenate(
        [jnp.concatenate([kr, -ki], 1), jnp.concatenate([ki, kr], 1)], 0
    ).astype(jnp.bfloat16)
    turned = jnp.concatenate(
        [jnp.concatenate([krt, kit], 1), jnp.concatenate([-kit, krt], 1)], 0
    ).astype(jnp.bfloat16)
    return whole, turned


def frame_kernel(
    peers,
    pos_hbm,
    index_hbm,
    count_hbm,
    phase_hbm,
    table_hbm,
    obj_hbm,
    probe_hbm,
    cot_hbm,
    row_hbm,
    col_hbm,
    *rest,
):
    mine, other, scratch = rest[:CHUNKS], rest[CHUNKS : 2 * CHUNKS], rest[2 * CHUNKS :]
    pos_ref, index_ref, count_ref = scratch[0:3]
    phase_ref, table_ref, obj_ref, probe_ref, cot_ref, row_ref, col_ref = scratch[3:10]
    sems, band, window, col_bf, row_scr = scratch[10:]
    slices = obj_ref.shape[2]
    copies = [
        pltpu.make_async_copy(src, dst, sems.at[i])
        for i, (src, dst) in enumerate(
            [
                (phase_hbm, phase_ref),
                (table_hbm, table_ref),
                (pos_hbm, pos_ref),
                (probe_hbm, probe_ref),
                (index_hbm, index_ref),
                (count_hbm, count_ref),
                (row_hbm, row_ref),
            ]
        )
    ]
    got_phase, got_table, got_pos, got_probe, got_index, got_count, got_row = copies
    got_obj = [
        pltpu.make_async_copy(obj_hbm.at[0, :, s], obj_ref.at[0, :, s], sems.at[len(copies) + s])
        for s in range(slices)
    ]
    got_cot = pltpu.make_async_copy(cot_hbm, cot_ref, sems.at[len(copies) + slices])
    got_col = pltpu.make_async_copy(col_hbm, col_ref, sems.at[len(copies) + slices + 1])
    order = [s for i in range((slices + 1) // 2) for s in sorted({i, slices - 1 - i})]
    for copy in (got_pos, got_phase, got_table, *[got_obj[s] for s in order], got_probe, got_cot):
        copy.start()
    for copy in (got_index, got_count, got_row, got_col):
        copy.start()

    core = lax.axis_index("rep")
    capacity = index_ref.shape[-1]
    size = probe_ref.shape[-1]
    rows, cols = obj_ref.shape[3:]
    count = cot_ref.shape[1]
    group = 2 if count % 2 == 0 else 1
    f32, bf16 = jnp.float32, jnp.bfloat16

    got_pos.wait()
    got_phase.wait()
    got_table.wait()
    col_down = lax.broadcasted_iota(jnp.int32, (cols, size), 0)
    lane = lax.broadcasted_iota(jnp.int32, (cols, size), 1)
    cut = jnp.concatenate(
        [(col_down == lane + pos_ref[0, w]).astype(bf16) for w in range(count)], 1
    )
    whole, turned = propagator_blocks(phase_ref[...], table_ref[...])

    for copy in got_obj:
        copy.wait()
    got_probe.wait()
    got_cot.wait()
    for s in order:
        source = jnp.concatenate([obj_ref[0, 0, s], obj_ref[0, 1, s]], 0)
        window[s] = dot(source, cut).astype(bf16)

    def tile(s, c, w):
        return window[s, c * rows : (c + 1) * rows, w * size : (w + 1) * size]

    def left(fields, matrix):
        parts = []
        for g in range(0, count, group):
            stack = jnp.concatenate(
                [jnp.concatenate([fields[w][c] for w in range(g, g + group)], 1) for c in (0, 1)], 0
            )
            parts.append(dot(matrix, stack).astype(bf16))
        return parts

    def right(parts, matrix):
        result = []
        for part in parts:
            stack = jnp.concatenate(
                [
                    jnp.concatenate(
                        [
                            part[c * size : (c + 1) * size, k * size : (k + 1) * size]
                            for c in (0, 1)
                        ],
                        1,
                    )
                    for k in range(group)
                ],
                0,
            )
            done = dot(stack, matrix).astype(bf16)
            for k in range(group):
                lines = done[k * size : (k + 1) * size]
                result.append((lines[:, :size], lines[:, size:]))
        return result

    def product(one, two, conjugate):
        a_re, a_im = one[0].astype(f32), one[1].astype(f32)
        b_re, b_im = two[0].astype(f32), two[1].astype(f32)
        if conjugate:
            a_im = -a_im
        return (
            (a_re * b_re - a_im * b_im).astype(bf16),
            (a_re * b_im + a_im * b_re).astype(bf16),
        )

    block_rows, block_cols = row_ref.shape[-1], col_ref.shape[-1]
    across = cols // block_cols
    psi, chi = {}, {}
    now = [(probe_ref[0], probe_ref[1])] * count
    back = [(cot_ref[0, w, 0], cot_ref[0, w, 1]) for w in range(count)]
    lane_down = lax.broadcasted_iota(jnp.int32, (size, cols), 0)
    col = lax.broadcasted_iota(jnp.int32, (size, cols), 1)
    paste = jnp.concatenate(
        [(col == lane_down + pos_ref[0, w]).astype(bf16) for w in range(count)], 0
    )
    for i in range(slices):
        s, e = i, slices - 1 - i
        psi[s], chi[e] = now, back
        if i + 1 < slices:
            here = [(tile(s, 0, w), tile(s, 1, w)) for w in range(count)]
            there = [(tile(e, 0, w), tile(e, 1, w)) for w in range(count)]
            passed = [product(here[w], now[w], False) for w in range(count)]
            rho = [product(there[w], back[w], True) for w in range(count)]
            now, back = left(passed, whole), left(rho, turned)
            now, back = right(now, turned), right(back, whole)
        for t in sorted({s, e}):
            if t not in psi or t not in chi or max(t, slices - 1 - t) != i:
                continue
            grads = [product(psi[t][w], chi[t][w], True) for w in range(count)]
            stack = jnp.concatenate(
                [jnp.concatenate([grads[w][c] for w in range(count)], 1) for c in (0, 1)], 0
            )
            spread = dot(stack, paste).astype(bf16)
            for c in (0, 1):
                for k in range(rows // block_rows):
                    top = c * rows + k * block_rows
                    for j in range(across):
                        band[c, (t * (rows // block_rows) + k) * across + j] = spread[
                            top : top + block_rows, j * block_cols : (j + 1) * block_cols
                        ]

    got_row.wait()
    got_col.wait()
    got_index.wait()
    got_count.wait()
    tiles = row_ref.shape[0]
    batch = 8
    wide = batch * block_rows
    col_bf[...] = col_ref[...].astype(bf16)
    down = lax.broadcasted_iota(jnp.int32, (block_rows, wide), 0)
    along = lax.broadcasted_iota(jnp.int32, (block_rows, wide), 1)
    repeat = (lax.rem(along, block_rows) == down).astype(bf16)
    row_wide = dot(row_ref[...].reshape(tiles * block_rows, block_rows).astype(bf16), repeat)
    row_scr[...] = row_wide.reshape(tiles, block_rows, wide)
    strip = lax.div(along, block_rows)
    half = block_rows // CHUNKS
    mark_down = lax.broadcasted_iota(jnp.int32, (half, capacity * half), 0)
    mark_along = lax.broadcasted_iota(jnp.int32, (half, capacity * half), 1)
    mark_slot = jnp.where(lax.rem(mark_along, half) == mark_down, lax.div(mark_along, half), -1)
    for dest in range(peers):
        live = count_ref[0, 0, dest]
        marks = jnp.full(mark_slot.shape, VB_DEV, jnp.int32)
        for first in range(0, capacity, batch):
            inner, picks = [], []
            for slot in range(first, first + batch, 2):
                pairs, factors = [], []
                for one in (slot, slot + 1):
                    block = index_ref[0, 0, 0, dest, one]
                    target = index_ref[1, 0, 0, dest, one]
                    t = index_ref[2, 0, 0, dest, one]
                    target = jnp.where(one < live, target, VB_DEV)
                    marks = jnp.where(mark_slot == one, target, marks)
                    pairs += [band[core, block], band[1 - core, block]]
                    factors.append(col_bf[t])
                    picked = jnp.where(strip == one - first, row_scr[t], 0.0)
                    picks.append(picked.astype(bf16))
                mixed = dot(jnp.concatenate(pairs, 0), jnp.concatenate(factors, 1)).astype(bf16)
                for n in (0, 1):
                    lanes = slice(n * block_cols, (n + 1) * block_cols)
                    top = 2 * n * block_rows
                    inner.append(
                        jnp.concatenate(
                            [
                                mixed[top : top + block_rows, lanes],
                                mixed[top + block_rows : top + 2 * block_rows, lanes],
                            ],
                            1,
                        )
                    )
            result = dot(jnp.concatenate(picks, 0), jnp.concatenate(inner, 0))
            for h in range(CHUNKS):
                for slot in range(first, first + batch):
                    top = (slot - first) * block_rows + h * half
                    place = slice(slot * half, (slot + 1) * half)
                    mine[h][dest, place] = result[top : top + half, :block_cols]
                    other[h][dest, place] = result[top : top + half, block_cols:]
        tail = slice(capacity * half, (capacity + 1) * half)
        mine[0][dest, tail] = marks.astype(f32)
        other[0][dest, tail] = jnp.zeros(marks.shape, f32)


def place_kernel(sources, owners, first, *refs):
    tilt, core = lax.axis_index("tilt"), lax.axis_index("rep")
    tilts, cores = lax.axis_size("tilt"), lax.axis_size("rep")
    each = VB_DEV // (tilts * cores)
    block_ref, refs = refs[0], refs[1:]
    half, lanes = CHUNK_ROWS, block_ref.shape[-1]
    size = each * half
    if first:
        outs, mark_ref = refs[:-1], refs[-1]
        mark_ref[...] = block_ref[:, lanes:]
    else:
        mark_ref, rest = refs[0], refs[1:]
        before, outs, done = rest[: len(owners)], rest[len(owners) : -1], rest[-1]
        for dr in range(cores):
            parts = [ref[...] for ref, (dt, r) in zip(before, owners) if r == dr]
            if dr:
                outs[dr][:size] = parts.pop(0)
            done[dr] = functools.reduce(jnp.add, parts, jnp.zeros((size, lanes), jnp.float32))
    data = block_ref[:, :lanes].astype(jnp.bfloat16).reshape(sources * lanes, -1)
    volume = lax.broadcasted_iota(jnp.int32, (each, half, lanes), 0).astype(jnp.float32)
    for out, (dt, dr) in zip(outs, owners):
        owner = lax.rem(tilt + dt, tilts) * cores + lax.rem(core + dr, cores)
        base = (owner * each).astype(jnp.float32)
        hot = []
        for k in range(sources):
            mark = mark_ref[k] - base
            hit = jnp.where(volume == mark[None], 1.0, 0.0)
            hot.append(hit.reshape(size, lanes).astype(jnp.bfloat16))
        begin = out.shape[0] - size
        out[begin : begin + size] = dot(jnp.concatenate(hot, 1), data)


def sum_kernel(owners, done_ref, *refs):
    parts, out_ref = refs[:-1], refs[-1]
    core, cores = lax.axis_index("rep"), lax.axis_size("rep")
    each, cols = out_ref.shape[0], out_ref.shape[-1]
    size = each * CHUNK_ROWS
    for dr in range(cores):
        at = lax.rem(core + dr, cores)
        early, late = done_ref[dr], None
        for ref, (dt, r) in zip(parts, owners):
            if r == dr:
                if dr and not dt:
                    early = early + ref[:size]
                value = ref[ref.shape[0] - size :]
                late = value if late is None else late + value
        for h, value in enumerate([early, late]):
            rows = pl.ds(h * CHUNK_ROWS, CHUNK_ROWS)
            out_ref[:, at, rows] = value.reshape(each, CHUNK_ROWS, cols)


def on_device(
    object_slab,
    probe_field,
    phases,
    cotangent,
    positions,
    pair_index,
    pair_counts,
    row_interp,
    col_interp,
):
    peers = lax.axis_size("slab")
    tilts, cores = lax.axis_size("tilt"), lax.axis_size("rep")
    capacity = pair_index.shape[-1]
    block_rows, block_cols = row_interp.shape[-1], col_interp.shape[-1]
    _, _, slices, rows, cols = object_slab.shape
    windows, size = cotangent.shape[1], cotangent.shape[-1]
    f32, bf16 = jnp.float32, jnp.bfloat16
    hbm, vmem = pl.BlockSpec(memory_space=pltpu.HBM), pl.BlockSpec(memory_space=VMEM)
    limit = pltpu.CompilerParams(vmem_limit_bytes=40 * 1024 * 1024)
    sources = peers
    lanes = capacity * CHUNK_ROWS

    phase_line = phases.reshape(1, -1)
    table = jnp.asarray(angle_table(size))
    frames = (slices * (rows // block_rows) * (cols // block_cols), block_rows, block_cols)
    shapes = [
        jax.ShapeDtypeStruct((peers, lanes + CHUNK_ROWS * (h == 0), block_cols), f32)
        for h in range(CHUNKS)
    ]
    fetched = [
        (phase_line, VMEM),
        (table, VMEM),
        (object_slab, VMEM),
        (probe_field, VMEM),
        (cotangent, VMEM),
        (row_interp, VMEM),
        (col_interp, VMEM),
    ]
    scalars = [positions, pair_index, pair_counts]
    held = pl.pallas_call(
        functools.partial(frame_kernel, peers),
        out_shape=shapes + shapes,
        in_specs=[hbm] * 10,
        out_specs=[vmem] * (2 * CHUNKS),
        scratch_shapes=[SMEM(x.shape, x.dtype) for x in scalars]
        + [space(x.shape, x.dtype) for x, space in fetched]
        + [
            pltpu.SemaphoreType.DMA((9 + slices,)),
            VMEM((2,) + frames, bf16),
            VMEM((slices, 2 * rows, windows * size), bf16),
            VMEM(col_interp.shape, bf16),
            VMEM((row_interp.shape[0], block_rows, 8 * block_rows), f32),
        ],
        compiler_params=limit,
        name="frame",
    )(*[pltpu.with_memory_space_constraint(x, pltpu.HBM) for x in scalars + [x for x, _ in fetched]])

    swap = [(r, (r + 1) % cores) for r in range(cores)]
    mine, other = held[:CHUNKS], held[CHUNKS:]
    sent = [mine[h] + lax.ppermute(other[h], "rep", swap) for h in range(CHUNKS)]

    owners = [(dt, dr) for dt in range(tilts) for dr in range(cores)]
    each = VB_DEV // len(owners)
    share = jax.ShapeDtypeStruct((each * CHUNK_ROWS, block_cols), f32)
    mark = jax.ShapeDtypeStruct((sources, CHUNK_ROWS, block_cols), f32)
    double = jax.ShapeDtypeStruct((2 * each * CHUNK_ROWS, block_cols), f32)
    done = jax.ShapeDtypeStruct((cores, each * CHUNK_ROWS, block_cols), f32)
    extra = []
    for h in range(CHUNKS):
        blocks = lax.all_to_all(sent[h], "slab", split_axis=0, concat_axis=0, tiled=True)
        *parts, more = pl.pallas_call(
            functools.partial(place_kernel, sources, owners, h == 0),
            out_shape=[double if h and dr and not dt else share for dt, dr in owners]
            + [done if h else mark],
            in_specs=[vmem] * (1 + len(extra)),
            out_specs=[vmem] * (len(owners) + 1),
            compiler_params=limit,
            name="place",
        )(blocks, *extra)
        for i, (dt, dr) in enumerate(owners):
            if dt or (dr and h):
                route = [
                    (t * cores + r, (t + dt) % tilts * cores + (r + dr) % cores)
                    for t in range(tilts)
                    for r in range(cores)
                ]
                parts[i] = lax.ppermute(parts[i], ("tilt", "rep"), route)
        extra = [more, *parts]
    return pl.pallas_call(
        functools.partial(sum_kernel, owners),
        out_shape=jax.ShapeDtypeStruct((each, cores, block_rows, block_cols), f32),
        in_specs=[vmem] * len(extra),
        out_specs=vmem,
        compiler_params=limit,
        name="total",
    )(*extra)


def solution(mesh):
    in_specs = (
        P(("groups", "tilt"), None, None, "slab", None),
        P(),
        P(),
        P(("groups", "tilt"), ("slab", "rep"), None, None, None),
        P(("groups", "tilt"), ("slab", "rep")),
        P(None, ("groups", "tilt"), "slab", None, None),
        P(("groups", "tilt"), "slab", None),
        P(),
        P(),
    )
    out_specs = P(("groups", "slab", "tilt", "rep"), None, None, None)
    return jax.shard_map(
        on_device, mesh=mesh, in_specs=in_specs, out_specs=out_specs, check_vma=False
    )
```

```python
import functools
import math

import jax
import jax.numpy as jnp
import numpy as np
from jax import lax
from jax.experimental import pallas as pl
from jax.experimental.pallas import tpu as pltpu
from jax.sharding import PartitionSpec as P

VB_DEV = 64
REACH = 3
CHUNKS = 2
CHUNK_ROWS = 8
HIGH = lax.Precision.HIGHEST
SMEM = pltpu.SMEM
VMEM = pltpu.VMEM


def dot(left, right, precision=None):
    return jnp.dot(left, right, precision=precision, preferred_element_type=jnp.float32)


def slab_steps(peers):
    if peers <= REACH + 1:
        return tuple(sorted(range(peers), key=lambda k: (k == 0, k < peers // 2, k)))
    ring = [s for k in range(REACH, 0, -1) for s in (peers - k, k)]
    return (*ring, 0)


def partner(slab, step, peers):
    if peers <= REACH + 1 and peers & (peers - 1) == 0:
        return slab ^ step
    return (slab + step) % peers


def angle_table(length):
    grid = np.arange(length)
    angles = (grid[:, None] * grid[None, :] % length) * (2.0 * math.pi / length)
    return np.concatenate([np.cos(angles), np.sin(angles)], axis=1).astype(np.float32)


def propagator_blocks(phases, table):
    length = phases.shape[-1]
    row = lax.broadcasted_iota(jnp.int32, (8, length), 0)
    waves = jnp.where(row == 0, jnp.cos(phases), jnp.sin(phases))
    sums = dot(waves, table, HIGH) * (1.0 / length)
    cc, cs = sums[0:1, :length], sums[0:1, length:]
    sc, ss = sums[1:2, :length], sums[1:2, length:]

    def circulant(line):
        wide = jnp.broadcast_to(line, (length, length))
        return pltpu.roll(wide, 0, 1, stride=1, stride_axis=0)

    kr, ki = circulant(cc + ss), circulant(sc - cs)
    krt, kit = circulant(cc - ss), circulant(sc + cs)
    whole = jnp.concatenate(
        [jnp.concatenate([kr, -ki], 1), jnp.concatenate([ki, kr], 1)], 0
    ).astype(jnp.bfloat16)
    turned = jnp.concatenate(
        [jnp.concatenate([krt, kit], 1), jnp.concatenate([-kit, krt], 1)], 0
    ).astype(jnp.bfloat16)
    return whole, turned


def frame_kernel(
    shifts,
    pos_hbm,
    index_hbm,
    count_hbm,
    phase_hbm,
    table_hbm,
    obj_hbm,
    probe_hbm,
    cot_hbm,
    row_hbm,
    col_hbm,
    *rest,
):
    far, steps = len(shifts) - 2, len(shifts)
    mine, other, scratch = rest[: 2 * steps], rest[2 * steps : 2 * steps + 2], rest[2 * steps + 2 :]
    pos_ref, index_ref, count_ref = scratch[0:3]
    phase_ref, table_ref, obj_ref, probe_ref, cot_ref, row_ref, col_ref = scratch[3:10]
    sems, band, window, col_bf, row_scr = scratch[10:]
    slices = obj_ref.shape[2]
    copies = [
        pltpu.make_async_copy(src, dst, sems.at[i])
        for i, (src, dst) in enumerate(
            [
                (phase_hbm, phase_ref),
                (table_hbm, table_ref),
                (pos_hbm, pos_ref),
                (probe_hbm, probe_ref),
                (index_hbm, index_ref),
                (count_hbm, count_ref),
                (row_hbm, row_ref),
            ]
        )
    ]
    got_phase, got_table, got_pos, got_probe, got_index, got_count, got_row = copies
    got_obj = [
        pltpu.make_async_copy(obj_hbm.at[0, :, s], obj_ref.at[0, :, s], sems.at[len(copies) + s])
        for s in range(slices)
    ]
    got_cot = pltpu.make_async_copy(cot_hbm, cot_ref, sems.at[len(copies) + slices])
    got_col = pltpu.make_async_copy(col_hbm, col_ref, sems.at[len(copies) + slices + 1])
    order = [s for i in range((slices + 1) // 2) for s in sorted({i, slices - 1 - i})]
    for copy in (got_pos, got_phase, got_table, *[got_obj[s] for s in order], got_probe, got_cot):
        copy.start()
    for copy in (got_index, got_count, got_row, got_col):
        copy.start()

    me, core = lax.axis_index("slab"), lax.axis_index("rep")
    peers = lax.axis_size("slab")
    capacity = index_ref.shape[-1]
    size = probe_ref.shape[-1]
    rows, cols = obj_ref.shape[3:]
    count = cot_ref.shape[1]
    group = 2 if count % 2 == 0 else 1
    f32, bf16 = jnp.float32, jnp.bfloat16

    got_pos.wait()
    got_phase.wait()
    got_table.wait()
    col_down = lax.broadcasted_iota(jnp.int32, (cols, size), 0)
    lane = lax.broadcasted_iota(jnp.int32, (cols, size), 1)
    cut = jnp.concatenate(
        [(col_down == lane + pos_ref[0, w]).astype(bf16) for w in range(count)], 1
    )
    whole, turned = propagator_blocks(phase_ref[...], table_ref[...])

    for copy in got_obj:
        copy.wait()
    got_probe.wait()
    got_cot.wait()
    for s in order:
        source = jnp.concatenate([obj_ref[0, 0, s], obj_ref[0, 1, s]], 0)
        window[s] = dot(source, cut).astype(bf16)

    def tile(s, c, w):
        return window[s, c * rows : (c + 1) * rows, w * size : (w + 1) * size]

    def left(fields, matrix):
        parts = []
        for g in range(0, count, group):
            stack = jnp.concatenate(
                [jnp.concatenate([fields[w][c] for w in range(g, g + group)], 1) for c in (0, 1)], 0
            )
            parts.append(dot(matrix, stack).astype(bf16))
        return parts

    def right(parts, matrix):
        result = []
        for part in parts:
            stack = jnp.concatenate(
                [
                    jnp.concatenate(
                        [
                            part[c * size : (c + 1) * size, k * size : (k + 1) * size]
                            for c in (0, 1)
                        ],
                        1,
                    )
                    for k in range(group)
                ],
                0,
            )
            done = dot(stack, matrix).astype(bf16)
            for k in range(group):
                lines = done[k * size : (k + 1) * size]
                result.append((lines[:, :size], lines[:, size:]))
        return result

    def product(one, two, conjugate):
        a_re, a_im = one[0].astype(f32), one[1].astype(f32)
        b_re, b_im = two[0].astype(f32), two[1].astype(f32)
        if conjugate:
            a_im = -a_im
        return (
            (a_re * b_re - a_im * b_im).astype(bf16),
            (a_re * b_im + a_im * b_re).astype(bf16),
        )

    block_rows, block_cols = row_ref.shape[-1], col_ref.shape[-1]
    across = cols // block_cols
    psi, chi = {}, {}
    now = [(probe_ref[0], probe_ref[1])] * count
    back = [(cot_ref[0, w, 0], cot_ref[0, w, 1]) for w in range(count)]
    lane_down = lax.broadcasted_iota(jnp.int32, (size, cols), 0)
    col = lax.broadcasted_iota(jnp.int32, (size, cols), 1)
    paste = jnp.concatenate(
        [(col == lane_down + pos_ref[0, w]).astype(bf16) for w in range(count)], 0
    )
    for i in range(slices):
        s, e = i, slices - 1 - i
        psi[s], chi[e] = now, back
        if i + 1 < slices:
            here = [(tile(s, 0, w), tile(s, 1, w)) for w in range(count)]
            there = [(tile(e, 0, w), tile(e, 1, w)) for w in range(count)]
            passed = [product(here[w], now[w], False) for w in range(count)]
            rho = [product(there[w], back[w], True) for w in range(count)]
            now, back = left(passed, whole), left(rho, turned)
            now, back = right(now, turned), right(back, whole)
        for t in sorted({s, e}):
            if t not in psi or t not in chi or max(t, slices - 1 - t) != i:
                continue
            grads = [product(psi[t][w], chi[t][w], True) for w in range(count)]
            stack = jnp.concatenate(
                [jnp.concatenate([grads[w][c] for w in range(count)], 1) for c in (0, 1)], 0
            )
            spread = dot(stack, paste).astype(bf16)
            for c in (0, 1):
                for k in range(rows // block_rows):
                    top = c * rows + k * block_rows
                    for j in range(across):
                        band[c, (t * (rows // block_rows) + k) * across + j] = spread[
                            top : top + block_rows, j * block_cols : (j + 1) * block_cols
                        ]

    got_row.wait()
    got_col.wait()
    got_index.wait()
    got_count.wait()
    tiles = row_ref.shape[0]
    batch = 8
    wide = batch * block_rows
    col_bf[...] = col_ref[...].astype(bf16)
    down = lax.broadcasted_iota(jnp.int32, (block_rows, wide), 0)
    along = lax.broadcasted_iota(jnp.int32, (block_rows, wide), 1)
    repeat = (lax.rem(along, block_rows) == down).astype(bf16)
    row_wide = dot(row_ref[...].reshape(tiles * block_rows, block_rows).astype(bf16), repeat)
    row_scr[...] = row_wide.reshape(tiles, block_rows, wide)
    strip = lax.div(along, block_rows)
    half = block_rows // CHUNKS
    mark_down = lax.broadcasted_iota(jnp.int32, (half, capacity * half), 0)
    mark_along = lax.broadcasted_iota(jnp.int32, (half, capacity * half), 1)
    mark_slot = jnp.where(lax.rem(mark_along, half) == mark_down, lax.div(mark_along, half), -1)
    lines = capacity * half
    late = (steps - far) * (lines + half)

    def put(k, h, slot, value):
        at = slot * half
        if h:
            swap, base = other[1], late + k * lines
        elif k < far:
            swap, base = other[0], k * (lines + half)
        else:
            swap, base = other[1], (k - far) * (lines + half)
        mine[h * steps + k][at : at + half] = value[:, :block_cols]
        swap[base + at : base + at + half] = value[:, block_cols:]

    for k, shift in enumerate(shifts):
        dest = partner(me, shift, peers)
        live = count_ref[0, 0, dest]
        marks = jnp.full(mark_slot.shape, VB_DEV, jnp.int32)
        for first in range(0, capacity, batch):
            inner, picks = [], []
            for slot in range(first, first + batch, 2):
                pairs, factors = [], []
                for one in (slot, slot + 1):
                    block = index_ref[0, 0, 0, dest, one]
                    target = index_ref[1, 0, 0, dest, one]
                    t = index_ref[2, 0, 0, dest, one]
                    target = jnp.where(one < live, target, VB_DEV)
                    marks = jnp.where(mark_slot == one, target, marks)
                    pairs += [band[core, block], band[1 - core, block]]
                    factors.append(col_bf[t])
                    picked = jnp.where(strip == one - first, row_scr[t], 0.0)
                    picks.append(picked.astype(bf16))
                mixed = dot(jnp.concatenate(pairs, 0), jnp.concatenate(factors, 1)).astype(bf16)
                for n in (0, 1):
                    lanes = slice(n * block_cols, (n + 1) * block_cols)
                    top = 2 * n * block_rows
                    inner.append(
                        jnp.concatenate(
                            [
                                mixed[top : top + block_rows, lanes],
                                mixed[top + block_rows : top + 2 * block_rows, lanes],
                            ],
                            1,
                        )
                    )
            result = dot(jnp.concatenate(picks, 0), jnp.concatenate(inner, 0))
            for slot in range(first, first + batch):
                for h in range(CHUNKS):
                    top = (slot - first) * block_rows + h * half
                    put(k, h, slot, result[top : top + half])
        marks = marks.astype(f32)
        put(k, 0, capacity, jnp.concatenate([marks, jnp.zeros_like(marks)], 1))


def join_kernel(base, first_ref, got_ref, *refs):
    count = len(refs) // 2
    for part, out in zip(refs[:count], refs[count:]):
        tall = part.shape[0]
        out[...] = part[...] + got_ref[base : base + tall]
        base += tall


def place_kernel(sources, owners, first, *refs):
    tilt, core = lax.axis_index("tilt"), lax.axis_index("rep")
    tilts, cores = lax.axis_size("tilt"), lax.axis_size("rep")
    each = VB_DEV // (tilts * cores)
    blocks = refs[:sources]
    half, lanes = CHUNK_ROWS, blocks[0].shape[-1]
    size = each * half
    if first:
        outs, mark_ref = refs[sources:-1], refs[-1]
        for k, block in enumerate(blocks):
            mark_ref[k] = block[lanes:]
    else:
        mark_ref, rest = refs[sources], refs[sources + 1 :]
        before, outs, done = rest[: len(owners)], rest[len(owners) : -1], rest[-1]
        for dr in range(cores):
            parts = [ref[...] for ref, (dt, r) in zip(before, owners) if r == dr]
            done[dr] = functools.reduce(jnp.add, parts)
    data = jnp.concatenate([block[:lanes].astype(jnp.bfloat16) for block in blocks], 0)
    volume = lax.broadcasted_iota(jnp.int32, (each, half, lanes), 0).astype(jnp.float32)
    for out, (dt, dr) in zip(outs, owners):
        owner = lax.rem(tilt + dt, tilts) * cores + lax.rem(core + dr, cores)
        base = (owner * each).astype(jnp.float32)
        hot = []
        for k in range(sources):
            mark = mark_ref[k] - base
            hit = jnp.where(volume == mark[None], 1.0, 0.0)
            hot.append(hit.reshape(size, lanes).astype(jnp.bfloat16))
        out[...] = dot(jnp.concatenate(hot, 1), data)


def sum_kernel(owners, done_ref, *refs):
    parts, out_ref = refs[:-1], refs[-1]
    core, cores = lax.axis_index("rep"), lax.axis_size("rep")
    each, cols = out_ref.shape[0], out_ref.shape[-1]
    for dr in range(cores):
        at = lax.rem(core + dr, cores)
        late = functools.reduce(jnp.add, [ref[...] for ref, (_, r) in zip(parts, owners) if r == dr])
        for h, value in enumerate([done_ref[dr], late]):
            rows = pl.ds(h * CHUNK_ROWS, CHUNK_ROWS)
            out_ref[:, at, rows] = value.reshape(each, CHUNK_ROWS, cols)


def on_device(
    object_slab,
    probe_field,
    phases,
    cotangent,
    positions,
    pair_index,
    pair_counts,
    row_interp,
    col_interp,
):
    peers = lax.axis_size("slab")
    tilts, cores = lax.axis_size("tilt"), lax.axis_size("rep")
    shifts = slab_steps(peers)
    capacity = pair_index.shape[-1]
    block_rows, block_cols = row_interp.shape[-1], col_interp.shape[-1]
    _, _, slices, rows, cols = object_slab.shape
    windows, size = cotangent.shape[1], cotangent.shape[-1]
    f32, bf16 = jnp.float32, jnp.bfloat16
    hbm, vmem = pl.BlockSpec(memory_space=pltpu.HBM), pl.BlockSpec(memory_space=VMEM)
    limit = pltpu.CompilerParams(vmem_limit_bytes=40 * 1024 * 1024)
    sources = len(shifts)
    lanes = capacity * CHUNK_ROWS

    phase_line = phases.reshape(1, -1)
    table = jnp.asarray(angle_table(size))
    frames = (slices * (rows // block_rows) * (cols // block_cols), block_rows, block_cols)
    far = sources - 2
    tall = lanes + CHUNK_ROWS
    heights = [tall] * sources + [lanes] * sources
    swapped = [far * tall, (sources - far) * tall + sources * lanes]
    shapes = [jax.ShapeDtypeStruct((tall, block_cols), f32) for tall in heights + swapped]
    fetched = [
        (phase_line, VMEM),
        (table, VMEM),
        (object_slab, VMEM),
        (probe_field, VMEM),
        (cotangent, VMEM),
        (row_interp, VMEM),
        (col_interp, VMEM),
    ]
    scalars = [positions, pair_index, pair_counts]
    held = pl.pallas_call(
        functools.partial(frame_kernel, shifts),
        out_shape=shapes,
        in_specs=[hbm] * 10,
        out_specs=[vmem] * len(shapes),
        scratch_shapes=[SMEM(x.shape, x.dtype) for x in scalars]
        + [space(x.shape, x.dtype) for x, space in fetched]
        + [
            pltpu.SemaphoreType.DMA((9 + slices,)),
            VMEM((2,) + frames, bf16),
            VMEM((slices, 2 * rows, windows * size), bf16),
            VMEM(col_interp.shape, bf16),
            VMEM((row_interp.shape[0], block_rows, 8 * block_rows), f32),
        ],
        compiler_params=limit,
        name="frame",
    )(*[pltpu.with_memory_space_constraint(x, pltpu.HBM) for x in scalars + [x for x, _ in fetched]])

    swap = [(r, (r + 1) % cores) for r in range(cores)]
    owners = sorted(
        ((dt, dr) for dt in range(tilts) for dr in range(cores)), key=lambda o: (o[0] == 0, o)
    )
    each = VB_DEV // len(owners)
    share = jax.ShapeDtypeStruct((each * CHUNK_ROWS, block_cols), f32)
    mark = jax.ShapeDtypeStruct((sources, CHUNK_ROWS, block_cols), f32)
    done = jax.ShapeDtypeStruct((cores, each * CHUNK_ROWS, block_cols), f32)
    mine, other = held[: len(heights)], held[len(heights) :]
    got = [lax.ppermute(half, "rep", swap) for half in other]

    def send(block, step):
        ring = [(p, partner(p, step, peers)) for p in range(peers)]
        return lax.ppermute(block, "slab", ring)

    first = []
    for k in range(sources):
        h, at = (0, k * tall) if k < far else (1, (k - far) * tall)
        block = mine[k] + got[h][at : at + tall]
        first.append(send(block, shifts[k]) if shifts[k] else block)
    joined = []
    for k in range(far):
        part = slice(k, k + 1) if k + 1 < far else slice(k, sources)
        late = mine[sources:][part]
        joined += pl.pallas_call(
            functools.partial(join_kernel, (sources - far) * tall + k * lanes),
            out_shape=shapes[sources : 2 * sources][part],
            in_specs=[vmem] * (len(late) + 2),
            out_specs=[vmem] * len(late),
            compiler_params=limit,
            name="join",
        )(first[k], got[1], *late)
    second = [send(block, k) if k else block for block, k in zip(joined, shifts)]

    extra = []
    for h, blocks in enumerate([first, second]):
        *parts, more = pl.pallas_call(
            functools.partial(place_kernel, sources, owners, h == 0),
            out_shape=[share] * len(owners) + [done if h else mark],
            in_specs=[vmem] * (sources + len(extra)),
            out_specs=[vmem] * (len(owners) + 1),
            compiler_params=limit,
            name="place",
        )(*blocks, *extra)
        for i, (dt, dr) in enumerate(owners):
            if dt or dr:
                route = [
                    (t * cores + r, (t + dt) % tilts * cores + (r + dr) % cores)
                    for t in range(tilts)
                    for r in range(cores)
                ]
                parts[i] = lax.ppermute(parts[i], ("tilt", "rep"), route)
        extra = [more, *parts]
    return pl.pallas_call(
        functools.partial(sum_kernel, owners),
        out_shape=jax.ShapeDtypeStruct((each, cores, block_rows, block_cols), f32),
        in_specs=[vmem] * len(extra),
        out_specs=vmem,
        compiler_params=limit,
        name="total",
    )(*extra)


def solution(mesh):
    in_specs = (
        P(("groups", "tilt"), None, None, "slab", None),
        P(),
        P(),
        P(("groups", "tilt"), ("slab", "rep"), None, None, None),
        P(("groups", "tilt"), ("slab", "rep")),
        P(None, ("groups", "tilt"), "slab", None, None),
        P(("groups", "tilt"), "slab", None),
        P(),
        P(),
    )
    out_specs = P(("groups", "slab", "tilt", "rep"), None, None, None)
    return jax.shard_map(
        on_device, mesh=mesh, in_specs=in_specs, out_specs=out_specs, check_vma=False
    )
```

```python
import functools
import math

import jax
import jax.numpy as jnp
import numpy as np
from jax import lax
from jax.experimental import pallas as pl
from jax.experimental.pallas import tpu as pltpu
from jax.sharding import PartitionSpec as P

VB_DEV = 64
REACH = 3
CHUNKS = 2
CHUNK_ROWS = 8
HIGH = lax.Precision.HIGHEST
SMEM = pltpu.SMEM
VMEM = pltpu.VMEM


def dot(left, right, precision=None):
    return jnp.dot(left, right, precision=precision, preferred_element_type=jnp.float32)


def slab_steps(peers):
    if peers <= REACH + 1:
        return tuple(sorted(range(peers), key=lambda k: (k == 0, k < peers // 2, k)))
    ring = [s for k in range(REACH, 0, -1) for s in (peers - k, k)]
    return (*ring, 0)


def partner(slab, step, peers):
    if peers <= REACH + 1 and peers & (peers - 1) == 0:
        return slab ^ step
    return (slab + step) % peers


def angle_table(length):
    grid = np.arange(length)
    angles = (grid[:, None] * grid[None, :] % length) * (2.0 * math.pi / length)
    return np.concatenate([np.cos(angles), np.sin(angles)], axis=1).astype(np.float32)


def propagator_blocks(phases, table):
    length = phases.shape[-1]
    row = lax.broadcasted_iota(jnp.int32, (8, length), 0)
    waves = jnp.where(row == 0, jnp.cos(phases), jnp.sin(phases))
    sums = dot(waves, table, HIGH) * (1.0 / length)
    cc, cs = sums[0:1, :length], sums[0:1, length:]
    sc, ss = sums[1:2, :length], sums[1:2, length:]

    def circulant(line):
        wide = jnp.broadcast_to(line, (length, length))
        return pltpu.roll(wide, 0, 1, stride=1, stride_axis=0)

    kr, ki = circulant(cc + ss), circulant(sc - cs)
    krt, kit = circulant(cc - ss), circulant(sc + cs)
    whole = jnp.concatenate(
        [jnp.concatenate([kr, -ki], 1), jnp.concatenate([ki, kr], 1)], 0
    ).astype(jnp.bfloat16)
    turned = jnp.concatenate(
        [jnp.concatenate([krt, kit], 1), jnp.concatenate([-kit, krt], 1)], 0
    ).astype(jnp.bfloat16)
    return whole, turned


def frame_kernel(
    shifts,
    pos_hbm,
    index_hbm,
    count_hbm,
    phase_hbm,
    table_hbm,
    obj_hbm,
    probe_hbm,
    cot_hbm,
    row_hbm,
    col_hbm,
    *rest,
):
    far, steps = len(shifts) - 2, len(shifts)
    mine, other, scratch = rest[: 2 * steps], rest[2 * steps : 2 * steps + 2], rest[2 * steps + 2 :]
    pos_ref, index_ref, count_ref = scratch[0:3]
    phase_ref, table_ref, obj_ref, probe_ref, cot_ref, row_ref, col_ref = scratch[3:10]
    sems, band, window, col_bf, row_scr = scratch[10:]
    slices = obj_ref.shape[2]
    copies = [
        pltpu.make_async_copy(src, dst, sems.at[i])
        for i, (src, dst) in enumerate(
            [
                (phase_hbm, phase_ref),
                (table_hbm, table_ref),
                (pos_hbm, pos_ref),
                (probe_hbm, probe_ref),
                (index_hbm, index_ref),
                (count_hbm, count_ref),
                (row_hbm, row_ref),
            ]
        )
    ]
    got_phase, got_table, got_pos, got_probe, got_index, got_count, got_row = copies
    got_obj = [
        pltpu.make_async_copy(obj_hbm.at[0, :, s], obj_ref.at[0, :, s], sems.at[len(copies) + s])
        for s in range(slices)
    ]
    got_cot = pltpu.make_async_copy(cot_hbm, cot_ref, sems.at[len(copies) + slices])
    got_col = pltpu.make_async_copy(col_hbm, col_ref, sems.at[len(copies) + slices + 1])
    order = [s for i in range((slices + 1) // 2) for s in sorted({i, slices - 1 - i})]
    for copy in (got_pos, got_phase, got_table, *[got_obj[s] for s in order], got_probe, got_cot):
        copy.start()
    for copy in (got_index, got_count, got_row, got_col):
        copy.start()

    me, core = lax.axis_index("slab"), lax.axis_index("rep")
    peers = lax.axis_size("slab")
    capacity = index_ref.shape[-1]
    size = probe_ref.shape[-1]
    rows, cols = obj_ref.shape[3:]
    count = cot_ref.shape[1]
    group = 2 if count % 2 == 0 else 1
    f32, bf16 = jnp.float32, jnp.bfloat16

    got_pos.wait()
    got_phase.wait()
    got_table.wait()
    col_down = lax.broadcasted_iota(jnp.int32, (cols, size), 0)
    lane = lax.broadcasted_iota(jnp.int32, (cols, size), 1)
    cut = jnp.concatenate(
        [(col_down == lane + pos_ref[0, w]).astype(bf16) for w in range(count)], 1
    )
    whole, turned = propagator_blocks(phase_ref[...], table_ref[...])

    for copy in got_obj:
        copy.wait()
    got_probe.wait()
    got_cot.wait()
    for s in order:
        source = jnp.concatenate([obj_ref[0, 0, s], obj_ref[0, 1, s]], 0)
        window[s] = dot(source, cut).astype(bf16)

    def tile(s, c, w):
        return window[s, c * rows : (c + 1) * rows, w * size : (w + 1) * size]

    def left(fields, matrix):
        parts = []
        for g in range(0, count, group):
            stack = jnp.concatenate(
                [jnp.concatenate([fields[w][c] for w in range(g, g + group)], 1) for c in (0, 1)], 0
            )
            parts.append(dot(matrix, stack).astype(bf16))
        return parts

    def right(parts, matrix):
        result = []
        for part in parts:
            stack = jnp.concatenate(
                [
                    jnp.concatenate(
                        [
                            part[c * size : (c + 1) * size, k * size : (k + 1) * size]
                            for c in (0, 1)
                        ],
                        1,
                    )
                    for k in range(group)
                ],
                0,
            )
            done = dot(stack, matrix).astype(bf16)
            for k in range(group):
                lines = done[k * size : (k + 1) * size]
                result.append((lines[:, :size], lines[:, size:]))
        return result

    def product(one, two, conjugate):
        a_re, a_im = one[0].astype(f32), one[1].astype(f32)
        b_re, b_im = two[0].astype(f32), two[1].astype(f32)
        if conjugate:
            a_im = -a_im
        return (
            (a_re * b_re - a_im * b_im).astype(bf16),
            (a_re * b_im + a_im * b_re).astype(bf16),
        )

    block_rows, block_cols = row_ref.shape[-1], col_ref.shape[-1]
    across = cols // block_cols
    psi, chi = {}, {}
    now = [(probe_ref[0], probe_ref[1])] * count
    back = [(cot_ref[0, w, 0], cot_ref[0, w, 1]) for w in range(count)]
    lane_down = lax.broadcasted_iota(jnp.int32, (size, cols), 0)
    col = lax.broadcasted_iota(jnp.int32, (size, cols), 1)
    paste = jnp.concatenate(
        [(col == lane_down + pos_ref[0, w]).astype(bf16) for w in range(count)], 0
    )
    for i in range(slices):
        s, e = i, slices - 1 - i
        psi[s], chi[e] = now, back
        if i + 1 < slices:
            here = [(tile(s, 0, w), tile(s, 1, w)) for w in range(count)]
            there = [(tile(e, 0, w), tile(e, 1, w)) for w in range(count)]
            passed = [product(here[w], now[w], False) for w in range(count)]
            rho = [product(there[w], back[w], True) for w in range(count)]
            now, back = left(passed, whole), left(rho, turned)
            now, back = right(now, turned), right(back, whole)
        for t in sorted({s, e}):
            if t not in psi or t not in chi or max(t, slices - 1 - t) != i:
                continue
            grads = [product(psi[t][w], chi[t][w], True) for w in range(count)]
            stack = jnp.concatenate(
                [jnp.concatenate([grads[w][c] for w in range(count)], 1) for c in (0, 1)], 0
            )
            spread = dot(stack, paste).astype(bf16)
            for c in (0, 1):
                for k in range(rows // block_rows):
                    top = c * rows + k * block_rows
                    for j in range(across):
                        band[c, (t * (rows // block_rows) + k) * across + j] = spread[
                            top : top + block_rows, j * block_cols : (j + 1) * block_cols
                        ]

    got_row.wait()
    got_col.wait()
    got_index.wait()
    got_count.wait()
    tiles = row_ref.shape[0]
    batch = 8
    wide = batch * block_rows
    col_bf[...] = col_ref[...].astype(bf16)
    down = lax.broadcasted_iota(jnp.int32, (block_rows, wide), 0)
    along = lax.broadcasted_iota(jnp.int32, (block_rows, wide), 1)
    repeat = (lax.rem(along, block_rows) == down).astype(bf16)
    row_wide = dot(row_ref[...].reshape(tiles * block_rows, block_rows).astype(bf16), repeat)
    row_scr[...] = row_wide.reshape(tiles, block_rows, wide)
    strip = lax.div(along, block_rows)
    half = block_rows // CHUNKS
    mark_down = lax.broadcasted_iota(jnp.int32, (half, capacity * half), 0)
    mark_along = lax.broadcasted_iota(jnp.int32, (half, capacity * half), 1)
    mark_slot = jnp.where(lax.rem(mark_along, half) == mark_down, lax.div(mark_along, half), -1)
    lines = capacity * half
    late = (steps - far) * (lines + half)

    def put(k, h, slot, value):
        at = slot * half
        if h:
            swap, base = other[1], late + k * lines
        elif k < far:
            swap, base = other[0], k * (lines + half)
        else:
            swap, base = other[1], (k - far) * (lines + half)
        mine[h * steps + k][at : at + half] = value[:, :block_cols]
        swap[base + at : base + at + half] = value[:, block_cols:]

    for k, shift in enumerate(shifts):
        dest = partner(me, shift, peers)
        live = count_ref[0, 0, dest]
        marks = jnp.full(mark_slot.shape, VB_DEV, jnp.int32)
        for first in range(0, capacity, batch):
            inner, picks = [], []
            for slot in range(first, first + batch, 2):
                pairs, factors = [], []
                for one in (slot, slot + 1):
                    block = index_ref[0, 0, 0, dest, one]
                    target = index_ref[1, 0, 0, dest, one]
                    t = index_ref[2, 0, 0, dest, one]
                    target = jnp.where(one < live, target, VB_DEV)
                    marks = jnp.where(mark_slot == one, target, marks)
                    pairs += [band[core, block], band[1 - core, block]]
                    factors.append(col_bf[t])
                    picked = jnp.where(strip == one - first, row_scr[t], 0.0)
                    picks.append(picked.astype(bf16))
                mixed = dot(jnp.concatenate(pairs, 0), jnp.concatenate(factors, 1)).astype(bf16)
                for n in (0, 1):
                    lanes = slice(n * block_cols, (n + 1) * block_cols)
                    top = 2 * n * block_rows
                    inner.append(
                        jnp.concatenate(
                            [
                                mixed[top : top + block_rows, lanes],
                                mixed[top + block_rows : top + 2 * block_rows, lanes],
                            ],
                            1,
                        )
                    )
            result = dot(jnp.concatenate(picks, 0), jnp.concatenate(inner, 0))
            for slot in range(first, first + batch):
                for h in range(CHUNKS):
                    top = (slot - first) * block_rows + h * half
                    put(k, h, slot, result[top : top + half])
        marks = marks.astype(f32)
        put(k, 0, capacity, jnp.concatenate([marks, jnp.zeros_like(marks)], 1))


def join_kernel(base, first_ref, got_ref, *refs):
    count = len(refs) // 2
    for part, out in zip(refs[:count], refs[count:]):
        tall = part.shape[0]
        out[...] = part[...] + got_ref[base : base + tall]
        base += tall


def place_kernel(sources, owners, first, *refs):
    tilt, core = lax.axis_index("tilt"), lax.axis_index("rep")
    tilts, cores = lax.axis_size("tilt"), lax.axis_size("rep")
    each = VB_DEV // (tilts * cores)
    blocks = refs[:sources]
    half, lanes = CHUNK_ROWS, blocks[0].shape[-1]
    size = each * half
    if first:
        outs, mark_ref = refs[sources:-1], refs[-1]
        for k, block in enumerate(blocks):
            mark_ref[k] = block[lanes:]
    else:
        mark_ref, rest = refs[sources], refs[sources + 1 :]
        before, outs, done = rest[: len(owners)], rest[len(owners) : -1], rest[-1]
        for ref, out, (dt, dr) in zip(before, outs, owners):
            if dr and not dt:
                out[:size] = ref[...]
        for dr in range(cores):
            parts = [ref[...] for ref, (dt, r) in zip(before, owners) if r == dr and (dt or not r)]
            done[dr] = functools.reduce(jnp.add, parts)
    data = jnp.concatenate([block[:lanes].astype(jnp.bfloat16) for block in blocks], 0)
    volume = lax.broadcasted_iota(jnp.int32, (each, half, lanes), 0).astype(jnp.float32)
    for out, (dt, dr) in zip(outs, owners):
        owner = lax.rem(tilt + dt, tilts) * cores + lax.rem(core + dr, cores)
        base = (owner * each).astype(jnp.float32)
        hot = []
        for k in range(sources):
            mark = mark_ref[k] - base
            hit = jnp.where(volume == mark[None], 1.0, 0.0)
            hot.append(hit.reshape(size, lanes).astype(jnp.bfloat16))
        begin = out.shape[0] - size
        out[begin : begin + size] = dot(jnp.concatenate(hot, 1), data)


def sum_kernel(owners, done_ref, *refs):
    parts, out_ref = refs[:-1], refs[-1]
    core, cores = lax.axis_index("rep"), lax.axis_size("rep")
    each, cols = out_ref.shape[0], out_ref.shape[-1]
    size = each * CHUNK_ROWS
    for dr in range(cores):
        at = lax.rem(core + dr, cores)
        early, late = done_ref[dr], None
        for ref, (dt, r) in zip(parts, owners):
            if r == dr:
                if dr and not dt:
                    early = early + ref[:size]
                value = ref[ref.shape[0] - size :]
                late = value if late is None else late + value
        for h, value in enumerate([early, late]):
            rows = pl.ds(h * CHUNK_ROWS, CHUNK_ROWS)
            out_ref[:, at, rows] = value.reshape(each, CHUNK_ROWS, cols)


def on_device(
    object_slab,
    probe_field,
    phases,
    cotangent,
    positions,
    pair_index,
    pair_counts,
    row_interp,
    col_interp,
):
    peers = lax.axis_size("slab")
    tilts, cores = lax.axis_size("tilt"), lax.axis_size("rep")
    shifts = slab_steps(peers)
    capacity = pair_index.shape[-1]
    block_rows, block_cols = row_interp.shape[-1], col_interp.shape[-1]
    _, _, slices, rows, cols = object_slab.shape
    windows, size = cotangent.shape[1], cotangent.shape[-1]
    f32, bf16 = jnp.float32, jnp.bfloat16
    hbm, vmem = pl.BlockSpec(memory_space=pltpu.HBM), pl.BlockSpec(memory_space=VMEM)
    limit = pltpu.CompilerParams(vmem_limit_bytes=40 * 1024 * 1024)
    sources = len(shifts)
    lanes = capacity * CHUNK_ROWS

    phase_line = phases.reshape(1, -1)
    table = jnp.asarray(angle_table(size))
    frames = (slices * (rows // block_rows) * (cols // block_cols), block_rows, block_cols)
    far = sources - 2
    tall = lanes + CHUNK_ROWS
    heights = [tall] * sources + [lanes] * sources
    swapped = [far * tall, (sources - far) * tall + sources * lanes]
    shapes = [jax.ShapeDtypeStruct((tall, block_cols), f32) for tall in heights + swapped]
    fetched = [
        (phase_line, VMEM),
        (table, VMEM),
        (object_slab, VMEM),
        (probe_field, VMEM),
        (cotangent, VMEM),
        (row_interp, VMEM),
        (col_interp, VMEM),
    ]
    scalars = [positions, pair_index, pair_counts]
    held = pl.pallas_call(
        functools.partial(frame_kernel, shifts),
        out_shape=shapes,
        in_specs=[hbm] * 10,
        out_specs=[vmem] * len(shapes),
        scratch_shapes=[SMEM(x.shape, x.dtype) for x in scalars]
        + [space(x.shape, x.dtype) for x, space in fetched]
        + [
            pltpu.SemaphoreType.DMA((9 + slices,)),
            VMEM((2,) + frames, bf16),
            VMEM((slices, 2 * rows, windows * size), bf16),
            VMEM(col_interp.shape, bf16),
            VMEM((row_interp.shape[0], block_rows, 8 * block_rows), f32),
        ],
        compiler_params=limit,
        name="frame",
    )(*[pltpu.with_memory_space_constraint(x, pltpu.HBM) for x in scalars + [x for x, _ in fetched]])

    swap = [(r, (r + 1) % cores) for r in range(cores)]
    owners = sorted(
        ((dt, dr) for dt in range(tilts) for dr in range(cores)), key=lambda o: (o[0] == 0, o)
    )
    each = VB_DEV // len(owners)
    share = jax.ShapeDtypeStruct((each * CHUNK_ROWS, block_cols), f32)
    mark = jax.ShapeDtypeStruct((sources, CHUNK_ROWS, block_cols), f32)
    double = jax.ShapeDtypeStruct((2 * each * CHUNK_ROWS, block_cols), f32)
    done = jax.ShapeDtypeStruct((cores, each * CHUNK_ROWS, block_cols), f32)
    mine, other = held[: len(heights)], held[len(heights) :]
    got = [lax.ppermute(half, "rep", swap) for half in other]

    def send(block, step):
        ring = [(p, partner(p, step, peers)) for p in range(peers)]
        return lax.ppermute(block, "slab", ring)

    first = []
    for k in range(sources):
        h, at = (0, k * tall) if k < far else (1, (k - far) * tall)
        block = mine[k] + got[h][at : at + tall]
        first.append(send(block, shifts[k]) if shifts[k] else block)
    def join(after, part):
        late = mine[sources:][part]
        return pl.pallas_call(
            functools.partial(join_kernel, (sources - far) * tall + part.start * lanes),
            out_shape=shapes[sources : 2 * sources][part],
            in_specs=[vmem] * (len(late) + 2),
            out_specs=[vmem] * len(late),
            compiler_params=limit,
            name="join",
        )(after, got[1], *late)

    def place(blocks, extra, h):
        return pl.pallas_call(
            functools.partial(place_kernel, sources, owners, h == 0),
            out_shape=[double if h and dr and not dt else share for dt, dr in owners]
            + [done if h else mark],
            in_specs=[vmem] * (sources + len(extra)),
            out_specs=[vmem] * (len(owners) + 1),
            compiler_params=limit,
            name="place",
        )(*blocks, *extra)

    def share_out(parts, h):
        sent = []
        for part, (dt, dr) in zip(parts, owners):
            if dt or (dr and h):
                route = [
                    (t * cores + r, (t + dt) % tilts * cores + (r + dr) % cores)
                    for t in range(tilts)
                    for r in range(cores)
                ]
                part = lax.ppermute(part, ("tilt", "rep"), route)
            sent.append(part)
        return sent

    joined = [block for k in range(far) for block in join(first[k], slice(k, k + 1))]
    *parts, marks = place(first, [], 0)
    parts = share_out(parts, 0)
    joined += join(marks, slice(far, sources))
    second = [send(block, k) if k else block for block, k in zip(joined, shifts)]
    *late_parts, sums = place(second, [marks, *parts], 1)
    extra = [sums, *share_out(late_parts, 1)]
    return pl.pallas_call(
        functools.partial(sum_kernel, owners),
        out_shape=jax.ShapeDtypeStruct((each, cores, block_rows, block_cols), f32),
        in_specs=[vmem] * len(extra),
        out_specs=vmem,
        compiler_params=limit,
        name="total",
    )(*extra)


def solution(mesh):
    in_specs = (
        P(("groups", "tilt"), None, None, "slab", None),
        P(),
        P(),
        P(("groups", "tilt"), ("slab", "rep"), None, None, None),
        P(("groups", "tilt"), ("slab", "rep")),
        P(None, ("groups", "tilt"), "slab", None, None),
        P(("groups", "tilt"), "slab", None),
        P(),
        P(),
    )
    out_specs = P(("groups", "slab", "tilt", "rep"), None, None, None)
    return jax.shard_map(
        on_device, mesh=mesh, in_specs=in_specs, out_specs=out_specs, check_vma=False
    )
```

```python
import functools
import math

import jax
import jax.numpy as jnp
import numpy as np
from jax import lax
from jax.experimental import pallas as pl
from jax.experimental.pallas import tpu as pltpu
from jax.sharding import PartitionSpec as P

VB_DEV = 64
REACH = 3
CHUNKS = 2
CHUNK_ROWS = 8
HIGH = lax.Precision.HIGHEST
SMEM = pltpu.SMEM
VMEM = pltpu.VMEM


def dot(left, right, precision=None):
    return jnp.dot(left, right, precision=precision, preferred_element_type=jnp.float32)


def slab_steps(peers):
    if peers <= REACH + 1:
        return tuple(sorted(range(peers), key=lambda k: (k == 0, k < peers // 2, k)))
    ring = [s for k in range(REACH, 0, -1) for s in (peers - k, k)]
    return (*ring, 0)


def partner(slab, step, peers):
    if peers <= REACH + 1 and peers & (peers - 1) == 0:
        return slab ^ step
    return (slab + step) % peers


def angle_table(length):
    grid = np.arange(length)
    angles = (grid[:, None] * grid[None, :] % length) * (2.0 * math.pi / length)
    return np.concatenate([np.cos(angles), np.sin(angles)], axis=1).astype(np.float32)


def propagator_blocks(phases, table):
    length = phases.shape[-1]
    row = lax.broadcasted_iota(jnp.int32, (8, length), 0)
    waves = jnp.where(row == 0, jnp.cos(phases), jnp.sin(phases))
    sums = dot(waves, table, HIGH) * (1.0 / length)
    cc, cs = sums[0:1, :length], sums[0:1, length:]
    sc, ss = sums[1:2, :length], sums[1:2, length:]

    def circulant(line):
        wide = jnp.broadcast_to(line, (length, length))
        return pltpu.roll(wide, 0, 1, stride=1, stride_axis=0)

    kr, ki = circulant(cc + ss), circulant(sc - cs)
    krt, kit = circulant(cc - ss), circulant(sc + cs)
    whole = jnp.concatenate(
        [jnp.concatenate([kr, -ki], 1), jnp.concatenate([ki, kr], 1)], 0
    ).astype(jnp.bfloat16)
    turned = jnp.concatenate(
        [jnp.concatenate([krt, kit], 1), jnp.concatenate([-kit, krt], 1)], 0
    ).astype(jnp.bfloat16)
    return whole, turned


def frame_kernel(
    shifts,
    pos_hbm,
    index_hbm,
    count_hbm,
    phase_hbm,
    table_hbm,
    obj_hbm,
    probe_hbm,
    cot_hbm,
    row_hbm,
    col_hbm,
    *rest,
):
    far, steps = len(shifts) - 2, len(shifts)
    mine, other, scratch = rest[: 2 * steps], rest[2 * steps : 2 * steps + 2], rest[2 * steps + 2 :]
    pos_ref, index_ref, count_ref = scratch[0:3]
    phase_ref, table_ref, obj_ref, probe_ref, cot_ref, row_ref, col_ref = scratch[3:10]
    sems, band, window, col_bf, row_scr = scratch[10:]
    slices = obj_ref.shape[2]
    copies = [
        pltpu.make_async_copy(src, dst, sems.at[i])
        for i, (src, dst) in enumerate(
            [
                (phase_hbm, phase_ref),
                (table_hbm, table_ref),
                (pos_hbm, pos_ref),
                (probe_hbm, probe_ref),
                (index_hbm, index_ref),
                (count_hbm, count_ref),
                (row_hbm, row_ref),
            ]
        )
    ]
    got_phase, got_table, got_pos, got_probe, got_index, got_count, got_row = copies
    got_obj = [
        pltpu.make_async_copy(obj_hbm.at[0, :, s], obj_ref.at[0, :, s], sems.at[len(copies) + s])
        for s in range(slices)
    ]
    got_cot = pltpu.make_async_copy(cot_hbm, cot_ref, sems.at[len(copies) + slices])
    got_col = pltpu.make_async_copy(col_hbm, col_ref, sems.at[len(copies) + slices + 1])
    order = [s for i in range((slices + 1) // 2) for s in sorted({i, slices - 1 - i})]
    for copy in (got_pos, got_phase, got_table, *[got_obj[s] for s in order], got_probe, got_cot):
        copy.start()
    for copy in (got_index, got_count, got_row, got_col):
        copy.start()

    me, core = lax.axis_index("slab"), lax.axis_index("rep")
    peers = lax.axis_size("slab")
    capacity = index_ref.shape[-1]
    size = probe_ref.shape[-1]
    rows, cols = obj_ref.shape[3:]
    count = cot_ref.shape[1]
    group = 2 if count % 2 == 0 else 1
    f32, bf16 = jnp.float32, jnp.bfloat16

    got_pos.wait()
    got_phase.wait()
    got_table.wait()
    col_down = lax.broadcasted_iota(jnp.int32, (cols, size), 0)
    lane = lax.broadcasted_iota(jnp.int32, (cols, size), 1)
    cut = jnp.concatenate(
        [(col_down == lane + pos_ref[0, w]).astype(bf16) for w in range(count)], 1
    )
    whole, turned = propagator_blocks(phase_ref[...], table_ref[...])

    for copy in got_obj:
        copy.wait()
    got_probe.wait()
    got_cot.wait()
    for s in order:
        source = jnp.concatenate([obj_ref[0, 0, s], obj_ref[0, 1, s]], 0)
        window[s] = dot(source, cut).astype(bf16)

    def tile(s, c, w):
        return window[s, c * rows : (c + 1) * rows, w * size : (w + 1) * size]

    def left(fields, matrix):
        parts = []
        for g in range(0, count, group):
            stack = jnp.concatenate(
                [jnp.concatenate([fields[w][c] for w in range(g, g + group)], 1) for c in (0, 1)], 0
            )
            parts.append(dot(matrix, stack).astype(bf16))
        return parts

    def right(parts, matrix):
        result = []
        for part in parts:
            stack = jnp.concatenate(
                [
                    jnp.concatenate(
                        [
                            part[c * size : (c + 1) * size, k * size : (k + 1) * size]
                            for c in (0, 1)
                        ],
                        1,
                    )
                    for k in range(group)
                ],
                0,
            )
            done = dot(stack, matrix).astype(bf16)
            for k in range(group):
                lines = done[k * size : (k + 1) * size]
                result.append((lines[:, :size], lines[:, size:]))
        return result

    def product(one, two, conjugate):
        a_re, a_im = one[0].astype(f32), one[1].astype(f32)
        b_re, b_im = two[0].astype(f32), two[1].astype(f32)
        if conjugate:
            a_im = -a_im
        return (
            (a_re * b_re - a_im * b_im).astype(bf16),
            (a_re * b_im + a_im * b_re).astype(bf16),
        )

    block_rows, block_cols = row_ref.shape[-1], col_ref.shape[-1]
    across = cols // block_cols
    psi, chi = {}, {}
    now = [(probe_ref[0], probe_ref[1])] * count
    back = [(cot_ref[0, w, 0], cot_ref[0, w, 1]) for w in range(count)]
    lane_down = lax.broadcasted_iota(jnp.int32, (size, cols), 0)
    col = lax.broadcasted_iota(jnp.int32, (size, cols), 1)
    paste = jnp.concatenate(
        [(col == lane_down + pos_ref[0, w]).astype(bf16) for w in range(count)], 0
    )
    for i in range(slices):
        s, e = i, slices - 1 - i
        psi[s], chi[e] = now, back
        if i + 1 < slices:
            here = [(tile(s, 0, w), tile(s, 1, w)) for w in range(count)]
            there = [(tile(e, 0, w), tile(e, 1, w)) for w in range(count)]
            passed = [product(here[w], now[w], False) for w in range(count)]
            rho = [product(there[w], back[w], True) for w in range(count)]
            now, back = left(passed, whole), left(rho, turned)
            now, back = right(now, turned), right(back, whole)
        for t in sorted({s, e}):
            if t not in psi or t not in chi or max(t, slices - 1 - t) != i:
                continue
            grads = [product(psi[t][w], chi[t][w], True) for w in range(count)]
            stack = jnp.concatenate(
                [jnp.concatenate([grads[w][c] for w in range(count)], 1) for c in (0, 1)], 0
            )
            spread = dot(stack, paste).astype(bf16)
            for c in (0, 1):
                for k in range(rows // block_rows):
                    top = c * rows + k * block_rows
                    for j in range(across):
                        band[c, (t * (rows // block_rows) + k) * across + j] = spread[
                            top : top + block_rows, j * block_cols : (j + 1) * block_cols
                        ]

    got_row.wait()
    got_col.wait()
    got_index.wait()
    got_count.wait()
    tiles = row_ref.shape[0]
    batch = 8
    wide = batch * block_rows
    col_bf[...] = col_ref[...].astype(bf16)
    down = lax.broadcasted_iota(jnp.int32, (block_rows, wide), 0)
    along = lax.broadcasted_iota(jnp.int32, (block_rows, wide), 1)
    repeat = (lax.rem(along, block_rows) == down).astype(bf16)
    row_wide = dot(row_ref[...].reshape(tiles * block_rows, block_rows).astype(bf16), repeat)
    row_scr[...] = row_wide.reshape(tiles, block_rows, wide)
    strip = lax.div(along, block_rows)
    half = block_rows // CHUNKS
    mark_down = lax.broadcasted_iota(jnp.int32, (half, capacity * half), 0)
    mark_along = lax.broadcasted_iota(jnp.int32, (half, capacity * half), 1)
    mark_slot = jnp.where(lax.rem(mark_along, half) == mark_down, lax.div(mark_along, half), -1)
    lines = capacity * half
    late = (steps - far) * (lines + half)

    def put(k, h, slot, value):
        at = slot * half
        if h:
            swap, base = other[1], late + k * lines
        elif k < far:
            swap, base = other[0], k * (lines + half)
        else:
            swap, base = other[1], (k - far) * (lines + half)
        mine[h * steps + k][at : at + half] = value[:, :block_cols]
        swap[base + at : base + at + half] = value[:, block_cols:]

    for k, shift in enumerate(shifts):
        dest = partner(me, shift, peers)
        live = count_ref[0, 0, dest]
        marks = jnp.full(mark_slot.shape, VB_DEV, jnp.int32)
        for first in range(0, capacity, batch):
            inner, picks = [], []
            for slot in range(first, first + batch, 2):
                pairs, factors = [], []
                for one in (slot, slot + 1):
                    block = index_ref[0, 0, 0, dest, one]
                    target = index_ref[1, 0, 0, dest, one]
                    t = index_ref[2, 0, 0, dest, one]
                    target = jnp.where(one < live, target, VB_DEV)
                    marks = jnp.where(mark_slot == one, target, marks)
                    pairs += [band[core, block], band[1 - core, block]]
                    factors.append(col_bf[t])
                    picked = jnp.where(strip == one - first, row_scr[t], 0.0)
                    picks.append(picked.astype(bf16))
                mixed = dot(jnp.concatenate(pairs, 0), jnp.concatenate(factors, 1)).astype(bf16)
                for n in (0, 1):
                    lanes = slice(n * block_cols, (n + 1) * block_cols)
                    top = 2 * n * block_rows
                    inner.append(
                        jnp.concatenate(
                            [
                                mixed[top : top + block_rows, lanes],
                                mixed[top + block_rows : top + 2 * block_rows, lanes],
                            ],
                            1,
                        )
                    )
            result = dot(jnp.concatenate(picks, 0), jnp.concatenate(inner, 0))
            for slot in range(first, first + batch):
                for h in range(CHUNKS):
                    top = (slot - first) * block_rows + h * half
                    put(k, h, slot, result[top : top + half])
        marks = marks.astype(f32)
        put(k, 0, capacity, jnp.concatenate([marks, jnp.zeros_like(marks)], 1))


def join_kernel(base, first_ref, got_ref, *refs):
    count = len(refs) // 2
    for part, out in zip(refs[:count], refs[count:]):
        tall = part.shape[0]
        out[...] = part[...] + got_ref[base : base + tall]
        base += tall


def place_kernel(sources, owners, first, *refs):
    tilt, core = lax.axis_index("tilt"), lax.axis_index("rep")
    tilts, cores = lax.axis_size("tilt"), lax.axis_size("rep")
    each = VB_DEV // (tilts * cores)
    blocks = refs[:sources]
    half, lanes = CHUNK_ROWS, blocks[0].shape[-1]
    size = each * half
    if first:
        outs, mark_ref = refs[sources:-1], refs[-1]
        for k, block in enumerate(blocks):
            mark_ref[k] = block[lanes:]
    else:
        mark_ref, outs = refs[sources], refs[sources + cores :]
    data = jnp.concatenate([block[:lanes].astype(jnp.bfloat16) for block in blocks], 0)
    volume = lax.broadcasted_iota(jnp.int32, (each, half, lanes), 0).astype(jnp.float32)
    for out, (dt, dr) in zip(outs, owners):
        owner = lax.rem(tilt + dt, tilts) * cores + lax.rem(core + dr, cores)
        base = (owner * each).astype(jnp.float32)
        hot = []
        for k in range(sources):
            mark = mark_ref[k] - base
            hit = jnp.where(volume == mark[None], 1.0, 0.0)
            hot.append(hit.reshape(size, lanes).astype(jnp.bfloat16))
        out[:size] = dot(jnp.concatenate(hot, 1), data)
        if out.shape[0] > size:
            out[size:] = jnp.zeros((out.shape[0] - size, out.shape[1]), jnp.float32)


def sum_kernel(owners, *refs):
    out_ref = refs[-1]
    core, cores = lax.axis_index("rep"), lax.axis_size("rep")
    each, cols = out_ref.shape[0], out_ref.shape[-1]
    size = each * CHUNK_ROWS
    for h in range(CHUNKS):
        parts = refs[h * len(owners) : (h + 1) * len(owners)]
        for dr in range(cores):
            values = [ref[:size] for ref, (_, r) in zip(parts, owners) if r == dr]
            total = functools.reduce(jnp.add, values).reshape(each, CHUNK_ROWS, cols)
            out_ref[:, lax.rem(core + dr, cores), pl.ds(h * CHUNK_ROWS, CHUNK_ROWS)] = total


def on_device(
    object_slab,
    probe_field,
    phases,
    cotangent,
    positions,
    pair_index,
    pair_counts,
    row_interp,
    col_interp,
):
    peers = lax.axis_size("slab")
    tilts, cores = lax.axis_size("tilt"), lax.axis_size("rep")
    shifts = slab_steps(peers)
    capacity = pair_index.shape[-1]
    block_rows, block_cols = row_interp.shape[-1], col_interp.shape[-1]
    _, _, slices, rows, cols = object_slab.shape
    windows, size = cotangent.shape[1], cotangent.shape[-1]
    f32, bf16 = jnp.float32, jnp.bfloat16
    hbm, vmem = pl.BlockSpec(memory_space=pltpu.HBM), pl.BlockSpec(memory_space=VMEM)
    limit = pltpu.CompilerParams(vmem_limit_bytes=40 * 1024 * 1024)
    sources = len(shifts)
    lanes = capacity * CHUNK_ROWS

    phase_line = phases.reshape(1, -1)
    table = jnp.asarray(angle_table(size))
    frames = (slices * (rows // block_rows) * (cols // block_cols), block_rows, block_cols)
    far = sources - 2
    tall = lanes + CHUNK_ROWS
    heights = [tall] * sources + [lanes] * sources
    swapped = [far * tall, (sources - far) * tall + sources * lanes]
    shapes = [jax.ShapeDtypeStruct((tall, block_cols), f32) for tall in heights + swapped]
    fetched = [
        (phase_line, VMEM),
        (table, VMEM),
        (object_slab, VMEM),
        (probe_field, VMEM),
        (cotangent, VMEM),
        (row_interp, VMEM),
        (col_interp, VMEM),
    ]
    scalars = [positions, pair_index, pair_counts]
    held = pl.pallas_call(
        functools.partial(frame_kernel, shifts),
        out_shape=shapes,
        in_specs=[hbm] * 10,
        out_specs=[vmem] * len(shapes),
        scratch_shapes=[SMEM(x.shape, x.dtype) for x in scalars]
        + [space(x.shape, x.dtype) for x, space in fetched]
        + [
            pltpu.SemaphoreType.DMA((9 + slices,)),
            VMEM((2,) + frames, bf16),
            VMEM((slices, 2 * rows, windows * size), bf16),
            VMEM(col_interp.shape, bf16),
            VMEM((row_interp.shape[0], block_rows, 8 * block_rows), f32),
        ],
        compiler_params=limit,
        name="frame",
    )(*[pltpu.with_memory_space_constraint(x, pltpu.HBM) for x in scalars + [x for x, _ in fetched]])

    swap = [(r, (r + 1) % cores) for r in range(cores)]
    owners = sorted(
        ((dt, dr) for dt in range(tilts) for dr in range(cores)), key=lambda o: (o[0] == 0, o)
    )
    each = VB_DEV // len(owners)
    share = jax.ShapeDtypeStruct((each * CHUNK_ROWS, block_cols), f32)
    mark = jax.ShapeDtypeStruct((sources, CHUNK_ROWS, block_cols), f32)
    padded = jax.ShapeDtypeStruct(((each + 1) * CHUNK_ROWS, block_cols), f32)
    mine, other = held[: len(heights)], held[len(heights) :]
    got = [lax.ppermute(half, "rep", swap) for half in other]

    def send(block, step):
        ring = [(p, partner(p, step, peers)) for p in range(peers)]
        return lax.ppermute(block, "slab", ring)

    first = []
    for k in range(sources):
        h, at = (0, k * tall) if k < far else (1, (k - far) * tall)
        block = mine[k] + got[h][at : at + tall]
        first.append(send(block, shifts[k]) if shifts[k] else block)
    def join(after, part):
        late = mine[sources:][part]
        return pl.pallas_call(
            functools.partial(join_kernel, (sources - far) * tall + part.start * lanes),
            out_shape=shapes[sources : 2 * sources][part],
            in_specs=[vmem] * (len(late) + 2),
            out_specs=[vmem] * len(late),
            compiler_params=limit,
            name="join",
        )(after, got[1], *late)

    def place(blocks, extra, h):
        shapes = [padded if dt else share for dt, dr in owners] + [mark]
        if h:
            shapes = [share] * len(owners)
        return pl.pallas_call(
            functools.partial(place_kernel, sources, owners, h == 0),
            out_shape=shapes,
            in_specs=[vmem] * (sources + len(extra)),
            out_specs=[vmem] * len(shapes),
            compiler_params=limit,
            name="place",
        )(*blocks, *extra)

    def share_out(part, owner):
        dt, dr = owner
        if not (dt or dr):
            return part
        route = [
            (t * cores + r, (t + dt) % tilts * cores + (r + dr) % cores)
            for t in range(tilts)
            for r in range(cores)
        ]
        return lax.ppermute(part, ("tilt", "rep"), route)

    joined = []
    for k in range(far):
        joined += join(first[k], slice(k, k + 1 if k + 1 < far else sources))
    second = [send(block, k) if k else block for block, k in zip(joined, shifts)]
    *parts, marks = place(first, [], 0)
    extra = [share_out(part, owner) for part, owner in zip(parts, owners)]
    held = [part for part, (dt, dr) in zip(extra, owners) if dr and not dt]
    late = place(second, [marks, *held], 1)
    extra += [share_out(part, owner) for part, owner in zip(late, owners)]
    return pl.pallas_call(
        functools.partial(sum_kernel, owners),
        out_shape=jax.ShapeDtypeStruct((each, cores, block_rows, block_cols), f32),
        in_specs=[vmem] * len(extra),
        out_specs=vmem,
        compiler_params=limit,
        name="total",
    )(*extra)


def solution(mesh):
    in_specs = (
        P(("groups", "tilt"), None, None, "slab", None),
        P(),
        P(),
        P(("groups", "tilt"), ("slab", "rep"), None, None, None),
        P(("groups", "tilt"), ("slab", "rep")),
        P(None, ("groups", "tilt"), "slab", None, None),
        P(("groups", "tilt"), "slab", None),
        P(),
        P(),
    )
    out_specs = P(("groups", "slab", "tilt", "rep"), None, None, None)
    return jax.shard_map(
        on_device, mesh=mesh, in_specs=in_specs, out_specs=out_specs, check_vma=False
    )
```

```python
import functools
import math

import jax
import jax.numpy as jnp
import numpy as np
from jax import lax
from jax.experimental import pallas as pl
from jax.experimental.pallas import tpu as pltpu
from jax.sharding import PartitionSpec as P

VB_DEV = 64
REACH = 3
CHUNKS = 2
CHUNK_ROWS = 8
HIGH = lax.Precision.HIGHEST
SMEM = pltpu.SMEM
VMEM = pltpu.VMEM


def dot(left, right, precision=None):
    return jnp.dot(left, right, precision=precision, preferred_element_type=jnp.float32)


def slab_steps(peers):
    if peers <= REACH + 1:
        return tuple(sorted(range(peers), key=lambda k: (k == 0, k < peers // 2, k)))
    ring = [s for k in range(REACH, 0, -1) for s in (peers - k, k)]
    return (*ring, 0)


def partner(slab, step, peers):
    if peers <= REACH + 1 and peers & (peers - 1) == 0:
        return slab ^ step
    return (slab + step) % peers


def angle_table(length):
    grid = np.arange(length)
    angles = (grid[:, None] * grid[None, :] % length) * (2.0 * math.pi / length)
    return np.concatenate([np.cos(angles), np.sin(angles)], axis=1).astype(np.float32)


def propagator_blocks(phases, table):
    length = phases.shape[-1]
    row = lax.broadcasted_iota(jnp.int32, (8, length), 0)
    waves = jnp.where(row == 0, jnp.cos(phases), jnp.sin(phases))
    sums = dot(waves, table, HIGH) * (1.0 / length)
    cc, cs = sums[0:1, :length], sums[0:1, length:]
    sc, ss = sums[1:2, :length], sums[1:2, length:]

    def circulant(line):
        wide = jnp.broadcast_to(line, (length, length))
        return pltpu.roll(wide, 0, 1, stride=1, stride_axis=0)

    kr, ki = circulant(cc + ss), circulant(sc - cs)
    krt, kit = circulant(cc - ss), circulant(sc + cs)
    whole = jnp.concatenate(
        [jnp.concatenate([kr, -ki], 1), jnp.concatenate([ki, kr], 1)], 0
    ).astype(jnp.bfloat16)
    turned = jnp.concatenate(
        [jnp.concatenate([krt, kit], 1), jnp.concatenate([-kit, krt], 1)], 0
    ).astype(jnp.bfloat16)
    return whole, turned


def frame_kernel(
    shifts,
    pos_hbm,
    index_hbm,
    count_hbm,
    phase_hbm,
    table_hbm,
    obj_hbm,
    probe_hbm,
    cot_hbm,
    row_hbm,
    col_hbm,
    *rest,
):
    far, steps = len(shifts) - 2, len(shifts)
    mine, other, scratch = rest[: 2 * steps], rest[2 * steps : 2 * steps + 3], rest[2 * steps + 3 :]
    pos_ref, index_ref, count_ref = scratch[0:3]
    phase_ref, table_ref, obj_ref, probe_ref, cot_ref, row_ref, col_ref = scratch[3:10]
    sems, band, window, col_bf, row_scr, row_mix = scratch[10:]
    slices = obj_ref.shape[2]
    copies = [
        pltpu.make_async_copy(src, dst, sems.at[i])
        for i, (src, dst) in enumerate(
            [
                (phase_hbm, phase_ref),
                (table_hbm, table_ref),
                (pos_hbm, pos_ref),
                (probe_hbm, probe_ref),
                (index_hbm, index_ref),
                (count_hbm, count_ref),
                (row_hbm, row_ref),
            ]
        )
    ]
    got_phase, got_table, got_pos, got_probe, got_index, got_count, got_row = copies
    got_obj = [
        pltpu.make_async_copy(obj_hbm.at[0, :, s], obj_ref.at[0, :, s], sems.at[len(copies) + s])
        for s in range(slices)
    ]
    got_cot = pltpu.make_async_copy(cot_hbm, cot_ref, sems.at[len(copies) + slices])
    got_col = pltpu.make_async_copy(col_hbm, col_ref, sems.at[len(copies) + slices + 1])
    order = [s for i in range((slices + 1) // 2) for s in sorted({i, slices - 1 - i})]
    for copy in (got_pos, got_phase, got_table, *[got_obj[s] for s in order], got_probe, got_cot):
        copy.start()
    for copy in (got_index, got_count, got_row, got_col):
        copy.start()

    me, core = lax.axis_index("slab"), lax.axis_index("rep")
    peers = lax.axis_size("slab")
    capacity = index_ref.shape[-1]
    size = probe_ref.shape[-1]
    rows, cols = obj_ref.shape[3:]
    count = cot_ref.shape[1]
    group = 2 if count % 2 == 0 else 1
    f32, bf16 = jnp.float32, jnp.bfloat16

    got_pos.wait()
    got_phase.wait()
    got_table.wait()
    col_down = lax.broadcasted_iota(jnp.int32, (cols, size), 0)
    lane = lax.broadcasted_iota(jnp.int32, (cols, size), 1)
    cut = jnp.concatenate(
        [(col_down == lane + pos_ref[0, w]).astype(bf16) for w in range(count)], 1
    )
    whole, turned = propagator_blocks(phase_ref[...], table_ref[...])

    for copy in got_obj:
        copy.wait()
    got_probe.wait()
    got_cot.wait()
    got_row.wait()
    got_col.wait()
    got_index.wait()
    got_count.wait()
    for s in order:
        source = jnp.concatenate([obj_ref[0, 0, s], obj_ref[0, 1, s]], 0)
        window[s] = dot(source, cut).astype(bf16)

    block_rows, block_cols = row_ref.shape[-1], col_ref.shape[-1]
    tiles = row_ref.shape[0]
    batch = 8
    wide = batch * block_rows
    col_bf[...] = col_ref[...].astype(bf16)
    down = lax.broadcasted_iota(jnp.int32, (block_rows, wide), 0)
    along = lax.broadcasted_iota(jnp.int32, (block_rows, wide), 1)
    repeat = (lax.rem(along, block_rows) == down).astype(bf16)
    row_wide = dot(row_ref[...].reshape(tiles * block_rows, block_rows).astype(bf16), repeat)
    row_scr[...] = row_wide.reshape(tiles, block_rows, wide)
    strip = lax.div(along, block_rows)
    half = block_rows // CHUNKS
    mark_down = lax.broadcasted_iota(jnp.int32, (half, capacity * half), 0)
    mark_along = lax.broadcasted_iota(jnp.int32, (half, capacity * half), 1)
    mark_slot = jnp.where(lax.rem(mark_along, half) == mark_down, lax.div(mark_along, half), -1)
    lines = capacity * half

    def put(k, h, slot, value):
        at = slot * half
        late = h and k >= far
        base = (k - far if late else k) * mine[h * steps].shape[0]
        mine[h * steps + k][at : at + half] = value[:, :block_cols]
        other[h + late][base + at : base + at + half] = value[:, block_cols:]

    for k, shift in enumerate(shifts):
        dest = partner(me, shift, peers)
        live = count_ref[0, 0, dest]
        marks = jnp.full(mark_slot.shape, VB_DEV, jnp.int32)
        for slot in range(capacity):
            target = jnp.where(slot < live, index_ref[1, 0, 0, dest, slot], VB_DEV)
            marks = jnp.where(mark_slot == slot, target, marks)
            group, at = divmod(slot, batch)
            picked = jnp.where(strip == at, row_scr[index_ref[2, 0, 0, dest, slot]], 0.0)
            row_mix[
                k * (capacity // batch) + group, at * block_rows : (at + 1) * block_rows
            ] = picked.astype(bf16)
        marks = marks.astype(f32)
        put(k, 0, capacity, jnp.concatenate([marks, jnp.zeros_like(marks)], 1))

    def tile(s, c, w):
        return window[s, c * rows : (c + 1) * rows, w * size : (w + 1) * size]

    def left(fields, matrix):
        parts = []
        for g in range(0, count, group):
            stack = jnp.concatenate(
                [jnp.concatenate([fields[w][c] for w in range(g, g + group)], 1) for c in (0, 1)], 0
            )
            parts.append(dot(matrix, stack).astype(bf16))
        return parts

    def right(parts, matrix):
        result = []
        for part in parts:
            stack = jnp.concatenate(
                [
                    jnp.concatenate(
                        [
                            part[c * size : (c + 1) * size, k * size : (k + 1) * size]
                            for c in (0, 1)
                        ],
                        1,
                    )
                    for k in range(group)
                ],
                0,
            )
            done = dot(stack, matrix).astype(bf16)
            for k in range(group):
                lines = done[k * size : (k + 1) * size]
                result.append((lines[:, :size], lines[:, size:]))
        return result

    def product(one, two, conjugate):
        a_re, a_im = one[0].astype(f32), one[1].astype(f32)
        b_re, b_im = two[0].astype(f32), two[1].astype(f32)
        if conjugate:
            re, im = a_re * b_re + a_im * b_im, a_re * b_im - a_im * b_re
        else:
            re, im = a_re * b_re - a_im * b_im, a_re * b_im + a_im * b_re
        return re.astype(bf16), im.astype(bf16)

    across = cols // block_cols
    psi, chi = {}, {}
    now = [(probe_ref[0], probe_ref[1])] * count
    back = [(cot_ref[0, w, 0], cot_ref[0, w, 1]) for w in range(count)]
    lane_down = lax.broadcasted_iota(jnp.int32, (size, cols), 0)
    col = lax.broadcasted_iota(jnp.int32, (size, cols), 1)
    paste = jnp.concatenate(
        [(col == lane_down + pos_ref[0, w]).astype(bf16) for w in range(count)], 0
    )
    for i in range(slices):
        s, e = i, slices - 1 - i
        psi[s], chi[e] = now, back
        if i + 1 < slices:
            here = [(tile(s, 0, w), tile(s, 1, w)) for w in range(count)]
            there = [(tile(e, 0, w), tile(e, 1, w)) for w in range(count)]
            passed = [product(here[w], now[w], False) for w in range(count)]
            rho = [product(there[w], back[w], True) for w in range(count)]
            now, back = left(passed, whole), left(rho, turned)
            now, back = right(now, turned), right(back, whole)
        for t in sorted({s, e}):
            if t not in psi or t not in chi or max(t, slices - 1 - t) != i:
                continue
            grads = [product(psi[t][w], chi[t][w], True) for w in range(count)]
            stack = jnp.concatenate(
                [jnp.concatenate([grads[w][c] for w in range(count)], 1) for c in (0, 1)], 0
            )
            spread = dot(stack, paste).astype(bf16)
            for c in (0, 1):
                for k in range(rows // block_rows):
                    top = c * rows + k * block_rows
                    for j in range(across):
                        band[c, (t * (rows // block_rows) + k) * across + j] = spread[
                            top : top + block_rows, j * block_cols : (j + 1) * block_cols
                        ]

    for k, shift in enumerate(shifts):
        dest = partner(me, shift, peers)
        for first in range(0, capacity, batch):
            inner = []
            for slot in range(first, first + batch, 2):
                pairs, factors = [], []
                for one in (slot, slot + 1):
                    block = index_ref[0, 0, 0, dest, one]
                    pairs += [band[core, block], band[1 - core, block]]
                    factors.append(col_bf[index_ref[2, 0, 0, dest, one]])
                mixed = dot(jnp.concatenate(pairs, 0), jnp.concatenate(factors, 1)).astype(bf16)
                for n in (0, 1):
                    lanes = slice(n * block_cols, (n + 1) * block_cols)
                    top = 2 * n * block_rows
                    inner.append(
                        jnp.concatenate(
                            [
                                mixed[top : top + block_rows, lanes],
                                mixed[top + block_rows : top + 2 * block_rows, lanes],
                            ],
                            1,
                        )
                    )
            result = dot(row_mix[k * (capacity // batch) + first // batch], jnp.concatenate(inner, 0))
            for slot in range(first, first + batch):
                for h in range(CHUNKS):
                    top = (slot - first) * block_rows + h * half
                    put(k, h, slot, result[top : top + half])


def join_kernel(base, after_ref, got_ref, part_ref, out_ref):
    out_ref[...] = part_ref[...] + got_ref[base : base + out_ref.shape[0]]


def place_kernel(sources, owners, first, *refs):
    tilt, core = lax.axis_index("tilt"), lax.axis_index("rep")
    tilts, cores = lax.axis_size("tilt"), lax.axis_size("rep")
    each = VB_DEV // (tilts * cores)
    blocks = refs[:sources]
    half, lanes = CHUNK_ROWS, blocks[0].shape[-1]
    size = each * half
    if first:
        outs, mark_ref = refs[sources:-1], refs[-1]
        for k, block in enumerate(blocks):
            mark_ref[k] = block[lanes:]
    else:
        mark_ref, outs = refs[sources], refs[sources + cores :]
    data = jnp.concatenate([block[:lanes].astype(jnp.bfloat16) for block in blocks], 0)
    volume = lax.broadcasted_iota(jnp.int32, (each, half, lanes), 0).astype(jnp.float32)
    for out, (dt, dr) in zip(outs, owners):
        owner = lax.rem(tilt + dt, tilts) * cores + lax.rem(core + dr, cores)
        base = (owner * each).astype(jnp.float32)
        hot = []
        for k in range(sources):
            mark = mark_ref[k] - base
            hit = jnp.where(volume == mark[None], 1.0, 0.0)
            hot.append(hit.reshape(size, lanes).astype(jnp.bfloat16))
        out[:size] = dot(jnp.concatenate(hot, 1), data)
        if out.shape[0] > size:
            out[size:] = jnp.zeros((out.shape[0] - size, out.shape[1]), jnp.float32)


def sum_kernel(owners, *refs):
    out_ref = refs[-1]
    core, cores = lax.axis_index("rep"), lax.axis_size("rep")
    each, cols = out_ref.shape[0], out_ref.shape[-1]
    size = each * CHUNK_ROWS
    for h in range(CHUNKS):
        parts = refs[h * len(owners) : (h + 1) * len(owners)]
        for dr in range(cores):
            values = [ref[:size] for ref, (_, r) in zip(parts, owners) if r == dr]
            total = functools.reduce(jnp.add, values).reshape(each, CHUNK_ROWS, cols)
            out_ref[:, lax.rem(core + dr, cores), pl.ds(h * CHUNK_ROWS, CHUNK_ROWS)] = total


def on_device(
    object_slab,
    probe_field,
    phases,
    cotangent,
    positions,
    pair_index,
    pair_counts,
    row_interp,
    col_interp,
):
    peers = lax.axis_size("slab")
    tilts, cores = lax.axis_size("tilt"), lax.axis_size("rep")
    shifts = slab_steps(peers)
    capacity = pair_index.shape[-1]
    block_rows, block_cols = row_interp.shape[-1], col_interp.shape[-1]
    _, _, slices, rows, cols = object_slab.shape
    windows, size = cotangent.shape[1], cotangent.shape[-1]
    f32, bf16 = jnp.float32, jnp.bfloat16
    hbm, vmem = pl.BlockSpec(memory_space=pltpu.HBM), pl.BlockSpec(memory_space=VMEM)
    limit = pltpu.CompilerParams(vmem_limit_bytes=40 * 1024 * 1024)
    sources = len(shifts)
    lanes = capacity * CHUNK_ROWS

    phase_line = phases.reshape(1, -1)
    table = jnp.asarray(angle_table(size))
    frames = (slices * (rows // block_rows) * (cols // block_cols), block_rows, block_cols)
    far = sources - 2
    tall = lanes + CHUNK_ROWS
    heights = [tall] * sources + [lanes] * sources
    swapped = [sources * tall, far * lanes, (sources - far) * lanes]
    shapes = [jax.ShapeDtypeStruct((tall, block_cols), f32) for tall in heights + swapped]
    fetched = [
        (phase_line, VMEM),
        (table, VMEM),
        (object_slab, VMEM),
        (probe_field, VMEM),
        (cotangent, VMEM),
        (row_interp, VMEM),
        (col_interp, VMEM),
    ]
    scalars = [positions, pair_index, pair_counts]
    held = pl.pallas_call(
        functools.partial(frame_kernel, shifts),
        out_shape=shapes,
        in_specs=[hbm] * 10,
        out_specs=[vmem] * len(shapes),
        scratch_shapes=[SMEM(x.shape, x.dtype) for x in scalars]
        + [space(x.shape, x.dtype) for x, space in fetched]
        + [
            pltpu.SemaphoreType.DMA((9 + slices,)),
            VMEM((2,) + frames, bf16),
            VMEM((slices, 2 * rows, windows * size), bf16),
            VMEM(col_interp.shape, bf16),
            VMEM((row_interp.shape[0], block_rows, 8 * block_rows), f32),
            VMEM((sources * capacity // 8, 8 * block_rows, 8 * block_rows), bf16),
        ],
        compiler_params=limit,
        name="frame",
    )(*[pltpu.with_memory_space_constraint(x, pltpu.HBM) for x in scalars + [x for x, _ in fetched]])

    swap = [(r, (r + 1) % cores) for r in range(cores)]
    owners = sorted(
        ((dt, dr) for dt in range(tilts) for dr in range(cores)), key=lambda o: (o[0] == 0, o)
    )
    each = VB_DEV // len(owners)
    share = jax.ShapeDtypeStruct((each * CHUNK_ROWS, block_cols), f32)
    mark = jax.ShapeDtypeStruct((sources, CHUNK_ROWS, block_cols), f32)
    padded = jax.ShapeDtypeStruct(((each + 1) * CHUNK_ROWS, block_cols), f32)
    mine, other = held[: len(heights)], held[len(heights) :]
    got = [lax.ppermute(half, "rep", swap) for half in other]

    def send(block, step):
        ring = [(p, partner(p, step, peers)) for p in range(peers)]
        return lax.ppermute(block, "slab", ring)

    def near_sum(h, k):
        part = mine[h * sources + k]
        late = h and k >= far
        at = (k - far if late else k) * part.shape[0]
        return part + got[h + late][at : at + part.shape[0]]

    def join(after, k):
        return pl.pallas_call(
            functools.partial(join_kernel, k * lanes),
            out_shape=shapes[sources],
            in_specs=[vmem] * 3,
            out_specs=vmem,
            compiler_params=limit,
            name="join",
        )(after, got[1], mine[sources + k])

    first = [send(near_sum(0, k), step) if step else near_sum(0, k) for k, step in enumerate(shifts)]
    second = [
        send(join(first[k], k) if k < far else near_sum(1, k), step) if step else near_sum(1, k)
        for k, step in enumerate(shifts)
    ]

    def place(blocks, extra, h):
        shapes = [padded if dt else share for dt, dr in owners] + [mark]
        if h:
            shapes = [share] * len(owners)
        return pl.pallas_call(
            functools.partial(place_kernel, sources, owners, h == 0),
            out_shape=shapes,
            in_specs=[vmem] * (sources + len(extra)),
            out_specs=[vmem] * len(shapes),
            compiler_params=limit,
            name="place",
        )(*blocks, *extra)

    def share_out(part, owner):
        dt, dr = owner
        if not (dt or dr):
            return part
        route = [
            (t * cores + r, (t + dt) % tilts * cores + (r + dr) % cores)
            for t in range(tilts)
            for r in range(cores)
        ]
        return lax.ppermute(part, ("tilt", "rep"), route)

    *parts, marks = place(first, [], 0)
    extra = [share_out(part, owner) for part, owner in zip(parts, owners)]
    held = [part for part, (dt, dr) in zip(extra, owners) if dr and not dt]
    late = place(second, [marks, *held], 1)
    extra += [share_out(part, owner) for part, owner in zip(late, owners)]
    return pl.pallas_call(
        functools.partial(sum_kernel, owners),
        out_shape=jax.ShapeDtypeStruct((each, cores, block_rows, block_cols), f32),
        in_specs=[vmem] * len(extra),
        out_specs=vmem,
        compiler_params=limit,
        name="total",
    )(*extra)


def solution(mesh):
    in_specs = (
        P(("groups", "tilt"), None, None, "slab", None),
        P(),
        P(),
        P(("groups", "tilt"), ("slab", "rep"), None, None, None),
        P(("groups", "tilt"), ("slab", "rep")),
        P(None, ("groups", "tilt"), "slab", None, None),
        P(("groups", "tilt"), "slab", None),
        P(),
        P(),
    )
    out_specs = P(("groups", "slab", "tilt", "rep"), None, None, None)
    return jax.shard_map(
        on_device, mesh=mesh, in_specs=in_specs, out_specs=out_specs, check_vma=False
    )
```

```python
import functools
import math

import jax
import jax.numpy as jnp
import numpy as np
from jax import lax
from jax.experimental import pallas as pl
from jax.experimental.pallas import tpu as pltpu
from jax.sharding import PartitionSpec as P

VB_DEV = 64
REACH = 3
CHUNKS = 2
CHUNK_ROWS = 8
HIGH = lax.Precision.HIGHEST
SMEM = pltpu.SMEM
VMEM = pltpu.VMEM


def dot(left, right, precision=None):
    return jnp.dot(left, right, precision=precision, preferred_element_type=jnp.float32)


def slab_steps(peers):
    if peers <= REACH + 1:
        return tuple(sorted(range(peers), key=lambda k: (k == 0, k < peers // 2, k)))
    ring = [s for k in range(REACH, 0, -1) for s in (peers - k, k)]
    return (*ring, 0)


def partner(slab, step, peers):
    if peers <= REACH + 1 and peers & (peers - 1) == 0:
        return slab ^ step
    return (slab + step) % peers


def angle_table(length):
    grid = np.arange(length)
    angles = (grid[:, None] * grid[None, :] % length) * (2.0 * math.pi / length)
    return np.concatenate([np.cos(angles), np.sin(angles)], axis=1).astype(np.float32)


def propagator_blocks(phases, table):
    length = phases.shape[-1]
    row = lax.broadcasted_iota(jnp.int32, (8, length), 0)
    waves = jnp.where(row == 0, jnp.cos(phases), jnp.sin(phases))
    sums = dot(waves, table, HIGH) * (1.0 / length)
    cc, cs = sums[0:1, :length], sums[0:1, length:]
    sc, ss = sums[1:2, :length], sums[1:2, length:]

    def circulant(line):
        wide = jnp.broadcast_to(line, (length, length))
        return pltpu.roll(wide, 0, 1, stride=1, stride_axis=0)

    kr, ki = circulant(cc + ss), circulant(sc - cs)
    krt, kit = circulant(cc - ss), circulant(sc + cs)
    whole = jnp.concatenate(
        [jnp.concatenate([kr, -ki], 1), jnp.concatenate([ki, kr], 1)], 0
    ).astype(jnp.bfloat16)
    turned = jnp.concatenate(
        [jnp.concatenate([krt, kit], 1), jnp.concatenate([-kit, krt], 1)], 0
    ).astype(jnp.bfloat16)
    return whole, turned


def frame_kernel(
    shifts,
    pos_hbm,
    index_hbm,
    count_hbm,
    phase_hbm,
    table_hbm,
    obj_hbm,
    probe_hbm,
    cot_hbm,
    row_hbm,
    col_hbm,
    *rest,
):
    far, steps = len(shifts) - 2, len(shifts)
    mine, other, scratch = rest[: 2 * steps], rest[2 * steps : 2 * steps + 3], rest[2 * steps + 3 :]
    pos_ref, index_ref, count_ref = scratch[0:3]
    phase_ref, table_ref, obj_ref, probe_ref, cot_ref, row_ref, col_ref = scratch[3:10]
    sems, band, window, col_bf, row_scr = scratch[10:]
    slices = obj_ref.shape[2]
    copies = [
        pltpu.make_async_copy(src, dst, sems.at[i])
        for i, (src, dst) in enumerate(
            [
                (phase_hbm, phase_ref),
                (table_hbm, table_ref),
                (pos_hbm, pos_ref),
                (probe_hbm, probe_ref),
                (index_hbm, index_ref),
                (count_hbm, count_ref),
                (row_hbm, row_ref),
            ]
        )
    ]
    got_phase, got_table, got_pos, got_probe, got_index, got_count, got_row = copies
    got_obj = [
        pltpu.make_async_copy(obj_hbm.at[0, :, s], obj_ref.at[0, :, s], sems.at[len(copies) + s])
        for s in range(slices)
    ]
    got_cot = pltpu.make_async_copy(cot_hbm, cot_ref, sems.at[len(copies) + slices])
    got_col = pltpu.make_async_copy(col_hbm, col_ref, sems.at[len(copies) + slices + 1])
    order = [s for i in range((slices + 1) // 2) for s in sorted({i, slices - 1 - i})]
    for copy in (got_pos, got_phase, got_table, *[got_obj[s] for s in order], got_probe, got_cot):
        copy.start()
    for copy in (got_index, got_count, got_row, got_col):
        copy.start()

    me, core = lax.axis_index("slab"), lax.axis_index("rep")
    peers = lax.axis_size("slab")
    capacity = index_ref.shape[-1]
    size = probe_ref.shape[-1]
    rows, cols = obj_ref.shape[3:]
    count = cot_ref.shape[1]
    group = 2 if count % 2 == 0 else 1
    f32, bf16 = jnp.float32, jnp.bfloat16

    got_pos.wait()
    got_phase.wait()
    got_table.wait()
    col_down = lax.broadcasted_iota(jnp.int32, (cols, size), 0)
    lane = lax.broadcasted_iota(jnp.int32, (cols, size), 1)
    cut = jnp.concatenate(
        [(col_down == lane + pos_ref[0, w]).astype(bf16) for w in range(count)], 1
    )
    whole, turned = propagator_blocks(phase_ref[...], table_ref[...])

    for s in order:
        got_obj[s].wait()
        source = jnp.concatenate([obj_ref[0, 0, s], obj_ref[0, 1, s]], 0)
        window[s] = dot(source, cut).astype(bf16)

    def tile(s, c, w):
        return window[s, c * rows : (c + 1) * rows, w * size : (w + 1) * size]

    def left(fields, matrix):
        parts = []
        for g in range(0, count, group):
            stack = jnp.concatenate(
                [jnp.concatenate([fields[w][c] for w in range(g, g + group)], 1) for c in (0, 1)], 0
            )
            parts.append(dot(matrix, stack).astype(bf16))
        return parts

    def right(parts, matrix):
        result = []
        for part in parts:
            stack = jnp.concatenate(
                [
                    jnp.concatenate(
                        [
                            part[c * size : (c + 1) * size, k * size : (k + 1) * size]
                            for c in (0, 1)
                        ],
                        1,
                    )
                    for k in range(group)
                ],
                0,
            )
            done = dot(stack, matrix).astype(bf16)
            for k in range(group):
                lines = done[k * size : (k + 1) * size]
                result.append((lines[:, :size], lines[:, size:]))
        return result

    def product(one, two, conjugate):
        a_re, a_im = one[0].astype(f32), one[1].astype(f32)
        b_re, b_im = two[0].astype(f32), two[1].astype(f32)
        if conjugate:
            re, im = a_re * b_re + a_im * b_im, a_re * b_im - a_im * b_re
        else:
            re, im = a_re * b_re - a_im * b_im, a_re * b_im + a_im * b_re
        return re.astype(bf16), im.astype(bf16)

    block_rows, block_cols = row_ref.shape[-1], col_ref.shape[-1]
    across = cols // block_cols
    psi, chi = {}, {}
    got_probe.wait()
    got_cot.wait()
    now = [(probe_ref[0], probe_ref[1])] * count
    back = [(cot_ref[0, w, 0], cot_ref[0, w, 1]) for w in range(count)]
    lane_down = lax.broadcasted_iota(jnp.int32, (size, cols), 0)
    col = lax.broadcasted_iota(jnp.int32, (size, cols), 1)
    paste = jnp.concatenate(
        [(col == lane_down + pos_ref[0, w]).astype(bf16) for w in range(count)], 0
    )
    for i in range(slices):
        s, e = i, slices - 1 - i
        psi[s], chi[e] = now, back
        if i + 1 < slices:
            here = [(tile(s, 0, w), tile(s, 1, w)) for w in range(count)]
            there = [(tile(e, 0, w), tile(e, 1, w)) for w in range(count)]
            passed = [product(here[w], now[w], False) for w in range(count)]
            rho = [product(there[w], back[w], True) for w in range(count)]
            now, back = left(passed, whole), left(rho, turned)
            now, back = right(now, turned), right(back, whole)
        for t in sorted({s, e}):
            if t not in psi or t not in chi or max(t, slices - 1 - t) != i:
                continue
            grads = [product(psi[t][w], chi[t][w], True) for w in range(count)]
            stack = jnp.concatenate(
                [jnp.concatenate([grads[w][c] for w in range(count)], 1) for c in (0, 1)], 0
            )
            spread = dot(stack, paste).astype(bf16)
            for c in (0, 1):
                for k in range(rows // block_rows):
                    top = c * rows + k * block_rows
                    for j in range(across):
                        band[c, (t * (rows // block_rows) + k) * across + j] = spread[
                            top : top + block_rows, j * block_cols : (j + 1) * block_cols
                        ]

    got_row.wait()
    got_col.wait()
    got_index.wait()
    got_count.wait()
    tiles = row_ref.shape[0]
    batch = 8
    wide = batch * block_rows
    col_bf[...] = col_ref[...].astype(bf16)
    down = lax.broadcasted_iota(jnp.int32, (block_rows, wide), 0)
    along = lax.broadcasted_iota(jnp.int32, (block_rows, wide), 1)
    repeat = (lax.rem(along, block_rows) == down).astype(bf16)
    row_wide = dot(row_ref[...].reshape(tiles * block_rows, block_rows).astype(bf16), repeat)
    row_scr[...] = row_wide.reshape(tiles, block_rows, wide)
    strip = lax.div(along, block_rows)
    half = block_rows // CHUNKS
    mark_down = lax.broadcasted_iota(jnp.int32, (half, capacity * half), 0)
    mark_along = lax.broadcasted_iota(jnp.int32, (half, capacity * half), 1)
    mark_slot = jnp.where(lax.rem(mark_along, half) == mark_down, lax.div(mark_along, half), -1)
    lines = capacity * half

    def put(k, h, slot, value):
        at = slot * half
        late = h and k >= far
        base = (k - far if late else k) * mine[h * steps].shape[0]
        mine[h * steps + k][at : at + half] = value[:, :block_cols]
        other[h + late][base + at : base + at + half] = value[:, block_cols:]

    for k, shift in enumerate(shifts):
        dest = partner(me, shift, peers)
        live = count_ref[0, 0, dest]
        marks = jnp.full(mark_slot.shape, VB_DEV, jnp.int32)
        for first in range(0, capacity, batch):
            inner, picks = [], []
            for slot in range(first, first + batch, 2):
                pairs, factors = [], []
                for one in (slot, slot + 1):
                    block = index_ref[0, 0, 0, dest, one]
                    target = index_ref[1, 0, 0, dest, one]
                    t = index_ref[2, 0, 0, dest, one]
                    target = jnp.where(one < live, target, VB_DEV)
                    marks = jnp.where(mark_slot == one, target, marks)
                    pairs += [band[core, block], band[1 - core, block]]
                    factors.append(col_bf[t])
                    picked = jnp.where(strip == one - first, row_scr[t], 0.0)
                    picks.append(picked.astype(bf16))
                mixed = dot(jnp.concatenate(pairs, 0), jnp.concatenate(factors, 1)).astype(bf16)
                for n in (0, 1):
                    lanes = slice(n * block_cols, (n + 1) * block_cols)
                    top = 2 * n * block_rows
                    inner.append(
                        jnp.concatenate(
                            [
                                mixed[top : top + block_rows, lanes],
                                mixed[top + block_rows : top + 2 * block_rows, lanes],
                            ],
                            1,
                        )
                    )
            result = dot(jnp.concatenate(picks, 0), jnp.concatenate(inner, 0))
            for slot in range(first, first + batch):
                for h in range(CHUNKS):
                    top = (slot - first) * block_rows + h * half
                    put(k, h, slot, result[top : top + half])
        marks = marks.astype(f32)
        put(k, 0, capacity, jnp.concatenate([marks, jnp.zeros_like(marks)], 1))


def join_kernel(after_ref, got_ref, *refs):
    count = len(refs) // 2
    for k, (part, out) in enumerate(zip(refs[:count], refs[count:])):
        tall = part.shape[0]
        out[...] = part[...] + got_ref[k * tall : (k + 1) * tall]


def place_kernel(sources, owners, first, *refs):
    tilt, core = lax.axis_index("tilt"), lax.axis_index("rep")
    tilts, cores = lax.axis_size("tilt"), lax.axis_size("rep")
    each = VB_DEV // (tilts * cores)
    blocks = refs[:sources]
    half, lanes = CHUNK_ROWS, blocks[0].shape[-1]
    size = each * half
    if first:
        outs, mark_ref = refs[sources:-1], refs[-1]
        for k, block in enumerate(blocks):
            mark_ref[k] = block[lanes:]
    else:
        mark_ref, outs = refs[sources], refs[sources + cores :]
    data = jnp.concatenate([block[:lanes].astype(jnp.bfloat16) for block in blocks], 0)
    volume = lax.broadcasted_iota(jnp.int32, (each, half, lanes), 0).astype(jnp.float32)
    for out, (dt, dr) in zip(outs, owners):
        owner = lax.rem(tilt + dt, tilts) * cores + lax.rem(core + dr, cores)
        base = (owner * each).astype(jnp.float32)
        hot = []
        for k in range(sources):
            mark = mark_ref[k] - base
            hit = jnp.where(volume == mark[None], 1.0, 0.0)
            hot.append(hit.reshape(size, lanes).astype(jnp.bfloat16))
        out[:size] = dot(jnp.concatenate(hot, 1), data)
        if out.shape[0] > size:
            out[size:] = jnp.zeros((out.shape[0] - size, out.shape[1]), jnp.float32)


def sum_kernel(owners, *refs):
    out_ref = refs[-1]
    core, cores = lax.axis_index("rep"), lax.axis_size("rep")
    each, cols = out_ref.shape[0], out_ref.shape[-1]
    size = each * CHUNK_ROWS
    for h in range(CHUNKS):
        parts = refs[h * len(owners) : (h + 1) * len(owners)]
        for dr in range(cores):
            values = [ref[:size] for ref, (_, r) in zip(parts, owners) if r == dr]
            total = functools.reduce(jnp.add, values).reshape(each, CHUNK_ROWS, cols)
            out_ref[:, lax.rem(core + dr, cores), pl.ds(h * CHUNK_ROWS, CHUNK_ROWS)] = total


def on_device(
    object_slab,
    probe_field,
    phases,
    cotangent,
    positions,
    pair_index,
    pair_counts,
    row_interp,
    col_interp,
):
    peers = lax.axis_size("slab")
    tilts, cores = lax.axis_size("tilt"), lax.axis_size("rep")
    shifts = slab_steps(peers)
    capacity = pair_index.shape[-1]
    block_rows, block_cols = row_interp.shape[-1], col_interp.shape[-1]
    _, _, slices, rows, cols = object_slab.shape
    windows, size = cotangent.shape[1], cotangent.shape[-1]
    f32, bf16 = jnp.float32, jnp.bfloat16
    hbm, vmem = pl.BlockSpec(memory_space=pltpu.HBM), pl.BlockSpec(memory_space=VMEM)
    limit = pltpu.CompilerParams(vmem_limit_bytes=40 * 1024 * 1024)
    sources = len(shifts)
    lanes = capacity * CHUNK_ROWS

    phase_line = phases.reshape(1, -1)
    table = jnp.asarray(angle_table(size))
    frames = (slices * (rows // block_rows) * (cols // block_cols), block_rows, block_cols)
    far = sources - 2
    tall = lanes + CHUNK_ROWS
    heights = [tall] * sources + [lanes] * sources
    swapped = [sources * tall, far * lanes, (sources - far) * lanes]
    shapes = [jax.ShapeDtypeStruct((tall, block_cols), f32) for tall in heights + swapped]
    fetched = [
        (phase_line, VMEM),
        (table, VMEM),
        (object_slab, VMEM),
        (probe_field, VMEM),
        (cotangent, VMEM),
        (row_interp, VMEM),
        (col_interp, VMEM),
    ]
    scalars = [positions, pair_index, pair_counts]
    held = pl.pallas_call(
        functools.partial(frame_kernel, shifts),
        out_shape=shapes,
        in_specs=[hbm] * 10,
        out_specs=[vmem] * len(shapes),
        scratch_shapes=[SMEM(x.shape, x.dtype) for x in scalars]
        + [space(x.shape, x.dtype) for x, space in fetched]
        + [
            pltpu.SemaphoreType.DMA((9 + slices,)),
            VMEM((2,) + frames, bf16),
            VMEM((slices, 2 * rows, windows * size), bf16),
            VMEM(col_interp.shape, bf16),
            VMEM((row_interp.shape[0], block_rows, 8 * block_rows), f32),
        ],
        compiler_params=limit,
        name="frame",
    )(*[pltpu.with_memory_space_constraint(x, pltpu.HBM) for x in scalars + [x for x, _ in fetched]])

    swap = [(r, (r + 1) % cores) for r in range(cores)]
    owners = sorted(
        ((dt, dr) for dt in range(tilts) for dr in range(cores)), key=lambda o: (o[0] == 0, o)
    )
    each = VB_DEV // len(owners)
    share = jax.ShapeDtypeStruct((each * CHUNK_ROWS, block_cols), f32)
    mark = jax.ShapeDtypeStruct((sources, CHUNK_ROWS, block_cols), f32)
    padded = jax.ShapeDtypeStruct(((each + 1) * CHUNK_ROWS, block_cols), f32)
    mine, other = held[: len(heights)], held[len(heights) :]
    got = [lax.ppermute(half, "rep", swap) for half in other]

    def send(block, step):
        ring = [(p, partner(p, step, peers)) for p in range(peers)]
        return lax.ppermute(block, "slab", ring)

    def core_sum(h, k):
        part = mine[h * sources + k]
        late = h and k >= far
        at = (k - far if late else k) * part.shape[0]
        return part + got[h + late][at : at + part.shape[0]]

    def send_all(blocks):
        return [send(block, step) if step else block for block, step in zip(blocks, shifts)]

    first = send_all([core_sum(0, k) for k in range(sources)])
    joined = pl.pallas_call(
        join_kernel,
        out_shape=[shapes[sources]] * far,
        in_specs=[vmem] * (far + 2),
        out_specs=[vmem] * far,
        compiler_params=limit,
        name="join",
    )(first[far - 1], got[1], *mine[sources : sources + far])
    second = send_all([*joined, *[core_sum(1, k) for k in range(far, sources)]])

    def place(blocks, extra, h):
        shapes = [padded if dt else share for dt, dr in owners] + [mark]
        if h:
            shapes = [share] * len(owners)
        return pl.pallas_call(
            functools.partial(place_kernel, sources, owners, h == 0),
            out_shape=shapes,
            in_specs=[vmem] * (sources + len(extra)),
            out_specs=[vmem] * len(shapes),
            compiler_params=limit,
            name="place",
        )(*blocks, *extra)

    def share_out(part, owner):
        dt, dr = owner
        if not (dt or dr):
            return part
        route = [
            (t * cores + r, (t + dt) % tilts * cores + (r + dr) % cores)
            for t in range(tilts)
            for r in range(cores)
        ]
        return lax.ppermute(part, ("tilt", "rep"), route)

    *parts, marks = place(first, [], 0)
    extra = [share_out(part, owner) for part, owner in zip(parts, owners)]
    held = [part for part, (dt, dr) in zip(extra, owners) if dr and not dt]
    late = place(second, [marks, *held], 1)
    extra += [share_out(part, owner) for part, owner in zip(late, owners)]
    return pl.pallas_call(
        functools.partial(sum_kernel, owners),
        out_shape=jax.ShapeDtypeStruct((each, cores, block_rows, block_cols), f32),
        in_specs=[vmem] * len(extra),
        out_specs=vmem,
        compiler_params=limit,
        name="total",
    )(*extra)


def solution(mesh):
    in_specs = (
        P(("groups", "tilt"), None, None, "slab", None),
        P(),
        P(),
        P(("groups", "tilt"), ("slab", "rep"), None, None, None),
        P(("groups", "tilt"), ("slab", "rep")),
        P(None, ("groups", "tilt"), "slab", None, None),
        P(("groups", "tilt"), "slab", None),
        P(),
        P(),
    )
    out_specs = P(("groups", "slab", "tilt", "rep"), None, None, None)
    return jax.shard_map(
        on_device, mesh=mesh, in_specs=in_specs, out_specs=out_specs, check_vma=False
    )
```

```python
import functools
import math

import jax
import jax.numpy as jnp
import numpy as np
from jax import lax
from jax.experimental import pallas as pl
from jax.experimental.pallas import tpu as pltpu
from jax.sharding import PartitionSpec as P

VB_DEV = 64
REACH = 3
CHUNKS = 2
CHUNK_ROWS = 8
HIGH = lax.Precision.HIGHEST
SMEM = pltpu.SMEM
VMEM = pltpu.VMEM


def dot(left, right, precision=None):
    return jnp.dot(left, right, precision=precision, preferred_element_type=jnp.float32)


def slab_steps(peers):
    if peers <= REACH + 1:
        return tuple(sorted(range(peers), key=lambda k: (k == 0, k < peers // 2, k)))
    ring = [s for k in range(REACH, 0, -1) for s in (peers - k, k)]
    return (*ring, 0)


def partner(slab, step, peers):
    if peers <= REACH + 1 and peers & (peers - 1) == 0:
        return slab ^ step
    return (slab + step) % peers


def angle_table(length):
    grid = np.arange(length)
    angles = (grid[:, None] * grid[None, :] % length) * (2.0 * math.pi / length)
    return np.concatenate([np.cos(angles), np.sin(angles)], axis=1).astype(np.float32)


def propagator_blocks(phases, table):
    length = phases.shape[-1]
    row = lax.broadcasted_iota(jnp.int32, (8, length), 0)
    waves = jnp.where(row == 0, jnp.cos(phases), jnp.sin(phases))
    sums = dot(waves, table, HIGH) * (1.0 / length)
    cc, cs = sums[0:1, :length], sums[0:1, length:]
    sc, ss = sums[1:2, :length], sums[1:2, length:]

    def circulant(line):
        wide = jnp.broadcast_to(line, (length, length))
        return pltpu.roll(wide, 0, 1, stride=1, stride_axis=0)

    kr, ki = circulant(cc + ss), circulant(sc - cs)
    krt, kit = circulant(cc - ss), circulant(sc + cs)
    whole = jnp.concatenate(
        [jnp.concatenate([kr, -ki], 1), jnp.concatenate([ki, kr], 1)], 0
    ).astype(jnp.bfloat16)
    turned = jnp.concatenate(
        [jnp.concatenate([krt, kit], 1), jnp.concatenate([-kit, krt], 1)], 0
    ).astype(jnp.bfloat16)
    return whole, turned


def frame_kernel(
    shifts,
    pos_hbm,
    index_hbm,
    count_hbm,
    phase_hbm,
    table_hbm,
    obj_hbm,
    probe_hbm,
    cot_hbm,
    row_hbm,
    col_hbm,
    *rest,
):
    far, steps = len(shifts) - 2, len(shifts)
    mine, other, scratch = rest[: 2 * steps], rest[2 * steps : 2 * steps + 2], rest[2 * steps + 2 :]
    pos_ref, index_ref, count_ref = scratch[0:3]
    phase_ref, table_ref, obj_ref, probe_ref, cot_ref, row_ref, col_ref = scratch[3:10]
    sems, band, window, col_bf, row_scr = scratch[10:]
    slices = obj_ref.shape[2]
    copies = [
        pltpu.make_async_copy(src, dst, sems.at[i])
        for i, (src, dst) in enumerate(
            [
                (phase_hbm, phase_ref),
                (table_hbm, table_ref),
                (pos_hbm, pos_ref),
                (probe_hbm, probe_ref),
                (index_hbm, index_ref),
                (count_hbm, count_ref),
                (row_hbm, row_ref),
            ]
        )
    ]
    got_phase, got_table, got_pos, got_probe, got_index, got_count, got_row = copies
    got_obj = [
        pltpu.make_async_copy(obj_hbm.at[0, :, s], obj_ref.at[0, :, s], sems.at[len(copies) + s])
        for s in range(slices)
    ]
    got_cot = pltpu.make_async_copy(cot_hbm, cot_ref, sems.at[len(copies) + slices])
    got_col = pltpu.make_async_copy(col_hbm, col_ref, sems.at[len(copies) + slices + 1])
    order = [s for i in range((slices + 1) // 2) for s in sorted({i, slices - 1 - i})]
    for copy in (got_pos, got_phase, got_table, *[got_obj[s] for s in order], got_probe, got_cot):
        copy.start()
    for copy in (got_index, got_count, got_row, got_col):
        copy.start()

    me, core = lax.axis_index("slab"), lax.axis_index("rep")
    peers = lax.axis_size("slab")
    capacity = index_ref.shape[-1]
    size = probe_ref.shape[-1]
    rows, cols = obj_ref.shape[3:]
    count = cot_ref.shape[1]
    group = 2 if count % 2 == 0 else 1
    f32, bf16 = jnp.float32, jnp.bfloat16

    got_pos.wait()
    got_phase.wait()
    got_table.wait()
    col_down = lax.broadcasted_iota(jnp.int32, (cols, size), 0)
    lane = lax.broadcasted_iota(jnp.int32, (cols, size), 1)
    cut = jnp.concatenate(
        [(col_down == lane + pos_ref[0, w]).astype(bf16) for w in range(count)], 1
    )
    whole, turned = propagator_blocks(phase_ref[...], table_ref[...])

    for copy in got_obj:
        copy.wait()
    got_probe.wait()
    got_cot.wait()
    got_row.wait()
    got_col.wait()
    got_index.wait()
    got_count.wait()
    for s in order:
        source = jnp.concatenate([obj_ref[0, 0, s], obj_ref[0, 1, s]], 0)
        window[s] = dot(source, cut).astype(bf16)

    def tile(s, c, w):
        return window[s, c * rows : (c + 1) * rows, w * size : (w + 1) * size]

    def left(fields, matrix):
        parts = []
        for g in range(0, count, group):
            stack = jnp.concatenate(
                [jnp.concatenate([fields[w][c] for w in range(g, g + group)], 1) for c in (0, 1)], 0
            )
            parts.append(dot(matrix, stack).astype(bf16))
        return parts

    def right(parts, matrix):
        result = []
        for part in parts:
            stack = jnp.concatenate(
                [
                    jnp.concatenate(
                        [
                            part[c * size : (c + 1) * size, k * size : (k + 1) * size]
                            for c in (0, 1)
                        ],
                        1,
                    )
                    for k in range(group)
                ],
                0,
            )
            done = dot(stack, matrix).astype(bf16)
            for k in range(group):
                lines = done[k * size : (k + 1) * size]
                result.append((lines[:, :size], lines[:, size:]))
        return result

    def product(one, two, conjugate):
        a_re, a_im = one[0].astype(f32), one[1].astype(f32)
        b_re, b_im = two[0].astype(f32), two[1].astype(f32)
        if conjugate:
            a_im = -a_im
        return (
            (a_re * b_re - a_im * b_im).astype(bf16),
            (a_re * b_im + a_im * b_re).astype(bf16),
        )

    block_rows, block_cols = row_ref.shape[-1], col_ref.shape[-1]
    across = cols // block_cols
    psi, chi = {}, {}
    now = [(probe_ref[0], probe_ref[1])] * count
    back = [(cot_ref[0, w, 0], cot_ref[0, w, 1]) for w in range(count)]
    lane_down = lax.broadcasted_iota(jnp.int32, (size, cols), 0)
    col = lax.broadcasted_iota(jnp.int32, (size, cols), 1)
    paste = jnp.concatenate(
        [(col == lane_down + pos_ref[0, w]).astype(bf16) for w in range(count)], 0
    )
    for i in range(slices):
        s, e = i, slices - 1 - i
        psi[s], chi[e] = now, back
        if i + 1 < slices:
            here = [(tile(s, 0, w), tile(s, 1, w)) for w in range(count)]
            there = [(tile(e, 0, w), tile(e, 1, w)) for w in range(count)]
            passed = [product(here[w], now[w], False) for w in range(count)]
            rho = [product(there[w], back[w], True) for w in range(count)]
            now, back = left(passed, whole), left(rho, turned)
            now, back = right(now, turned), right(back, whole)
        for t in sorted({s, e}):
            if t not in psi or t not in chi or max(t, slices - 1 - t) != i:
                continue
            grads = [product(psi[t][w], chi[t][w], True) for w in range(count)]
            stack = jnp.concatenate(
                [jnp.concatenate([grads[w][c] for w in range(count)], 1) for c in (0, 1)], 0
            )
            spread = dot(stack, paste).astype(bf16)
            for c in (0, 1):
                for k in range(rows // block_rows):
                    top = c * rows + k * block_rows
                    for j in range(across):
                        band[c, (t * (rows // block_rows) + k) * across + j] = spread[
                            top : top + block_rows, j * block_cols : (j + 1) * block_cols
                        ]

    tiles = row_ref.shape[0]
    batch = 8
    wide = batch * block_rows
    col_bf[...] = col_ref[...].astype(bf16)
    down = lax.broadcasted_iota(jnp.int32, (block_rows, wide), 0)
    along = lax.broadcasted_iota(jnp.int32, (block_rows, wide), 1)
    repeat = (lax.rem(along, block_rows) == down).astype(bf16)
    row_wide = dot(row_ref[...].reshape(tiles * block_rows, block_rows).astype(bf16), repeat)
    row_scr[...] = row_wide.reshape(tiles, block_rows, wide)
    strip = lax.div(along, block_rows)
    half = block_rows // CHUNKS
    mark_down = lax.broadcasted_iota(jnp.int32, (half, capacity * half), 0)
    mark_along = lax.broadcasted_iota(jnp.int32, (half, capacity * half), 1)
    mark_slot = jnp.where(lax.rem(mark_along, half) == mark_down, lax.div(mark_along, half), -1)
    lines = capacity * half
    late = (steps - far) * (lines + half)

    def put(k, h, slot, value):
        at = slot * half
        if h:
            swap, base = other[1], late + k * lines
        elif k < far:
            swap, base = other[0], k * (lines + half)
        else:
            swap, base = other[1], (k - far) * (lines + half)
        mine[h * steps + k][at : at + half] = value[:, :block_cols]
        swap[base + at : base + at + half] = value[:, block_cols:]

    for k, shift in enumerate(shifts):
        dest = partner(me, shift, peers)
        live = count_ref[0, 0, dest]
        marks = jnp.full(mark_slot.shape, VB_DEV, jnp.int32)
        for first in range(0, capacity, batch):
            inner, picks = [], []
            for slot in range(first, first + batch, 2):
                pairs, factors = [], []
                for one in (slot, slot + 1):
                    block = index_ref[0, 0, 0, dest, one]
                    target = index_ref[1, 0, 0, dest, one]
                    t = index_ref[2, 0, 0, dest, one]
                    target = jnp.where(one < live, target, VB_DEV)
                    marks = jnp.where(mark_slot == one, target, marks)
                    pairs += [band[core, block], band[1 - core, block]]
                    factors.append(col_bf[t])
                    picked = jnp.where(strip == one - first, row_scr[t], 0.0)
                    picks.append(picked.astype(bf16))
                mixed = dot(jnp.concatenate(pairs, 0), jnp.concatenate(factors, 1)).astype(bf16)
                for n in (0, 1):
                    lanes = slice(n * block_cols, (n + 1) * block_cols)
                    top = 2 * n * block_rows
                    inner.append(
                        jnp.concatenate(
                            [
                                mixed[top : top + block_rows, lanes],
                                mixed[top + block_rows : top + 2 * block_rows, lanes],
                            ],
                            1,
                        )
                    )
            result = dot(jnp.concatenate(picks, 0), jnp.concatenate(inner, 0))
            for slot in range(first, first + batch):
                for h in range(CHUNKS):
                    top = (slot - first) * block_rows + h * half
                    put(k, h, slot, result[top : top + half])
        marks = marks.astype(f32)
        put(k, 0, capacity, jnp.concatenate([marks, jnp.zeros_like(marks)], 1))


def keep_until(value, after):
    anywhere = pl.BlockSpec(memory_space=pl.ANY)

    def kernel(value_ref, after_ref, out_ref):
        pass

    return pl.pallas_call(
        kernel,
        out_shape=jax.ShapeDtypeStruct(value.shape, value.dtype),
        in_specs=[anywhere] * 2,
        out_specs=anywhere,
        input_output_aliases={0: 0},
        name="keep",
    )(value, after)


def join_kernel(base, first_ref, got_ref, *refs):
    count = len(refs) // 2
    for part, out in zip(refs[:count], refs[count:]):
        tall = part.shape[0]
        out[...] = part[...] + got_ref[base : base + tall]
        base += tall


def place_kernel(sources, owners, first, *refs):
    tilt, core = lax.axis_index("tilt"), lax.axis_index("rep")
    tilts, cores = lax.axis_size("tilt"), lax.axis_size("rep")
    each = VB_DEV // (tilts * cores)
    blocks = refs[:sources]
    half, lanes = CHUNK_ROWS, blocks[0].shape[-1]
    size = each * half
    if first:
        outs, mark_ref = refs[sources:-1], refs[-1]
        for k, block in enumerate(blocks):
            mark_ref[k] = block[lanes:]
    else:
        mark_ref, outs = refs[sources], refs[sources + cores :]
    data = jnp.concatenate([block[:lanes].astype(jnp.bfloat16) for block in blocks], 0)
    volume = lax.broadcasted_iota(jnp.int32, (each, half, lanes), 0).astype(jnp.float32)
    for out, (dt, dr) in zip(outs, owners):
        owner = lax.rem(tilt + dt, tilts) * cores + lax.rem(core + dr, cores)
        base = (owner * each).astype(jnp.float32)
        hot = []
        for k in range(sources):
            mark = mark_ref[k] - base
            hit = jnp.where(volume == mark[None], 1.0, 0.0)
            hot.append(hit.reshape(size, lanes).astype(jnp.bfloat16))
        out[:size] = dot(jnp.concatenate(hot, 1), data)
        if out.shape[0] > size:
            out[size:] = jnp.zeros((out.shape[0] - size, out.shape[1]), jnp.float32)


def sum_kernel(owners, *refs):
    out_ref = refs[-1]
    core, cores = lax.axis_index("rep"), lax.axis_size("rep")
    each, cols = out_ref.shape[0], out_ref.shape[-1]
    size = each * CHUNK_ROWS
    for h in range(CHUNKS):
        parts = refs[h * len(owners) : (h + 1) * len(owners)]
        for dr in range(cores):
            values = [ref[:size] for ref, (_, r) in zip(parts, owners) if r == dr]
            total = functools.reduce(jnp.add, values).reshape(each, CHUNK_ROWS, cols)
            out_ref[:, lax.rem(core + dr, cores), pl.ds(h * CHUNK_ROWS, CHUNK_ROWS)] = total


def on_device(
    object_slab,
    probe_field,
    phases,
    cotangent,
    positions,
    pair_index,
    pair_counts,
    row_interp,
    col_interp,
):
    peers = lax.axis_size("slab")
    tilts, cores = lax.axis_size("tilt"), lax.axis_size("rep")
    shifts = slab_steps(peers)
    capacity = pair_index.shape[-1]
    block_rows, block_cols = row_interp.shape[-1], col_interp.shape[-1]
    _, _, slices, rows, cols = object_slab.shape
    windows, size = cotangent.shape[1], cotangent.shape[-1]
    f32, bf16 = jnp.float32, jnp.bfloat16
    hbm, vmem = pl.BlockSpec(memory_space=pltpu.HBM), pl.BlockSpec(memory_space=VMEM)
    limit = pltpu.CompilerParams(vmem_limit_bytes=40 * 1024 * 1024)
    sources = len(shifts)
    lanes = capacity * CHUNK_ROWS

    phase_line = phases.reshape(1, -1)
    table = jnp.asarray(angle_table(size))
    frames = (slices * (rows // block_rows) * (cols // block_cols), block_rows, block_cols)
    far = sources - 2
    tall = lanes + CHUNK_ROWS
    heights = [tall] * sources + [lanes] * sources
    swapped = [far * tall, (sources - far) * tall + sources * lanes]
    shapes = [jax.ShapeDtypeStruct((tall, block_cols), f32) for tall in heights + swapped]
    fetched = [
        (phase_line, VMEM),
        (table, VMEM),
        (object_slab, VMEM),
        (probe_field, VMEM),
        (cotangent, VMEM),
        (row_interp, VMEM),
        (col_interp, VMEM),
    ]
    scalars = [positions, pair_index, pair_counts]
    held = pl.pallas_call(
        functools.partial(frame_kernel, shifts),
        out_shape=shapes,
        in_specs=[hbm] * 10,
        out_specs=[vmem] * len(shapes),
        scratch_shapes=[SMEM(x.shape, x.dtype) for x in scalars]
        + [space(x.shape, x.dtype) for x, space in fetched]
        + [
            pltpu.SemaphoreType.DMA((9 + slices,)),
            VMEM((2,) + frames, bf16),
            VMEM((slices, 2 * rows, windows * size), bf16),
            VMEM(col_interp.shape, bf16),
            VMEM((row_interp.shape[0], block_rows, 8 * block_rows), f32),
        ],
        compiler_params=limit,
        name="frame",
    )(*[pltpu.with_memory_space_constraint(x, pltpu.HBM) for x in scalars + [x for x, _ in fetched]])

    swap = [(r, (r + 1) % cores) for r in range(cores)]
    owners = sorted(
        ((dt, dr) for dt in range(tilts) for dr in range(cores)), key=lambda o: (o[0] == 0, o)
    )
    each = VB_DEV // len(owners)
    share = jax.ShapeDtypeStruct((each * CHUNK_ROWS, block_cols), f32)
    mark = jax.ShapeDtypeStruct((sources, CHUNK_ROWS, block_cols), f32)
    padded = jax.ShapeDtypeStruct(((each + 1) * CHUNK_ROWS, block_cols), f32)
    mine, other = held[: len(heights)], held[len(heights) :]
    got = [lax.ppermute(other[0], "rep", swap)]
    got.append(lax.ppermute(keep_until(other[1], got[0]), "rep", swap))

    def send(block, step):
        ring = [(p, partner(p, step, peers)) for p in range(peers)]
        return lax.ppermute(block, "slab", ring)

    first = []
    for k in range(sources):
        h, at = (0, k * tall) if k < far else (1, (k - far) * tall)
        block = mine[k] + got[h][at : at + tall]
        first.append(send(block, shifts[k]) if shifts[k] else block)
    def join(after, part):
        late = mine[sources:][part]
        return pl.pallas_call(
            functools.partial(join_kernel, (sources - far) * tall + part.start * lanes),
            out_shape=shapes[sources : 2 * sources][part],
            in_specs=[vmem] * (len(late) + 2),
            out_specs=[vmem] * len(late),
            compiler_params=limit,
            name="join",
        )(after, got[1], *late)

    def place(blocks, extra, h):
        shapes = [padded if dt else share for dt, dr in owners] + [mark]
        if h:
            shapes = [share] * len(owners)
        return pl.pallas_call(
            functools.partial(place_kernel, sources, owners, h == 0),
            out_shape=shapes,
            in_specs=[vmem] * (sources + len(extra)),
            out_specs=[vmem] * len(shapes),
            compiler_params=limit,
            name="place",
        )(*blocks, *extra)

    def share_out(part, owner):
        dt, dr = owner
        if not (dt or dr):
            return part
        route = [
            (t * cores + r, (t + dt) % tilts * cores + (r + dr) % cores)
            for t in range(tilts)
            for r in range(cores)
        ]
        return lax.ppermute(part, ("tilt", "rep"), route)

    joined = []
    for k in range(far):
        joined += join(first[k], slice(k, k + 1 if k + 1 < far else sources))
    second = [send(block, k) if k else block for block, k in zip(joined, shifts)]
    *parts, marks = place(first, [], 0)
    extra = [share_out(part, owner) for part, owner in zip(parts, owners)]
    held = [part for part, (dt, dr) in zip(extra, owners) if dr and not dt]
    late = place(second, [marks, *held], 1)
    extra += [share_out(part, owner) for part, owner in zip(late, owners)]
    return pl.pallas_call(
        functools.partial(sum_kernel, owners),
        out_shape=jax.ShapeDtypeStruct((each, cores, block_rows, block_cols), f32),
        in_specs=[vmem] * len(extra),
        out_specs=vmem,
        compiler_params=limit,
        name="total",
    )(*extra)


def solution(mesh):
    in_specs = (
        P(("groups", "tilt"), None, None, "slab", None),
        P(),
        P(),
        P(("groups", "tilt"), ("slab", "rep"), None, None, None),
        P(("groups", "tilt"), ("slab", "rep")),
        P(None, ("groups", "tilt"), "slab", None, None),
        P(("groups", "tilt"), "slab", None),
        P(),
        P(),
    )
    out_specs = P(("groups", "slab", "tilt", "rep"), None, None, None)
    return jax.shard_map(
        on_device, mesh=mesh, in_specs=in_specs, out_specs=out_specs, check_vma=False
    )
```

```python
import functools
import math

import jax
import jax.numpy as jnp
import numpy as np
from jax import lax
from jax.experimental import pallas as pl
from jax.experimental.pallas import tpu as pltpu
from jax.sharding import PartitionSpec as P

VB_DEV = 64
REACH = 3
CHUNKS = 2
CHUNK_ROWS = 8
HIGH = lax.Precision.HIGHEST
SMEM = pltpu.SMEM
VMEM = pltpu.VMEM
LIMIT = pltpu.CompilerParams(vmem_limit_bytes=40 * 1024 * 1024)


def dot(left, right, precision=None):
    return jnp.dot(left, right, precision=precision, preferred_element_type=jnp.float32)


def slab_steps(peers):
    if peers <= REACH + 1:
        return tuple(sorted(range(peers), key=lambda k: (k == 0, k < peers // 2, k)))
    ring = [s for k in range(REACH, 0, -1) for s in (peers - k, k)]
    return (*ring, 0)


def partner(slab, step, peers):
    if peers <= REACH + 1 and peers & (peers - 1) == 0:
        return slab ^ step
    return (slab + step) % peers


def angle_table(length):
    grid = np.arange(length)
    angles = (grid[:, None] * grid[None, :] % length) * (2.0 * math.pi / length)
    return np.concatenate([np.cos(angles), np.sin(angles)], axis=1).astype(np.float32)


def propagator_blocks(phases, table):
    length = phases.shape[-1]
    row = lax.broadcasted_iota(jnp.int32, (8, length), 0)
    waves = jnp.where(row == 0, jnp.cos(phases), jnp.sin(phases))
    sums = dot(waves, table, HIGH) * (1.0 / length)
    cc, cs = sums[0:1, :length], sums[0:1, length:]
    sc, ss = sums[1:2, :length], sums[1:2, length:]

    def circulant(line):
        wide = jnp.broadcast_to(line, (length, length))
        return pltpu.roll(wide, 0, 1, stride=1, stride_axis=0)

    kr, ki = circulant(cc + ss), circulant(sc - cs)
    krt, kit = circulant(cc - ss), circulant(sc + cs)
    whole = jnp.concatenate(
        [jnp.concatenate([kr, -ki], 1), jnp.concatenate([ki, kr], 1)], 0
    ).astype(jnp.bfloat16)
    turned = jnp.concatenate(
        [jnp.concatenate([krt, kit], 1), jnp.concatenate([-kit, krt], 1)], 0
    ).astype(jnp.bfloat16)
    return whole, turned


def frame_kernel(
    shifts,
    pos_hbm,
    index_hbm,
    count_hbm,
    phase_hbm,
    table_hbm,
    obj_hbm,
    probe_hbm,
    cot_hbm,
    row_hbm,
    col_hbm,
    *rest,
):
    far, steps = len(shifts) - 2, len(shifts)
    mine, other, scratch = rest[: 2 * steps], rest[2 * steps : 2 * steps + 2], rest[2 * steps + 2 :]
    pos_ref, index_ref, count_ref = scratch[0:3]
    phase_ref, table_ref, obj_ref, probe_ref, cot_ref, row_ref, col_ref = scratch[3:10]
    sems, band, window, col_bf, row_scr = scratch[10:]
    slices = obj_ref.shape[2]
    copies = [
        pltpu.make_async_copy(src, dst, sems.at[i])
        for i, (src, dst) in enumerate(
            [
                (phase_hbm, phase_ref),
                (table_hbm, table_ref),
                (pos_hbm, pos_ref),
                (probe_hbm, probe_ref),
                (index_hbm, index_ref),
                (count_hbm, count_ref),
                (row_hbm, row_ref),
            ]
        )
    ]
    got_phase, got_table, got_pos, got_probe, got_index, got_count, got_row = copies
    got_obj = [
        pltpu.make_async_copy(obj_hbm.at[0, :, s], obj_ref.at[0, :, s], sems.at[len(copies) + s])
        for s in range(slices)
    ]
    got_cot = pltpu.make_async_copy(cot_hbm, cot_ref, sems.at[len(copies) + slices])
    got_col = pltpu.make_async_copy(col_hbm, col_ref, sems.at[len(copies) + slices + 1])
    order = [s for i in range((slices + 1) // 2) for s in sorted({i, slices - 1 - i})]
    for copy in (got_pos, got_phase, got_table, *[got_obj[s] for s in order], got_probe, got_cot):
        copy.start()
    for copy in (got_index, got_count, got_row, got_col):
        copy.start()

    me, core = lax.axis_index("slab"), lax.axis_index("rep")
    peers = lax.axis_size("slab")
    capacity = index_ref.shape[-1]
    size = probe_ref.shape[-1]
    rows, cols = obj_ref.shape[3:]
    count = cot_ref.shape[1]
    group = 2 if count % 2 == 0 else 1
    f32, bf16 = jnp.float32, jnp.bfloat16

    got_pos.wait()
    got_phase.wait()
    got_table.wait()
    col_down = lax.broadcasted_iota(jnp.int32, (cols, size), 0)
    lane = lax.broadcasted_iota(jnp.int32, (cols, size), 1)
    cut = jnp.concatenate(
        [(col_down == lane + pos_ref[0, w]).astype(bf16) for w in range(count)], 1
    )
    whole, turned = propagator_blocks(phase_ref[...], table_ref[...])

    for copy in got_obj:
        copy.wait()
    got_probe.wait()
    got_cot.wait()
    got_row.wait()
    got_col.wait()
    got_index.wait()
    got_count.wait()
    for s in order:
        source = jnp.concatenate([obj_ref[0, 0, s], obj_ref[0, 1, s]], 0)
        window[s] = dot(source, cut).astype(bf16)

    def tile(s, c, w):
        return window[s, c * rows : (c + 1) * rows, w * size : (w + 1) * size]

    def left(fields, matrix):
        parts = []
        for g in range(0, count, group):
            stack = jnp.concatenate(
                [jnp.concatenate([fields[w][c] for w in range(g, g + group)], 1) for c in (0, 1)], 0
            )
            parts.append(dot(matrix, stack).astype(bf16))
        return parts

    def right(parts, matrix):
        result = []
        for part in parts:
            stack = jnp.concatenate(
                [
                    jnp.concatenate(
                        [
                            part[c * size : (c + 1) * size, k * size : (k + 1) * size]
                            for c in (0, 1)
                        ],
                        1,
                    )
                    for k in range(group)
                ],
                0,
            )
            done = dot(stack, matrix).astype(bf16)
            for k in range(group):
                lines = done[k * size : (k + 1) * size]
                result.append((lines[:, :size], lines[:, size:]))
        return result

    def product(one, two, conjugate):
        a_re, a_im = one[0].astype(f32), one[1].astype(f32)
        b_re, b_im = two[0].astype(f32), two[1].astype(f32)
        if conjugate:
            a_im = -a_im
        return (
            (a_re * b_re - a_im * b_im).astype(bf16),
            (a_re * b_im + a_im * b_re).astype(bf16),
        )

    block_rows, block_cols = row_ref.shape[-1], col_ref.shape[-1]
    across = cols // block_cols
    psi, chi = {}, {}
    now = [(probe_ref[0], probe_ref[1])] * count
    back = [(cot_ref[0, w, 0], cot_ref[0, w, 1]) for w in range(count)]
    lane_down = lax.broadcasted_iota(jnp.int32, (size, cols), 0)
    col = lax.broadcasted_iota(jnp.int32, (size, cols), 1)
    paste = jnp.concatenate(
        [(col == lane_down + pos_ref[0, w]).astype(bf16) for w in range(count)], 0
    )
    for i in range(slices):
        s, e = i, slices - 1 - i
        psi[s], chi[e] = now, back
        if i + 1 < slices:
            here = [(tile(s, 0, w), tile(s, 1, w)) for w in range(count)]
            there = [(tile(e, 0, w), tile(e, 1, w)) for w in range(count)]
            passed = [product(here[w], now[w], False) for w in range(count)]
            rho = [product(there[w], back[w], True) for w in range(count)]
            now, back = left(passed, whole), left(rho, turned)
            now, back = right(now, turned), right(back, whole)
        for t in sorted({s, e}):
            if t not in psi or t not in chi or max(t, slices - 1 - t) != i:
                continue
            grads = [product(psi[t][w], chi[t][w], True) for w in range(count)]
            stack = jnp.concatenate(
                [jnp.concatenate([grads[w][c] for w in range(count)], 1) for c in (0, 1)], 0
            )
            spread = dot(stack, paste).astype(bf16)
            for c in (0, 1):
                for k in range(rows // block_rows):
                    top = c * rows + k * block_rows
                    for j in range(across):
                        band[c, (t * (rows // block_rows) + k) * across + j] = spread[
                            top : top + block_rows, j * block_cols : (j + 1) * block_cols
                        ]

    tiles = row_ref.shape[0]
    batch = 8
    wide = batch * block_rows
    col_bf[...] = col_ref[...].astype(bf16)
    down = lax.broadcasted_iota(jnp.int32, (block_rows, wide), 0)
    along = lax.broadcasted_iota(jnp.int32, (block_rows, wide), 1)
    repeat = (lax.rem(along, block_rows) == down).astype(bf16)
    row_wide = dot(row_ref[...].reshape(tiles * block_rows, block_rows).astype(bf16), repeat)
    row_scr[...] = row_wide.reshape(tiles, block_rows, wide)
    strip = lax.div(along, block_rows)
    half = block_rows // CHUNKS
    mark_down = lax.broadcasted_iota(jnp.int32, (half, capacity * half), 0)
    mark_along = lax.broadcasted_iota(jnp.int32, (half, capacity * half), 1)
    mark_slot = jnp.where(lax.rem(mark_along, half) == mark_down, lax.div(mark_along, half), -1)
    lines = capacity * half
    late = (steps - far) * (lines + half)

    def put(k, h, slot, value):
        at = slot * half
        if h:
            swap, base = other[1], late + k * lines
        elif k < far:
            swap, base = other[0], k * (lines + half)
        else:
            swap, base = other[1], (k - far) * (lines + half)
        mine[h * steps + k][at : at + half] = value[:, :block_cols]
        swap[base + at : base + at + half] = value[:, block_cols:]

    for k, shift in enumerate(shifts):
        dest = partner(me, shift, peers)
        live = count_ref[0, 0, dest]
        marks = jnp.full(mark_slot.shape, VB_DEV, jnp.int32)
        for first in range(0, capacity, batch):
            inner, picks = [], []
            for slot in range(first, first + batch, 2):
                pairs, factors = [], []
                for one in (slot, slot + 1):
                    block = index_ref[0, 0, 0, dest, one]
                    target = index_ref[1, 0, 0, dest, one]
                    t = index_ref[2, 0, 0, dest, one]
                    target = jnp.where(one < live, target, VB_DEV)
                    marks = jnp.where(mark_slot == one, target, marks)
                    pairs += [band[core, block], band[1 - core, block]]
                    factors.append(col_bf[t])
                    picked = jnp.where(strip == one - first, row_scr[t], 0.0)
                    picks.append(picked.astype(bf16))
                mixed = dot(jnp.concatenate(pairs, 0), jnp.concatenate(factors, 1)).astype(bf16)
                for n in (0, 1):
                    lanes = slice(n * block_cols, (n + 1) * block_cols)
                    top = 2 * n * block_rows
                    inner.append(
                        jnp.concatenate(
                            [
                                mixed[top : top + block_rows, lanes],
                                mixed[top + block_rows : top + 2 * block_rows, lanes],
                            ],
                            1,
                        )
                    )
            result = dot(jnp.concatenate(picks, 0), jnp.concatenate(inner, 0))
            for slot in range(first, first + batch):
                for h in range(CHUNKS):
                    top = (slot - first) * block_rows + h * half
                    put(k, h, slot, result[top : top + half])
        marks = marks.astype(f32)
        put(k, 0, capacity, jnp.concatenate([marks, jnp.zeros_like(marks)], 1))


def keep_until(value, after):
    anywhere = pl.BlockSpec(memory_space=pl.ANY)

    def kernel(value_ref, after_ref, out_ref):
        pass

    return pl.pallas_call(
        kernel,
        out_shape=jax.ShapeDtypeStruct(value.shape, value.dtype),
        in_specs=[anywhere] * 2,
        out_specs=anywhere,
        input_output_aliases={0: 0},
        compiler_params=LIMIT,
        name="keep",
    )(value, after)


def join_kernel(base, first_ref, got_ref, *refs):
    count = len(refs) // 2
    for part, out in zip(refs[:count], refs[count:]):
        tall = part.shape[0]
        out[...] = part[...] + got_ref[base : base + tall]
        base += tall


def place_kernel(sources, owners, first, *refs):
    tilt, core = lax.axis_index("tilt"), lax.axis_index("rep")
    tilts, cores = lax.axis_size("tilt"), lax.axis_size("rep")
    each = VB_DEV // (tilts * cores)
    blocks = refs[:sources]
    half, lanes = CHUNK_ROWS, blocks[0].shape[-1]
    size = each * half
    if first:
        outs, mark_ref = refs[sources:-1], refs[-1]
        for k, block in enumerate(blocks):
            mark_ref[k] = block[lanes:]
    else:
        mark_ref, outs = refs[sources], refs[sources + cores :]
    data = jnp.concatenate([block[:lanes].astype(jnp.bfloat16) for block in blocks], 0)
    volume = lax.broadcasted_iota(jnp.int32, (each, half, lanes), 0).astype(jnp.float32)
    for out, (dt, dr) in zip(outs, owners):
        owner = lax.rem(tilt + dt, tilts) * cores + lax.rem(core + dr, cores)
        base = (owner * each).astype(jnp.float32)
        hot = []
        for k in range(sources):
            mark = mark_ref[k] - base
            hit = jnp.where(volume == mark[None], 1.0, 0.0)
            hot.append(hit.reshape(size, lanes).astype(jnp.bfloat16))
        out[:size] = dot(jnp.concatenate(hot, 1), data)
        if out.shape[0] > size:
            out[size:] = jnp.zeros((out.shape[0] - size, out.shape[1]), jnp.float32)


def sum_kernel(owners, *refs):
    out_ref = refs[-1]
    core, cores = lax.axis_index("rep"), lax.axis_size("rep")
    each, cols = out_ref.shape[0], out_ref.shape[-1]
    size = each * CHUNK_ROWS
    for h in range(CHUNKS):
        parts = refs[h * len(owners) : (h + 1) * len(owners)]
        for dr in range(cores):
            values = [ref[:size] for ref, (_, r) in zip(parts, owners) if r == dr]
            total = functools.reduce(jnp.add, values).reshape(each, CHUNK_ROWS, cols)
            out_ref[:, lax.rem(core + dr, cores), pl.ds(h * CHUNK_ROWS, CHUNK_ROWS)] = total


def on_device(
    object_slab,
    probe_field,
    phases,
    cotangent,
    positions,
    pair_index,
    pair_counts,
    row_interp,
    col_interp,
):
    peers = lax.axis_size("slab")
    tilts, cores = lax.axis_size("tilt"), lax.axis_size("rep")
    shifts = slab_steps(peers)
    capacity = pair_index.shape[-1]
    block_rows, block_cols = row_interp.shape[-1], col_interp.shape[-1]
    _, _, slices, rows, cols = object_slab.shape
    windows, size = cotangent.shape[1], cotangent.shape[-1]
    f32, bf16 = jnp.float32, jnp.bfloat16
    hbm, vmem = pl.BlockSpec(memory_space=pltpu.HBM), pl.BlockSpec(memory_space=VMEM)
    sources = len(shifts)
    lanes = capacity * CHUNK_ROWS

    phase_line = phases.reshape(1, -1)
    table = jnp.asarray(angle_table(size))
    frames = (slices * (rows // block_rows) * (cols // block_cols), block_rows, block_cols)
    far = sources - 2
    tall = lanes + CHUNK_ROWS
    heights = [tall] * sources + [lanes] * sources
    swapped = [far * tall, (sources - far) * tall + sources * lanes]
    shapes = [jax.ShapeDtypeStruct((tall, block_cols), f32) for tall in heights + swapped]
    fetched = [
        (phase_line, VMEM),
        (table, VMEM),
        (object_slab, VMEM),
        (probe_field, VMEM),
        (cotangent, VMEM),
        (row_interp, VMEM),
        (col_interp, VMEM),
    ]
    scalars = [positions, pair_index, pair_counts]
    held = pl.pallas_call(
        functools.partial(frame_kernel, shifts),
        out_shape=shapes,
        in_specs=[hbm] * 10,
        out_specs=[vmem] * len(shapes),
        scratch_shapes=[SMEM(x.shape, x.dtype) for x in scalars]
        + [space(x.shape, x.dtype) for x, space in fetched]
        + [
            pltpu.SemaphoreType.DMA((9 + slices,)),
            VMEM((2,) + frames, bf16),
            VMEM((slices, 2 * rows, windows * size), bf16),
            VMEM(col_interp.shape, bf16),
            VMEM((row_interp.shape[0], block_rows, 8 * block_rows), f32),
        ],
        compiler_params=LIMIT,
        name="frame",
    )(*[pltpu.with_memory_space_constraint(x, pltpu.HBM) for x in scalars + [x for x, _ in fetched]])

    swap = [(r, (r + 1) % cores) for r in range(cores)]
    owners = sorted(
        ((dt, dr) for dt in range(tilts) for dr in range(cores)), key=lambda o: (o[0] == 0, o)
    )
    each = VB_DEV // len(owners)
    share = jax.ShapeDtypeStruct((each * CHUNK_ROWS, block_cols), f32)
    mark = jax.ShapeDtypeStruct((sources, CHUNK_ROWS, block_cols), f32)
    padded = jax.ShapeDtypeStruct(((each + 1) * CHUNK_ROWS, block_cols), f32)
    mine, other = held[: len(heights)], held[len(heights) :]
    got = [lax.ppermute(other[0], "rep", swap)]
    got.append(lax.ppermute(keep_until(other[1], got[0]), "rep", swap))

    def send(block, step):
        ring = [(p, partner(p, step, peers)) for p in range(peers)]
        return lax.ppermute(block, "slab", ring)

    first = []
    for k in range(sources):
        h, at = (0, k * tall) if k < far else (1, (k - far) * tall)
        block = mine[k] + got[h][at : at + tall]
        first.append(send(block, shifts[k]) if shifts[k] else block)
    def join(after, part):
        late = mine[sources:][part]
        return pl.pallas_call(
            functools.partial(join_kernel, (sources - far) * tall + part.start * lanes),
            out_shape=shapes[sources : 2 * sources][part],
            in_specs=[vmem] * (len(late) + 2),
            out_specs=[vmem] * len(late),
            compiler_params=LIMIT,
            name="join",
        )(after, got[1], *late)

    def place(blocks, extra, h):
        shapes = [padded if dt else share for dt, dr in owners] + [mark]
        if h:
            shapes = [share] * len(owners)
        return pl.pallas_call(
            functools.partial(place_kernel, sources, owners, h == 0),
            out_shape=shapes,
            in_specs=[vmem] * (sources + len(extra)),
            out_specs=[vmem] * len(shapes),
            compiler_params=LIMIT,
            name="place",
        )(*blocks, *extra)

    def share_out(part, owner):
        dt, dr = owner
        if not (dt or dr):
            return part
        route = [
            (t * cores + r, (t + dt) % tilts * cores + (r + dr) % cores)
            for t in range(tilts)
            for r in range(cores)
        ]
        return lax.ppermute(part, ("tilt", "rep"), route)

    joined = []
    for k in range(far):
        joined += join(first[k], slice(k, k + 1 if k + 1 < far else sources))
    second = [send(block, k) if k else block for block, k in zip(joined, shifts)]
    *parts, marks = place(first, [], 0)
    extra = [share_out(part, owner) for part, owner in zip(parts, owners)]
    held = [part for part, (dt, dr) in zip(extra, owners) if dr and not dt]
    late = place(second, [marks, *held], 1)
    extra += [share_out(part, owner) for part, owner in zip(late, owners)]
    return pl.pallas_call(
        functools.partial(sum_kernel, owners),
        out_shape=jax.ShapeDtypeStruct((each, cores, block_rows, block_cols), f32),
        in_specs=[vmem] * len(extra),
        out_specs=vmem,
        compiler_params=LIMIT,
        name="total",
    )(*extra)


def solution(mesh):
    in_specs = (
        P(("groups", "tilt"), None, None, "slab", None),
        P(),
        P(),
        P(("groups", "tilt"), ("slab", "rep"), None, None, None),
        P(("groups", "tilt"), ("slab", "rep")),
        P(None, ("groups", "tilt"), "slab", None, None),
        P(("groups", "tilt"), "slab", None),
        P(),
        P(),
    )
    out_specs = P(("groups", "slab", "tilt", "rep"), None, None, None)
    return jax.shard_map(
        on_device, mesh=mesh, in_specs=in_specs, out_specs=out_specs, check_vma=False
    )
```

```python
import functools
import math

import jax
import jax.numpy as jnp
import numpy as np
from jax import lax
from jax.experimental import pallas as pl
from jax.experimental.pallas import tpu as pltpu
from jax.sharding import PartitionSpec as P

VB_DEV = 64
REACH = 3
CHUNKS = 2
CHUNK_ROWS = 8
HIGH = lax.Precision.HIGHEST
SMEM = pltpu.SMEM
VMEM = pltpu.VMEM
LIMIT = pltpu.CompilerParams(vmem_limit_bytes=40 * 1024 * 1024)


def dot(left, right, precision=None):
    return jnp.dot(left, right, precision=precision, preferred_element_type=jnp.float32)


def slab_steps(peers):
    if peers <= REACH + 1:
        return tuple(sorted(range(peers), key=lambda k: (k == 0, k < peers // 2, k)))
    ring = [s for k in range(REACH, 0, -1) for s in (peers - k, k)]
    return (*ring, 0)


def partner(slab, step, peers):
    if peers <= REACH + 1 and peers & (peers - 1) == 0:
        return slab ^ step
    return (slab + step) % peers


def angle_table(length):
    grid = np.arange(length)
    angles = (grid[:, None] * grid[None, :] % length) * (2.0 * math.pi / length)
    return np.concatenate([np.cos(angles), np.sin(angles)], axis=1).astype(np.float32)


def propagator_blocks(phases, table):
    length = phases.shape[-1]
    row = lax.broadcasted_iota(jnp.int32, (8, length), 0)
    waves = jnp.where(row == 0, jnp.cos(phases), jnp.sin(phases))
    sums = dot(waves, table, HIGH) * (1.0 / length)
    cc, cs = sums[0:1, :length], sums[0:1, length:]
    sc, ss = sums[1:2, :length], sums[1:2, length:]

    def circulant(line):
        wide = jnp.broadcast_to(line, (length, length))
        return pltpu.roll(wide, 0, 1, stride=1, stride_axis=0)

    kr, ki = circulant(cc + ss), circulant(sc - cs)
    krt, kit = circulant(cc - ss), circulant(sc + cs)
    whole = jnp.concatenate(
        [jnp.concatenate([kr, -ki], 1), jnp.concatenate([ki, kr], 1)], 0
    ).astype(jnp.bfloat16)
    turned = jnp.concatenate(
        [jnp.concatenate([krt, kit], 1), jnp.concatenate([-kit, krt], 1)], 0
    ).astype(jnp.bfloat16)
    return whole, turned


def frame_kernel(
    shifts,
    pos_hbm,
    index_hbm,
    count_hbm,
    phase_hbm,
    table_hbm,
    obj_hbm,
    probe_hbm,
    cot_hbm,
    row_hbm,
    col_hbm,
    *rest,
):
    far, steps = len(shifts) - 2, len(shifts)
    mine, other, scratch = rest[: 2 * steps], rest[2 * steps : 2 * steps + 2], rest[2 * steps + 2 :]
    pos_ref, index_ref, count_ref = scratch[0:3]
    phase_ref, table_ref, obj_ref, probe_ref, cot_ref, row_ref, col_ref = scratch[3:10]
    sems, band, window, col_bf, row_scr = scratch[10:]
    slices = obj_ref.shape[2]
    copies = [
        pltpu.make_async_copy(src, dst, sems.at[i])
        for i, (src, dst) in enumerate(
            [
                (phase_hbm, phase_ref),
                (table_hbm, table_ref),
                (pos_hbm, pos_ref),
                (probe_hbm, probe_ref),
                (index_hbm, index_ref),
                (count_hbm, count_ref),
                (row_hbm, row_ref),
            ]
        )
    ]
    got_phase, got_table, got_pos, got_probe, got_index, got_count, got_row = copies
    got_obj = [
        pltpu.make_async_copy(obj_hbm.at[0, :, s], obj_ref.at[0, :, s], sems.at[len(copies) + s])
        for s in range(slices)
    ]
    got_cot = pltpu.make_async_copy(cot_hbm, cot_ref, sems.at[len(copies) + slices])
    got_col = pltpu.make_async_copy(col_hbm, col_ref, sems.at[len(copies) + slices + 1])
    order = [s for i in range((slices + 1) // 2) for s in sorted({i, slices - 1 - i})]
    for copy in (got_pos, got_phase, got_table, *[got_obj[s] for s in order], got_probe, got_cot):
        copy.start()
    for copy in (got_index, got_count, got_row, got_col):
        copy.start()

    me, core = lax.axis_index("slab"), lax.axis_index("rep")
    peers = lax.axis_size("slab")
    capacity = index_ref.shape[-1]
    size = probe_ref.shape[-1]
    rows, cols = obj_ref.shape[3:]
    count = cot_ref.shape[1]
    group = 2 if count % 2 == 0 else 1
    f32, bf16 = jnp.float32, jnp.bfloat16

    got_pos.wait()
    got_phase.wait()
    got_table.wait()
    col_down = lax.broadcasted_iota(jnp.int32, (cols, size), 0)
    lane = lax.broadcasted_iota(jnp.int32, (cols, size), 1)
    cut = jnp.concatenate(
        [(col_down == lane + pos_ref[0, w]).astype(bf16) for w in range(count)], 1
    )
    whole, turned = propagator_blocks(phase_ref[...], table_ref[...])

    for copy in got_obj:
        copy.wait()
    got_probe.wait()
    got_cot.wait()
    got_row.wait()
    got_col.wait()
    got_index.wait()
    got_count.wait()
    for s in order:
        source = jnp.concatenate([obj_ref[0, 0, s], obj_ref[0, 1, s]], 0)
        window[s] = dot(source, cut).astype(bf16)

    def tile(s, c, w):
        return window[s, c * rows : (c + 1) * rows, w * size : (w + 1) * size]

    def left(fields, matrix):
        parts = []
        for g in range(0, count, group):
            stack = jnp.concatenate(
                [jnp.concatenate([fields[w][c] for w in range(g, g + group)], 1) for c in (0, 1)], 0
            )
            parts.append(dot(matrix, stack).astype(bf16))
        return parts

    def right(parts, matrix):
        result = []
        for part in parts:
            stack = jnp.concatenate(
                [
                    jnp.concatenate(
                        [
                            part[c * size : (c + 1) * size, k * size : (k + 1) * size]
                            for c in (0, 1)
                        ],
                        1,
                    )
                    for k in range(group)
                ],
                0,
            )
            done = dot(stack, matrix).astype(bf16)
            for k in range(group):
                lines = done[k * size : (k + 1) * size]
                result.append((lines[:, :size], lines[:, size:]))
        return result

    def product(one, two, conjugate):
        a_re, a_im = one[0].astype(f32), one[1].astype(f32)
        b_re, b_im = two[0].astype(f32), two[1].astype(f32)
        if conjugate:
            a_im = -a_im
        return (
            (a_re * b_re - a_im * b_im).astype(bf16),
            (a_re * b_im + a_im * b_re).astype(bf16),
        )

    block_rows, block_cols = row_ref.shape[-1], col_ref.shape[-1]
    across = cols // block_cols
    psi, chi = {}, {}
    now = [(probe_ref[0], probe_ref[1])] * count
    back = [(cot_ref[0, w, 0], cot_ref[0, w, 1]) for w in range(count)]
    lane_down = lax.broadcasted_iota(jnp.int32, (size, cols), 0)
    col = lax.broadcasted_iota(jnp.int32, (size, cols), 1)
    paste = jnp.concatenate(
        [(col == lane_down + pos_ref[0, w]).astype(bf16) for w in range(count)], 0
    )
    for i in range(slices):
        s, e = i, slices - 1 - i
        psi[s], chi[e] = now, back
        if i + 1 < slices:
            here = [(tile(s, 0, w), tile(s, 1, w)) for w in range(count)]
            there = [(tile(e, 0, w), tile(e, 1, w)) for w in range(count)]
            passed = [product(here[w], now[w], False) for w in range(count)]
            rho = [product(there[w], back[w], True) for w in range(count)]
            now, back = left(passed, whole), left(rho, turned)
            now, back = right(now, turned), right(back, whole)
        for t in sorted({s, e}):
            if t not in psi or t not in chi or max(t, slices - 1 - t) != i:
                continue
            grads = [product(psi[t][w], chi[t][w], True) for w in range(count)]
            stack = jnp.concatenate(
                [jnp.concatenate([grads[w][c] for w in range(count)], 1) for c in (0, 1)], 0
            )
            spread = dot(stack, paste).astype(bf16)
            for c in (0, 1):
                for k in range(rows // block_rows):
                    top = c * rows + k * block_rows
                    for j in range(across):
                        band[c, (t * (rows // block_rows) + k) * across + j] = spread[
                            top : top + block_rows, j * block_cols : (j + 1) * block_cols
                        ]

    tiles = row_ref.shape[0]
    batch = 8
    wide = batch * block_rows
    col_bf[...] = col_ref[...].astype(bf16)
    down = lax.broadcasted_iota(jnp.int32, (block_rows, wide), 0)
    along = lax.broadcasted_iota(jnp.int32, (block_rows, wide), 1)
    repeat = (lax.rem(along, block_rows) == down).astype(bf16)
    row_wide = dot(row_ref[...].reshape(tiles * block_rows, block_rows).astype(bf16), repeat)
    row_scr[...] = row_wide.reshape(tiles, block_rows, wide)
    strip = lax.div(along, block_rows)
    half = block_rows // CHUNKS
    mark_down = lax.broadcasted_iota(jnp.int32, (half, capacity * half), 0)
    mark_along = lax.broadcasted_iota(jnp.int32, (half, capacity * half), 1)
    mark_slot = jnp.where(lax.rem(mark_along, half) == mark_down, lax.div(mark_along, half), -1)
    lines = capacity * half
    late = (steps - far) * (lines + half)

    def put(k, h, slot, value):
        at = slot * half
        if h:
            swap, base = other[1], late + k * lines
        elif k < far:
            swap, base = other[0], k * (lines + half)
        else:
            swap, base = other[1], (k - far) * (lines + half)
        mine[h * steps + k][at : at + half] = value[:, :block_cols]
        swap[base + at : base + at + half] = value[:, block_cols:]

    for k, shift in enumerate(shifts):
        dest = partner(me, shift, peers)
        live = count_ref[0, 0, dest]
        marks = jnp.full(mark_slot.shape, VB_DEV, jnp.int32)
        for first in range(0, capacity, batch):
            inner, picks = [], []
            for slot in range(first, first + batch, 2):
                pairs, factors = [], []
                for one in (slot, slot + 1):
                    block = index_ref[0, 0, 0, dest, one]
                    target = index_ref[1, 0, 0, dest, one]
                    t = index_ref[2, 0, 0, dest, one]
                    target = jnp.where(one < live, target, VB_DEV)
                    marks = jnp.where(mark_slot == one, target, marks)
                    pairs += [band[core, block], band[1 - core, block]]
                    factors.append(col_bf[t])
                    picked = jnp.where(strip == one - first, row_scr[t], 0.0)
                    picks.append(picked.astype(bf16))
                mixed = dot(jnp.concatenate(pairs, 0), jnp.concatenate(factors, 1)).astype(bf16)
                for n in (0, 1):
                    lanes = slice(n * block_cols, (n + 1) * block_cols)
                    top = 2 * n * block_rows
                    inner.append(
                        jnp.concatenate(
                            [
                                mixed[top : top + block_rows, lanes],
                                mixed[top + block_rows : top + 2 * block_rows, lanes],
                            ],
                            1,
                        )
                    )
            result = dot(jnp.concatenate(picks, 0), jnp.concatenate(inner, 0))
            for slot in range(first, first + batch):
                for h in range(CHUNKS):
                    top = (slot - first) * block_rows + h * half
                    put(k, h, slot, result[top : top + half])
        marks = marks.astype(f32)
        put(k, 0, capacity, jnp.concatenate([marks, jnp.zeros_like(marks)], 1))


def keep_until(value, after):
    anywhere = pl.BlockSpec(memory_space=pl.ANY)

    def kernel(value_ref, after_ref, out_ref):
        pass

    return pl.pallas_call(
        kernel,
        out_shape=jax.ShapeDtypeStruct(value.shape, value.dtype),
        in_specs=[anywhere] * 2,
        out_specs=anywhere,
        input_output_aliases={0: 0},
        compiler_params=LIMIT,
        name="keep",
    )(value, after)


def join_kernel(base, first_ref, got_ref, *refs):
    count = len(refs) // 2
    for part, out in zip(refs[:count], refs[count:]):
        tall = part.shape[0]
        out[...] = part[...] + got_ref[base : base + tall]
        base += tall


def place_kernel(sources, owners, first, *refs):
    tilt, core = lax.axis_index("tilt"), lax.axis_index("rep")
    tilts, cores = lax.axis_size("tilt"), lax.axis_size("rep")
    each = VB_DEV // (tilts * cores)
    blocks = refs[:sources]
    half, lanes = CHUNK_ROWS, blocks[0].shape[-1]
    size = each * half
    if first:
        outs, mark_ref = refs[sources:-1], refs[-1]
        for k, block in enumerate(blocks):
            mark_ref[k] = block[lanes:]
    else:
        mark_ref, outs = refs[sources], refs[sources + cores :]
    data = jnp.concatenate([block[:lanes].astype(jnp.bfloat16) for block in blocks], 0)
    volume = lax.broadcasted_iota(jnp.int32, (each, half, lanes), 0).astype(jnp.float32)
    for out, (dt, dr) in zip(outs, owners):
        owner = lax.rem(tilt + dt, tilts) * cores + lax.rem(core + dr, cores)
        base = (owner * each).astype(jnp.float32)
        hot = []
        for k in range(sources):
            mark = mark_ref[k] - base
            hit = jnp.where(volume == mark[None], 1.0, 0.0)
            hot.append(hit.reshape(size, lanes).astype(jnp.bfloat16))
        out[:size] = dot(jnp.concatenate(hot, 1), data)
        if out.shape[0] > size:
            out[size:] = jnp.zeros((out.shape[0] - size, out.shape[1]), jnp.float32)


def sum_kernel(owners, *refs):
    out_ref = refs[-1]
    core, cores = lax.axis_index("rep"), lax.axis_size("rep")
    each, cols = out_ref.shape[0], out_ref.shape[-1]
    size = each * CHUNK_ROWS
    for h in range(CHUNKS):
        parts = refs[h * len(owners) : (h + 1) * len(owners)]
        for dr in range(cores):
            values = [ref[:size] for ref, (_, r) in zip(parts, owners) if r == dr]
            total = functools.reduce(jnp.add, values).reshape(each, CHUNK_ROWS, cols)
            out_ref[:, lax.rem(core + dr, cores), pl.ds(h * CHUNK_ROWS, CHUNK_ROWS)] = total


def on_device(
    object_slab,
    probe_field,
    phases,
    cotangent,
    positions,
    pair_index,
    pair_counts,
    row_interp,
    col_interp,
):
    peers = lax.axis_size("slab")
    tilts, cores = lax.axis_size("tilt"), lax.axis_size("rep")
    shifts = slab_steps(peers)
    capacity = pair_index.shape[-1]
    block_rows, block_cols = row_interp.shape[-1], col_interp.shape[-1]
    _, _, slices, rows, cols = object_slab.shape
    windows, size = cotangent.shape[1], cotangent.shape[-1]
    f32, bf16 = jnp.float32, jnp.bfloat16
    hbm, vmem = pl.BlockSpec(memory_space=pltpu.HBM), pl.BlockSpec(memory_space=VMEM)
    sources = len(shifts)
    lanes = capacity * CHUNK_ROWS

    phase_line = phases.reshape(1, -1)
    table = jnp.asarray(angle_table(size))
    frames = (slices * (rows // block_rows) * (cols // block_cols), block_rows, block_cols)
    far = sources - 2
    tall = lanes + CHUNK_ROWS
    heights = [tall] * sources + [lanes] * sources
    swapped = [far * tall, (sources - far) * tall + sources * lanes]
    shapes = [jax.ShapeDtypeStruct((tall, block_cols), f32) for tall in heights + swapped]
    fetched = [
        (phase_line, VMEM),
        (table, VMEM),
        (object_slab, VMEM),
        (probe_field, VMEM),
        (cotangent, VMEM),
        (row_interp, VMEM),
        (col_interp, VMEM),
    ]
    scalars = [positions, pair_index, pair_counts]
    held = pl.pallas_call(
        functools.partial(frame_kernel, shifts),
        out_shape=shapes,
        in_specs=[hbm] * 10,
        out_specs=[vmem] * len(shapes),
        scratch_shapes=[SMEM(x.shape, x.dtype) for x in scalars]
        + [space(x.shape, x.dtype) for x, space in fetched]
        + [
            pltpu.SemaphoreType.DMA((9 + slices,)),
            VMEM((2,) + frames, bf16),
            VMEM((slices, 2 * rows, windows * size), bf16),
            VMEM(col_interp.shape, bf16),
            VMEM((row_interp.shape[0], block_rows, 8 * block_rows), f32),
        ],
        compiler_params=LIMIT,
        name="frame",
    )(*[pltpu.with_memory_space_constraint(x, pltpu.HBM) for x in scalars + [x for x, _ in fetched]])

    swap = [(r, (r + 1) % cores) for r in range(cores)]
    owners = sorted(
        ((dt, dr) for dt in range(tilts) for dr in range(cores)), key=lambda o: (o[0] == 0, o)
    )
    each = VB_DEV // len(owners)
    share = jax.ShapeDtypeStruct((each * CHUNK_ROWS, block_cols), f32)
    mark = jax.ShapeDtypeStruct((sources, CHUNK_ROWS, block_cols), f32)
    padded = jax.ShapeDtypeStruct(((each + 1) * CHUNK_ROWS, block_cols), f32)
    mine, other = held[: len(heights)], held[len(heights) :]
    got = [lax.ppermute(other[0], "rep", swap)]
    got.append(lax.ppermute(keep_until(other[1], got[0]), "rep", swap))

    def send(block, step):
        ring = [(p, partner(p, step, peers)) for p in range(peers)]
        return lax.ppermute(block, "slab", ring)

    first = []
    for k in range(sources):
        h, at = (0, k * tall) if k < far else (1, (k - far) * tall)
        block = mine[k] + got[h][at : at + tall]
        first.append(send(block, shifts[k]) if shifts[k] else block)
    def join(after, part):
        late = mine[sources:][part]
        return pl.pallas_call(
            functools.partial(join_kernel, (sources - far) * tall + part.start * lanes),
            out_shape=shapes[sources : 2 * sources][part],
            in_specs=[vmem] * (len(late) + 2),
            out_specs=[vmem] * len(late),
            compiler_params=LIMIT,
            name="join",
        )(after, got[1], *late)

    def place(blocks, extra, h):
        shapes = [padded if dt else share for dt, dr in owners] + [mark]
        if h:
            shapes = [share] * len(owners)
        return pl.pallas_call(
            functools.partial(place_kernel, sources, owners, h == 0),
            out_shape=shapes,
            in_specs=[vmem] * (sources + len(extra)),
            out_specs=[vmem] * len(shapes),
            compiler_params=LIMIT,
            name="place",
        )(*blocks, *extra)

    def share_out(part, owner):
        dt, dr = owner
        if not (dt or dr):
            return part
        route = [
            (t * cores + r, (t + dt) % tilts * cores + (r + dr) % cores)
            for t in range(tilts)
            for r in range(cores)
        ]
        return lax.ppermute(part, ("tilt", "rep"), route)

    joined = [block for k in range(far) for block in join(first[k], slice(k, k + 1))]
    *parts, marks = place(first, [], 0)
    joined += join(marks, slice(far, sources))
    second = [send(block, k) if k else block for block, k in zip(joined, shifts)]
    extra = [share_out(part, owner) for part, owner in zip(parts, owners)]
    held = [part for part, (dt, dr) in zip(extra, owners) if dr and not dt]
    late = place(second, [marks, *held], 1)
    extra += [share_out(part, owner) for part, owner in zip(late, owners)]
    return pl.pallas_call(
        functools.partial(sum_kernel, owners),
        out_shape=jax.ShapeDtypeStruct((each, cores, block_rows, block_cols), f32),
        in_specs=[vmem] * len(extra),
        out_specs=vmem,
        compiler_params=LIMIT,
        name="total",
    )(*extra)


def solution(mesh):
    in_specs = (
        P(("groups", "tilt"), None, None, "slab", None),
        P(),
        P(),
        P(("groups", "tilt"), ("slab", "rep"), None, None, None),
        P(("groups", "tilt"), ("slab", "rep")),
        P(None, ("groups", "tilt"), "slab", None, None),
        P(("groups", "tilt"), "slab", None),
        P(),
        P(),
    )
    out_specs = P(("groups", "slab", "tilt", "rep"), None, None, None)
    return jax.shard_map(
        on_device, mesh=mesh, in_specs=in_specs, out_specs=out_specs, check_vma=False
    )
```

```python
import functools
import math

import jax
import jax.numpy as jnp
import numpy as np
from jax import lax
from jax.experimental import pallas as pl
from jax.experimental.pallas import tpu as pltpu
from jax.sharding import PartitionSpec as P

VB_DEV = 64
REACH = 3
CHUNKS = 2
CHUNK_ROWS = 8
HIGH = lax.Precision.HIGHEST
SMEM = pltpu.SMEM
VMEM = pltpu.VMEM
LIMIT = pltpu.CompilerParams(vmem_limit_bytes=40 * 1024 * 1024)


def dot(left, right, precision=None):
    return jnp.dot(left, right, precision=precision, preferred_element_type=jnp.float32)


def slab_steps(peers):
    if peers <= REACH + 1:
        return tuple(sorted(range(peers), key=lambda k: (k == 0, -k)))
    ring = [s for k in range(REACH, 0, -1) for s in (peers - k, k)]
    return (*ring, 0)


def partner(slab, step, peers):
    if peers <= REACH + 1 and peers & (peers - 1) == 0:
        return slab ^ step
    return (slab + step) % peers


def angle_table(length):
    grid = np.arange(length)
    angles = (grid[:, None] * grid[None, :] % length) * (2.0 * math.pi / length)
    return np.concatenate([np.cos(angles), np.sin(angles)], axis=1).astype(np.float32)


def propagator_blocks(phases, table):
    length = phases.shape[-1]
    row = lax.broadcasted_iota(jnp.int32, (8, length), 0)
    waves = jnp.where(row == 0, jnp.cos(phases), jnp.sin(phases))
    sums = dot(waves, table, HIGH) * (1.0 / length)
    cc, cs = sums[0:1, :length], sums[0:1, length:]
    sc, ss = sums[1:2, :length], sums[1:2, length:]

    def circulant(line):
        wide = jnp.broadcast_to(line, (length, length))
        return pltpu.roll(wide, 0, 1, stride=1, stride_axis=0)

    kr, ki = circulant(cc + ss), circulant(sc - cs)
    krt, kit = circulant(cc - ss), circulant(sc + cs)
    whole = jnp.concatenate(
        [jnp.concatenate([kr, -ki], 1), jnp.concatenate([ki, kr], 1)], 0
    ).astype(jnp.bfloat16)
    turned = jnp.concatenate(
        [jnp.concatenate([krt, kit], 1), jnp.concatenate([-kit, krt], 1)], 0
    ).astype(jnp.bfloat16)
    return whole, turned


def frame_kernel(
    shifts,
    pos_hbm,
    index_hbm,
    count_hbm,
    phase_hbm,
    table_hbm,
    obj_hbm,
    probe_hbm,
    cot_hbm,
    row_hbm,
    col_hbm,
    *rest,
):
    far, steps = len(shifts) - 2, len(shifts)
    mine, other, scratch = rest[: 2 * steps], rest[2 * steps : 2 * steps + 2], rest[2 * steps + 2 :]
    pos_ref, index_ref, count_ref = scratch[0:3]
    phase_ref, table_ref, obj_ref, probe_ref, cot_ref, row_ref, col_ref = scratch[3:10]
    sems, band, window, col_bf, row_scr = scratch[10:]
    slices = obj_ref.shape[2]
    copies = [
        pltpu.make_async_copy(src, dst, sems.at[i])
        for i, (src, dst) in enumerate(
            [
                (phase_hbm, phase_ref),
                (table_hbm, table_ref),
                (pos_hbm, pos_ref),
                (probe_hbm, probe_ref),
                (index_hbm, index_ref),
                (count_hbm, count_ref),
                (row_hbm, row_ref),
            ]
        )
    ]
    got_phase, got_table, got_pos, got_probe, got_index, got_count, got_row = copies
    got_obj = [
        pltpu.make_async_copy(obj_hbm.at[0, :, s], obj_ref.at[0, :, s], sems.at[len(copies) + s])
        for s in range(slices)
    ]
    got_cot = pltpu.make_async_copy(cot_hbm, cot_ref, sems.at[len(copies) + slices])
    got_col = pltpu.make_async_copy(col_hbm, col_ref, sems.at[len(copies) + slices + 1])
    order = [s for i in range((slices + 1) // 2) for s in sorted({i, slices - 1 - i})]
    for copy in (got_pos, got_phase, got_table, *[got_obj[s] for s in order], got_probe, got_cot):
        copy.start()
    for copy in (got_index, got_count, got_row, got_col):
        copy.start()

    me, core = lax.axis_index("slab"), lax.axis_index("rep")
    peers = lax.axis_size("slab")
    capacity = index_ref.shape[-1]
    size = probe_ref.shape[-1]
    rows, cols = obj_ref.shape[3:]
    count = cot_ref.shape[1]
    group = 2 if count % 2 == 0 else 1
    f32, bf16 = jnp.float32, jnp.bfloat16

    got_pos.wait()
    got_phase.wait()
    got_table.wait()
    col_down = lax.broadcasted_iota(jnp.int32, (cols, size), 0)
    lane = lax.broadcasted_iota(jnp.int32, (cols, size), 1)
    cut = jnp.concatenate(
        [(col_down == lane + pos_ref[0, w]).astype(bf16) for w in range(count)], 1
    )
    whole, turned = propagator_blocks(phase_ref[...], table_ref[...])

    for copy in got_obj:
        copy.wait()
    got_probe.wait()
    got_cot.wait()
    got_row.wait()
    got_col.wait()
    got_index.wait()
    got_count.wait()
    for s in order:
        source = jnp.concatenate([obj_ref[0, 0, s], obj_ref[0, 1, s]], 0)
        window[s] = dot(source, cut).astype(bf16)

    def tile(s, c, w):
        return window[s, c * rows : (c + 1) * rows, w * size : (w + 1) * size]

    def left(fields, matrix):
        parts = []
        for g in range(0, count, group):
            stack = jnp.concatenate(
                [jnp.concatenate([fields[w][c] for w in range(g, g + group)], 1) for c in (0, 1)], 0
            )
            parts.append(dot(matrix, stack).astype(bf16))
        return parts

    def right(parts, matrix):
        result = []
        for part in parts:
            stack = jnp.concatenate(
                [
                    jnp.concatenate(
                        [
                            part[c * size : (c + 1) * size, k * size : (k + 1) * size]
                            for c in (0, 1)
                        ],
                        1,
                    )
                    for k in range(group)
                ],
                0,
            )
            done = dot(stack, matrix).astype(bf16)
            for k in range(group):
                lines = done[k * size : (k + 1) * size]
                result.append((lines[:, :size], lines[:, size:]))
        return result

    def product(one, two, conjugate):
        a_re, a_im = one[0].astype(f32), one[1].astype(f32)
        b_re, b_im = two[0].astype(f32), two[1].astype(f32)
        if conjugate:
            a_im = -a_im
        return (
            (a_re * b_re - a_im * b_im).astype(bf16),
            (a_re * b_im + a_im * b_re).astype(bf16),
        )

    block_rows, block_cols = row_ref.shape[-1], col_ref.shape[-1]
    across = cols // block_cols
    psi, chi = {}, {}
    now = [(probe_ref[0], probe_ref[1])] * count
    back = [(cot_ref[0, w, 0], cot_ref[0, w, 1]) for w in range(count)]
    lane_down = lax.broadcasted_iota(jnp.int32, (size, cols), 0)
    col = lax.broadcasted_iota(jnp.int32, (size, cols), 1)
    paste = jnp.concatenate(
        [(col == lane_down + pos_ref[0, w]).astype(bf16) for w in range(count)], 0
    )
    for i in range(slices):
        s, e = i, slices - 1 - i
        psi[s], chi[e] = now, back
        if i + 1 < slices:
            here = [(tile(s, 0, w), tile(s, 1, w)) for w in range(count)]
            there = [(tile(e, 0, w), tile(e, 1, w)) for w in range(count)]
            passed = [product(here[w], now[w], False) for w in range(count)]
            rho = [product(there[w], back[w], True) for w in range(count)]
            now, back = left(passed, whole), left(rho, turned)
            now, back = right(now, turned), right(back, whole)
        for t in sorted({s, e}):
            if t not in psi or t not in chi or max(t, slices - 1 - t) != i:
                continue
            grads = [product(psi[t][w], chi[t][w], True) for w in range(count)]
            stack = jnp.concatenate(
                [jnp.concatenate([grads[w][c] for w in range(count)], 1) for c in (0, 1)], 0
            )
            spread = dot(stack, paste).astype(bf16)
            for c in (0, 1):
                for k in range(rows // block_rows):
                    top = c * rows + k * block_rows
                    for j in range(across):
                        band[c, (t * (rows // block_rows) + k) * across + j] = spread[
                            top : top + block_rows, j * block_cols : (j + 1) * block_cols
                        ]

    tiles = row_ref.shape[0]
    batch = 8
    wide = batch * block_rows
    col_bf[...] = col_ref[...].astype(bf16)
    down = lax.broadcasted_iota(jnp.int32, (block_rows, wide), 0)
    along = lax.broadcasted_iota(jnp.int32, (block_rows, wide), 1)
    repeat = (lax.rem(along, block_rows) == down).astype(bf16)
    row_wide = dot(row_ref[...].reshape(tiles * block_rows, block_rows).astype(bf16), repeat)
    row_scr[...] = row_wide.reshape(tiles, block_rows, wide)
    strip = lax.div(along, block_rows)
    half = block_rows // CHUNKS
    mark_down = lax.broadcasted_iota(jnp.int32, (half, capacity * half), 0)
    mark_along = lax.broadcasted_iota(jnp.int32, (half, capacity * half), 1)
    mark_slot = jnp.where(lax.rem(mark_along, half) == mark_down, lax.div(mark_along, half), -1)
    lines = capacity * half
    late = (steps - far) * (lines + half)

    def put(k, h, slot, value):
        at = slot * half
        if h:
            swap, base = other[1], late + k * lines
        elif k < far:
            swap, base = other[0], k * (lines + half)
        else:
            swap, base = other[1], (k - far) * (lines + half)
        mine[h * steps + k][at : at + half] = value[:, :block_cols]
        swap[base + at : base + at + half] = value[:, block_cols:]

    for k, shift in enumerate(shifts):
        dest = partner(me, shift, peers)
        live = count_ref[0, 0, dest]
        marks = jnp.full(mark_slot.shape, VB_DEV, jnp.int32)
        for first in range(0, capacity, batch):
            inner, picks = [], []
            for slot in range(first, first + batch, 2):
                pairs, factors = [], []
                for one in (slot, slot + 1):
                    block = index_ref[0, 0, 0, dest, one]
                    target = index_ref[1, 0, 0, dest, one]
                    t = index_ref[2, 0, 0, dest, one]
                    target = jnp.where(one < live, target, VB_DEV)
                    marks = jnp.where(mark_slot == one, target, marks)
                    pairs += [band[core, block], band[1 - core, block]]
                    factors.append(col_bf[t])
                    picked = jnp.where(strip == one - first, row_scr[t], 0.0)
                    picks.append(picked.astype(bf16))
                mixed = dot(jnp.concatenate(pairs, 0), jnp.concatenate(factors, 1)).astype(bf16)
                for n in (0, 1):
                    lanes = slice(n * block_cols, (n + 1) * block_cols)
                    top = 2 * n * block_rows
                    inner.append(
                        jnp.concatenate(
                            [
                                mixed[top : top + block_rows, lanes],
                                mixed[top + block_rows : top + 2 * block_rows, lanes],
                            ],
                            1,
                        )
                    )
            result = dot(jnp.concatenate(picks, 0), jnp.concatenate(inner, 0))
            for slot in range(first, first + batch):
                for h in range(CHUNKS):
                    top = (slot - first) * block_rows + h * half
                    put(k, h, slot, result[top : top + half])
        marks = marks.astype(f32)
        put(k, 0, capacity, jnp.concatenate([marks, jnp.zeros_like(marks)], 1))


def keep_until(value, after):
    anywhere = pl.BlockSpec(memory_space=pl.ANY)

    def kernel(value_ref, after_ref, out_ref):
        pass

    return pl.pallas_call(
        kernel,
        out_shape=jax.ShapeDtypeStruct(value.shape, value.dtype),
        in_specs=[anywhere] * 2,
        out_specs=anywhere,
        input_output_aliases={0: 0},
        compiler_params=LIMIT,
        name="keep",
    )(value, after)


def join_kernel(base, first_ref, got_ref, *refs):
    count = len(refs) // 2
    for part, out in zip(refs[:count], refs[count:]):
        tall = part.shape[0]
        out[...] = part[...] + got_ref[base : base + tall]
        base += tall


def place_kernel(sources, owners, first, *refs):
    tilt, core = lax.axis_index("tilt"), lax.axis_index("rep")
    tilts, cores = lax.axis_size("tilt"), lax.axis_size("rep")
    each = VB_DEV // (tilts * cores)
    blocks = refs[:sources]
    half, lanes = CHUNK_ROWS, blocks[0].shape[-1]
    size = each * half
    if first:
        outs, mark_ref = refs[sources:-1], refs[-1]
        for k, block in enumerate(blocks):
            mark_ref[k] = block[lanes:]
    else:
        mark_ref, outs = refs[sources], refs[sources + cores :]
    data = jnp.concatenate([block[:lanes].astype(jnp.bfloat16) for block in blocks], 0)
    volume = lax.broadcasted_iota(jnp.int32, (each, half, lanes), 0).astype(jnp.float32)
    for out, (dt, dr) in zip(outs, owners):
        owner = lax.rem(tilt + dt, tilts) * cores + lax.rem(core + dr, cores)
        base = (owner * each).astype(jnp.float32)
        hot = []
        for k in range(sources):
            mark = mark_ref[k] - base
            hit = jnp.where(volume == mark[None], 1.0, 0.0)
            hot.append(hit.reshape(size, lanes).astype(jnp.bfloat16))
        out[:size] = dot(jnp.concatenate(hot, 1), data)
        if out.shape[0] > size:
            out[size:] = jnp.zeros((out.shape[0] - size, out.shape[1]), jnp.float32)


def sum_kernel(owners, *refs):
    out_ref = refs[-1]
    core, cores = lax.axis_index("rep"), lax.axis_size("rep")
    each, cols = out_ref.shape[0], out_ref.shape[-1]
    size = each * CHUNK_ROWS
    for h in range(CHUNKS):
        parts = refs[h * len(owners) : (h + 1) * len(owners)]
        for dr in range(cores):
            values = [ref[:size] for ref, (_, r) in zip(parts, owners) if r == dr]
            total = functools.reduce(jnp.add, values).reshape(each, CHUNK_ROWS, cols)
            out_ref[:, lax.rem(core + dr, cores), pl.ds(h * CHUNK_ROWS, CHUNK_ROWS)] = total


def on_device(
    object_slab,
    probe_field,
    phases,
    cotangent,
    positions,
    pair_index,
    pair_counts,
    row_interp,
    col_interp,
):
    peers = lax.axis_size("slab")
    tilts, cores = lax.axis_size("tilt"), lax.axis_size("rep")
    shifts = slab_steps(peers)
    capacity = pair_index.shape[-1]
    block_rows, block_cols = row_interp.shape[-1], col_interp.shape[-1]
    _, _, slices, rows, cols = object_slab.shape
    windows, size = cotangent.shape[1], cotangent.shape[-1]
    f32, bf16 = jnp.float32, jnp.bfloat16
    hbm, vmem = pl.BlockSpec(memory_space=pltpu.HBM), pl.BlockSpec(memory_space=VMEM)
    sources = len(shifts)
    lanes = capacity * CHUNK_ROWS

    phase_line = phases.reshape(1, -1)
    table = jnp.asarray(angle_table(size))
    frames = (slices * (rows // block_rows) * (cols // block_cols), block_rows, block_cols)
    far = sources - 2
    tall = lanes + CHUNK_ROWS
    heights = [tall] * sources + [lanes] * sources
    swapped = [far * tall, (sources - far) * tall + sources * lanes]
    shapes = [jax.ShapeDtypeStruct((tall, block_cols), f32) for tall in heights + swapped]
    fetched = [
        (phase_line, VMEM),
        (table, VMEM),
        (object_slab, VMEM),
        (probe_field, VMEM),
        (cotangent, VMEM),
        (row_interp, VMEM),
        (col_interp, VMEM),
    ]
    scalars = [positions, pair_index, pair_counts]
    held = pl.pallas_call(
        functools.partial(frame_kernel, shifts),
        out_shape=shapes,
        in_specs=[hbm] * 10,
        out_specs=[vmem] * len(shapes),
        scratch_shapes=[SMEM(x.shape, x.dtype) for x in scalars]
        + [space(x.shape, x.dtype) for x, space in fetched]
        + [
            pltpu.SemaphoreType.DMA((9 + slices,)),
            VMEM((2,) + frames, bf16),
            VMEM((slices, 2 * rows, windows * size), bf16),
            VMEM(col_interp.shape, bf16),
            VMEM((row_interp.shape[0], block_rows, 8 * block_rows), f32),
        ],
        compiler_params=LIMIT,
        name="frame",
    )(*[pltpu.with_memory_space_constraint(x, pltpu.HBM) for x in scalars + [x for x, _ in fetched]])

    swap = [(r, (r + 1) % cores) for r in range(cores)]
    owners = sorted(
        ((dt, dr) for dt in range(tilts) for dr in range(cores)), key=lambda o: (o[0] == 0, o)
    )
    each = VB_DEV // len(owners)
    share = jax.ShapeDtypeStruct((each * CHUNK_ROWS, block_cols), f32)
    mark = jax.ShapeDtypeStruct((sources, CHUNK_ROWS, block_cols), f32)
    padded = jax.ShapeDtypeStruct(((each + 1) * CHUNK_ROWS, block_cols), f32)
    mine, other = held[: len(heights)], held[len(heights) :]
    got = [lax.ppermute(other[0], "rep", swap)]
    got.append(lax.ppermute(keep_until(other[1], got[0]), "rep", swap))

    def send(block, step):
        ring = [(p, partner(p, step, peers)) for p in range(peers)]
        return lax.ppermute(block, "slab", ring)

    first = []
    for k in range(sources):
        h, at = (0, k * tall) if k < far else (1, (k - far) * tall)
        block = mine[k] + got[h][at : at + tall]
        first.append(send(block, shifts[k]) if shifts[k] else block)
    def join(after, part):
        late = mine[sources:][part]
        return pl.pallas_call(
            functools.partial(join_kernel, (sources - far) * tall + part.start * lanes),
            out_shape=shapes[sources : 2 * sources][part],
            in_specs=[vmem] * (len(late) + 2),
            out_specs=[vmem] * len(late),
            compiler_params=LIMIT,
            name="join",
        )(after, got[1], *late)

    def place(blocks, extra, h):
        shapes = [padded if dt else share for dt, dr in owners] + [mark]
        if h:
            shapes = [share] * len(owners)
        return pl.pallas_call(
            functools.partial(place_kernel, sources, owners, h == 0),
            out_shape=shapes,
            in_specs=[vmem] * (sources + len(extra)),
            out_specs=[vmem] * len(shapes),
            compiler_params=LIMIT,
            name="place",
        )(*blocks, *extra)

    def share_out(part, owner):
        dt, dr = owner
        if not (dt or dr):
            return part
        route = [
            (t * cores + r, (t + dt) % tilts * cores + (r + dr) % cores)
            for t in range(tilts)
            for r in range(cores)
        ]
        return lax.ppermute(part, ("tilt", "rep"), route)

    joined = []
    for k in range(far):
        joined += join(first[k], slice(k, k + 1 if k + 1 < far else sources))
    second = [send(block, k) if k else block for block, k in zip(joined, shifts)]
    *parts, marks = place(first, [], 0)
    extra = [share_out(part, owner) for part, owner in zip(parts, owners)]
    held = [part for part, (dt, dr) in zip(extra, owners) if dr and not dt]
    late = place(second, [marks, *held], 1)
    extra += [share_out(part, owner) for part, owner in zip(late, owners)]
    return pl.pallas_call(
        functools.partial(sum_kernel, owners),
        out_shape=jax.ShapeDtypeStruct((each, cores, block_rows, block_cols), f32),
        in_specs=[vmem] * len(extra),
        out_specs=vmem,
        compiler_params=LIMIT,
        name="total",
    )(*extra)


def solution(mesh):
    in_specs = (
        P(("groups", "tilt"), None, None, "slab", None),
        P(),
        P(),
        P(("groups", "tilt"), ("slab", "rep"), None, None, None),
        P(("groups", "tilt"), ("slab", "rep")),
        P(None, ("groups", "tilt"), "slab", None, None),
        P(("groups", "tilt"), "slab", None),
        P(),
        P(),
    )
    out_specs = P(("groups", "slab", "tilt", "rep"), None, None, None)
    return jax.shard_map(
        on_device, mesh=mesh, in_specs=in_specs, out_specs=out_specs, check_vma=False
    )
```

```python
import functools
import math

import jax
import jax.numpy as jnp
import numpy as np
from jax import lax
from jax.experimental import pallas as pl
from jax.experimental.pallas import tpu as pltpu
from jax.sharding import PartitionSpec as P

VB_DEV = 64
REACH = 3
CHUNKS = 2
CHUNK_ROWS = 8
BATCH = 8
HIGH = lax.Precision.HIGHEST
SMEM = pltpu.SMEM
VMEM = pltpu.VMEM
LIMIT = pltpu.CompilerParams(vmem_limit_bytes=40 * 1024 * 1024)


def dot(left, right, precision=None):
    return jnp.dot(left, right, precision=precision, preferred_element_type=jnp.float32)


def slab_steps(peers):
    if peers <= REACH + 1:
        return tuple(sorted(range(peers), key=lambda k: (k == 0, k < peers // 2, k)))
    ring = [s for k in range(REACH, 0, -1) for s in (peers - k, k)]
    return (*ring, 0)


def partner(slab, step, peers):
    if peers <= REACH + 1 and peers & (peers - 1) == 0:
        return slab ^ step
    return (slab + step) % peers


def angle_table(length):
    grid = np.arange(length)
    angles = (grid[:, None] * grid[None, :] % length) * (2.0 * math.pi / length)
    return np.concatenate([np.cos(angles), np.sin(angles)], axis=1).astype(np.float32)


def propagator_blocks(phases, table):
    length = phases.shape[-1]
    row = lax.broadcasted_iota(jnp.int32, (8, length), 0)
    waves = jnp.where(row == 0, jnp.cos(phases), jnp.sin(phases))
    sums = dot(waves, table, HIGH) * (1.0 / length)
    cc, cs = sums[0:1, :length], sums[0:1, length:]
    sc, ss = sums[1:2, :length], sums[1:2, length:]

    def circulant(line):
        wide = jnp.broadcast_to(line, (length, length))
        return pltpu.roll(wide, 0, 1, stride=1, stride_axis=0)

    kr, ki = circulant(cc + ss), circulant(sc - cs)
    krt, kit = circulant(cc - ss), circulant(sc + cs)
    whole = jnp.concatenate(
        [jnp.concatenate([kr, -ki], 1), jnp.concatenate([ki, kr], 1)], 0
    ).astype(jnp.bfloat16)
    turned = jnp.concatenate(
        [jnp.concatenate([krt, kit], 1), jnp.concatenate([-kit, krt], 1)], 0
    ).astype(jnp.bfloat16)
    return whole, turned


def mix_blocks(shifts, which, index_ref, count_ref, band, col_bf, row_scr, put):
    me, core = lax.axis_index("slab"), lax.axis_index("rep")
    peers = lax.axis_size("slab")
    f32, bf16 = jnp.float32, jnp.bfloat16
    capacity = index_ref.shape[-1]
    block_rows, block_cols = band.shape[-2:]
    wide = BATCH * block_rows
    strip = lax.div(lax.broadcasted_iota(jnp.int32, (block_rows, wide), 1), block_rows)
    half = block_rows // CHUNKS
    mark_down = lax.broadcasted_iota(jnp.int32, (half, capacity * half), 0)
    mark_along = lax.broadcasted_iota(jnp.int32, (half, capacity * half), 1)
    mark_slot = jnp.where(lax.rem(mark_along, half) == mark_down, lax.div(mark_along, half), -1)
    for k in which:
        dest = partner(me, shifts[k], peers)
        live = count_ref[0, 0, dest]
        marks = jnp.full(mark_slot.shape, VB_DEV, jnp.int32)
        for first in range(0, capacity, BATCH):
            inner, picks = [], []
            for slot in range(first, first + BATCH, 2):
                pairs, factors = [], []
                for one in (slot, slot + 1):
                    block = index_ref[0, 0, 0, dest, one]
                    target = index_ref[1, 0, 0, dest, one]
                    t = index_ref[2, 0, 0, dest, one]
                    target = jnp.where(one < live, target, VB_DEV)
                    marks = jnp.where(mark_slot == one, target, marks)
                    pairs += [band[core, block], band[1 - core, block]]
                    factors.append(col_bf[t])
                    picked = jnp.where(strip == one - first, row_scr[t], 0.0)
                    picks.append(picked.astype(bf16))
                mixed = dot(jnp.concatenate(pairs, 0), jnp.concatenate(factors, 1)).astype(bf16)
                for n in (0, 1):
                    lanes = slice(n * block_cols, (n + 1) * block_cols)
                    top = 2 * n * block_rows
                    inner.append(
                        jnp.concatenate(
                            [
                                mixed[top : top + block_rows, lanes],
                                mixed[top + block_rows : top + 2 * block_rows, lanes],
                            ],
                            1,
                        )
                    )
            result = dot(jnp.concatenate(picks, 0), jnp.concatenate(inner, 0))
            for h in range(CHUNKS):
                for slot in range(first, first + BATCH):
                    top = (slot - first) * block_rows + h * half
                    put(k, h, slot * half, result[top : top + half])
        marks = marks.astype(f32)
        put(k, 0, capacity * half, jnp.concatenate([marks, jnp.zeros_like(marks)], 1))


def near_kernel(shifts, index_ref, count_ref, band, col_bf, row_scr, spare, *refs):
    mine, other = refs[:-1], refs[-1]
    far, near = len(shifts) - 2, 2
    half, cols = CHUNK_ROWS, band.shape[-1]
    lines = index_ref.shape[-1] * half
    late = near * (lines + half)
    other[late : late + far * lines] = spare[...]

    def put(k, h, row, value):
        base = late + k * lines if h else (k - far) * (lines + half)
        mine[h * near + k - far][row : row + half] = value[:, :cols]
        other[base + row : base + row + half] = value[:, cols:]

    mix_blocks(shifts, range(far, far + near), index_ref, count_ref, band, col_bf, row_scr, put)


def frame_kernel(
    shifts,
    pos_hbm,
    index_hbm,
    count_hbm,
    phase_hbm,
    table_hbm,
    obj_hbm,
    probe_hbm,
    cot_hbm,
    row_hbm,
    col_hbm,
    *rest,
):
    far = len(shifts) - 2
    mine, swaps = rest[: 2 * far], rest[2 * far : 2 * far + 2]
    band, col_bf, row_scr = rest[2 * far + 2 : 2 * far + 5]
    scratch = rest[2 * far + 5 :]
    pos_ref, index_ref, count_ref = scratch[0:3]
    phase_ref, table_ref, obj_ref, probe_ref, cot_ref, row_ref, col_ref = scratch[3:10]
    sems, window = scratch[10:]
    slices = obj_ref.shape[2]
    copies = [
        pltpu.make_async_copy(src, dst, sems.at[i])
        for i, (src, dst) in enumerate(
            [
                (phase_hbm, phase_ref),
                (table_hbm, table_ref),
                (pos_hbm, pos_ref),
                (probe_hbm, probe_ref),
                (index_hbm, index_ref),
                (count_hbm, count_ref),
                (row_hbm, row_ref),
            ]
        )
    ]
    got_phase, got_table, got_pos, got_probe, got_index, got_count, got_row = copies
    got_obj = [
        pltpu.make_async_copy(obj_hbm.at[0, :, s], obj_ref.at[0, :, s], sems.at[len(copies) + s])
        for s in range(slices)
    ]
    got_cot = pltpu.make_async_copy(cot_hbm, cot_ref, sems.at[len(copies) + slices])
    got_col = pltpu.make_async_copy(col_hbm, col_ref, sems.at[len(copies) + slices + 1])
    order = [s for i in range((slices + 1) // 2) for s in sorted({i, slices - 1 - i})]
    for copy in (got_pos, got_phase, got_table, *[got_obj[s] for s in order], got_probe, got_cot):
        copy.start()
    for copy in (got_index, got_count, got_row, got_col):
        copy.start()

    size = probe_ref.shape[-1]
    rows, cols = obj_ref.shape[3:]
    count = cot_ref.shape[1]
    group = 2 if count % 2 == 0 else 1
    f32, bf16 = jnp.float32, jnp.bfloat16

    got_pos.wait()
    got_phase.wait()
    got_table.wait()
    col_down = lax.broadcasted_iota(jnp.int32, (cols, size), 0)
    lane = lax.broadcasted_iota(jnp.int32, (cols, size), 1)
    cut = jnp.concatenate(
        [(col_down == lane + pos_ref[0, w]).astype(bf16) for w in range(count)], 1
    )
    whole, turned = propagator_blocks(phase_ref[...], table_ref[...])

    for copy in got_obj:
        copy.wait()
    got_probe.wait()
    got_cot.wait()
    got_row.wait()
    got_col.wait()
    got_index.wait()
    got_count.wait()
    for s in order:
        source = jnp.concatenate([obj_ref[0, 0, s], obj_ref[0, 1, s]], 0)
        window[s] = dot(source, cut).astype(bf16)

    def tile(s, c, w):
        return window[s, c * rows : (c + 1) * rows, w * size : (w + 1) * size]

    def left(fields, matrix):
        parts = []
        for g in range(0, count, group):
            stack = jnp.concatenate(
                [jnp.concatenate([fields[w][c] for w in range(g, g + group)], 1) for c in (0, 1)], 0
            )
            parts.append(dot(matrix, stack).astype(bf16))
        return parts

    def right(parts, matrix):
        result = []
        for part in parts:
            stack = jnp.concatenate(
                [
                    jnp.concatenate(
                        [
                            part[c * size : (c + 1) * size, k * size : (k + 1) * size]
                            for c in (0, 1)
                        ],
                        1,
                    )
                    for k in range(group)
                ],
                0,
            )
            done = dot(stack, matrix).astype(bf16)
            for k in range(group):
                lines = done[k * size : (k + 1) * size]
                result.append((lines[:, :size], lines[:, size:]))
        return result

    def product(one, two, conjugate):
        a_re, a_im = one[0].astype(f32), one[1].astype(f32)
        b_re, b_im = two[0].astype(f32), two[1].astype(f32)
        if conjugate:
            a_im = -a_im
        return (
            (a_re * b_re - a_im * b_im).astype(bf16),
            (a_re * b_im + a_im * b_re).astype(bf16),
        )

    block_rows, block_cols = row_ref.shape[-1], col_ref.shape[-1]
    across = cols // block_cols
    psi, chi = {}, {}
    now = [(probe_ref[0], probe_ref[1])] * count
    back = [(cot_ref[0, w, 0], cot_ref[0, w, 1]) for w in range(count)]
    lane_down = lax.broadcasted_iota(jnp.int32, (size, cols), 0)
    col = lax.broadcasted_iota(jnp.int32, (size, cols), 1)
    paste = jnp.concatenate(
        [(col == lane_down + pos_ref[0, w]).astype(bf16) for w in range(count)], 0
    )
    for i in range(slices):
        s, e = i, slices - 1 - i
        psi[s], chi[e] = now, back
        if i + 1 < slices:
            here = [(tile(s, 0, w), tile(s, 1, w)) for w in range(count)]
            there = [(tile(e, 0, w), tile(e, 1, w)) for w in range(count)]
            passed = [product(here[w], now[w], False) for w in range(count)]
            rho = [product(there[w], back[w], True) for w in range(count)]
            now, back = left(passed, whole), left(rho, turned)
            now, back = right(now, turned), right(back, whole)
        for t in sorted({s, e}):
            if t not in psi or t not in chi or max(t, slices - 1 - t) != i:
                continue
            grads = [product(psi[t][w], chi[t][w], True) for w in range(count)]
            stack = jnp.concatenate(
                [jnp.concatenate([grads[w][c] for w in range(count)], 1) for c in (0, 1)], 0
            )
            spread = dot(stack, paste).astype(bf16)
            for c in (0, 1):
                for k in range(rows // block_rows):
                    top = c * rows + k * block_rows
                    for j in range(across):
                        band[c, (t * (rows // block_rows) + k) * across + j] = spread[
                            top : top + block_rows, j * block_cols : (j + 1) * block_cols
                        ]

    tiles = row_ref.shape[0]
    wide = BATCH * block_rows
    col_bf[...] = col_ref[...].astype(bf16)
    down = lax.broadcasted_iota(jnp.int32, (block_rows, wide), 0)
    along = lax.broadcasted_iota(jnp.int32, (block_rows, wide), 1)
    repeat = (lax.rem(along, block_rows) == down).astype(bf16)
    row_wide = dot(row_ref[...].reshape(tiles * block_rows, block_rows).astype(bf16), repeat)
    row_scr[...] = row_wide.reshape(tiles, block_rows, wide)
    half = block_rows // CHUNKS

    def put(k, h, row, value):
        base = k * mine[h * far].shape[0] + row
        mine[h * far + k][row : row + half] = value[:, :block_cols]
        swaps[h][base : base + half] = value[:, block_cols:]

    mix_blocks(shifts, range(far), index_ref, count_ref, band, col_bf, row_scr, put)


def keep_until(value, after):
    anywhere = pl.BlockSpec(memory_space=pl.ANY)

    def kernel(value_ref, after_ref, out_ref):
        pass

    return pl.pallas_call(
        kernel,
        out_shape=jax.ShapeDtypeStruct(value.shape, value.dtype),
        in_specs=[anywhere] * 2,
        out_specs=anywhere,
        input_output_aliases={0: 0},
        compiler_params=LIMIT,
        name="keep",
    )(value, after)


def join_kernel(base, first_ref, got_ref, *refs):
    count = len(refs) // 2
    for part, out in zip(refs[:count], refs[count:]):
        tall = part.shape[0]
        out[...] = part[...] + got_ref[base : base + tall]
        base += tall


def place_kernel(sources, owners, first, *refs):
    tilt, core = lax.axis_index("tilt"), lax.axis_index("rep")
    tilts, cores = lax.axis_size("tilt"), lax.axis_size("rep")
    each = VB_DEV // (tilts * cores)
    blocks = refs[:sources]
    half, lanes = CHUNK_ROWS, blocks[0].shape[-1]
    size = each * half
    if first:
        outs, mark_ref = refs[sources:-1], refs[-1]
        for k, block in enumerate(blocks):
            mark_ref[k] = block[lanes:]
    else:
        mark_ref, outs = refs[sources], refs[sources + cores :]
    data = jnp.concatenate([block[:lanes].astype(jnp.bfloat16) for block in blocks], 0)
    volume = lax.broadcasted_iota(jnp.int32, (each, half, lanes), 0).astype(jnp.float32)
    for out, (dt, dr) in zip(outs, owners):
        owner = lax.rem(tilt + dt, tilts) * cores + lax.rem(core + dr, cores)
        base = (owner * each).astype(jnp.float32)
        hot = []
        for k in range(sources):
            mark = mark_ref[k] - base
            hit = jnp.where(volume == mark[None], 1.0, 0.0)
            hot.append(hit.reshape(size, lanes).astype(jnp.bfloat16))
        out[:size] = dot(jnp.concatenate(hot, 1), data)
        if out.shape[0] > size:
            out[size:] = jnp.zeros((out.shape[0] - size, out.shape[1]), jnp.float32)


def sum_kernel(owners, *refs):
    out_ref = refs[-1]
    core, cores = lax.axis_index("rep"), lax.axis_size("rep")
    each, cols = out_ref.shape[0], out_ref.shape[-1]
    size = each * CHUNK_ROWS
    for h in range(CHUNKS):
        parts = refs[h * len(owners) : (h + 1) * len(owners)]
        for dr in range(cores):
            values = [ref[:size] for ref, (_, r) in zip(parts, owners) if r == dr]
            total = functools.reduce(jnp.add, values).reshape(each, CHUNK_ROWS, cols)
            out_ref[:, lax.rem(core + dr, cores), pl.ds(h * CHUNK_ROWS, CHUNK_ROWS)] = total


def on_device(
    object_slab,
    probe_field,
    phases,
    cotangent,
    positions,
    pair_index,
    pair_counts,
    row_interp,
    col_interp,
):
    peers = lax.axis_size("slab")
    tilts, cores = lax.axis_size("tilt"), lax.axis_size("rep")
    shifts = slab_steps(peers)
    capacity = pair_index.shape[-1]
    block_rows, block_cols = row_interp.shape[-1], col_interp.shape[-1]
    _, _, slices, rows, cols = object_slab.shape
    windows, size = cotangent.shape[1], cotangent.shape[-1]
    f32, bf16 = jnp.float32, jnp.bfloat16
    hbm, vmem = pl.BlockSpec(memory_space=pltpu.HBM), pl.BlockSpec(memory_space=VMEM)
    sources = len(shifts)
    lanes = capacity * CHUNK_ROWS

    phase_line = phases.reshape(1, -1)
    table = jnp.asarray(angle_table(size))
    frames = (slices * (rows // block_rows) * (cols // block_cols), block_rows, block_cols)
    far = sources - 2
    tall = lanes + CHUNK_ROWS
    heights = [tall] * sources + [lanes] * sources
    swapped = [far * tall, (sources - far) * tall + sources * lanes]
    shapes = [jax.ShapeDtypeStruct((tall, block_cols), f32) for tall in heights + swapped]
    fetched = [
        (phase_line, VMEM),
        (table, VMEM),
        (object_slab, VMEM),
        (probe_field, VMEM),
        (cotangent, VMEM),
        (row_interp, VMEM),
        (col_interp, VMEM),
    ]
    scalars = [positions, pair_index, pair_counts]
    in_hbm = functools.partial(pltpu.with_memory_space_constraint, memory_space=pltpu.HBM)
    passed = [
        jax.ShapeDtypeStruct((2,) + frames, bf16),
        jax.ShapeDtypeStruct(col_interp.shape, bf16),
        jax.ShapeDtypeStruct((row_interp.shape[0], block_rows, BATCH * block_rows), f32),
    ]
    spare = jax.ShapeDtypeStruct((far * lanes, block_cols), f32)
    outs = shapes[:far] + shapes[sources : sources + far] + [shapes[-2], spare] + passed
    *held, other, spare, band, col_bf, row_wide = pl.pallas_call(
        functools.partial(frame_kernel, shifts),
        out_shape=outs,
        in_specs=[hbm] * 10,
        out_specs=[vmem] * len(outs),
        scratch_shapes=[SMEM(x.shape, x.dtype) for x in scalars]
        + [space(x.shape, x.dtype) for x, space in fetched]
        + [
            pltpu.SemaphoreType.DMA((9 + slices,)),
            VMEM((slices, 2 * rows, windows * size), bf16),
        ],
        compiler_params=LIMIT,
        name="frame",
    )(*[in_hbm(x) for x in scalars + [x for x, _ in fetched]])
    outs = shapes[far:sources] + shapes[sources + far : 2 * sources] + [shapes[-1]]
    *near, rest = pl.pallas_call(
        functools.partial(near_kernel, shifts),
        out_shape=outs,
        in_specs=[pl.BlockSpec(memory_space=SMEM)] * 2 + [vmem] * 4,
        out_specs=[vmem] * len(outs),
        compiler_params=LIMIT,
        name="near",
    )(in_hbm(pair_index), in_hbm(pair_counts), band, col_bf, row_wide, spare)
    mine = held[:far] + near[:2] + held[far:] + near[2:]

    swap = [(r, (r + 1) % cores) for r in range(cores)]
    owners = sorted(
        ((dt, dr) for dt in range(tilts) for dr in range(cores)), key=lambda o: (o[0] == 0, o)
    )
    each = VB_DEV // len(owners)
    share = jax.ShapeDtypeStruct((each * CHUNK_ROWS, block_cols), f32)
    mark = jax.ShapeDtypeStruct((sources, CHUNK_ROWS, block_cols), f32)
    padded = jax.ShapeDtypeStruct(((each + 1) * CHUNK_ROWS, block_cols), f32)
    got = [lax.ppermute(other, "rep", swap)]
    got.append(lax.ppermute(keep_until(rest, got[0]), "rep", swap))

    def send(block, step):
        ring = [(p, partner(p, step, peers)) for p in range(peers)]
        return lax.ppermute(block, "slab", ring)

    first = []
    for k in range(sources):
        h, at = (0, k * tall) if k < far else (1, (k - far) * tall)
        block = mine[k] + got[h][at : at + tall]
        first.append(send(block, shifts[k]) if shifts[k] else block)
    def join(after, part):
        late = mine[sources:][part]
        return pl.pallas_call(
            functools.partial(join_kernel, (sources - far) * tall + part.start * lanes),
            out_shape=shapes[sources : 2 * sources][part],
            in_specs=[vmem] * (len(late) + 2),
            out_specs=[vmem] * len(late),
            compiler_params=LIMIT,
            name="join",
        )(after, got[1], *late)

    def place(blocks, extra, h):
        shapes = [padded if dt else share for dt, dr in owners] + [mark]
        if h:
            shapes = [share] * len(owners)
        return pl.pallas_call(
            functools.partial(place_kernel, sources, owners, h == 0),
            out_shape=shapes,
            in_specs=[vmem] * (sources + len(extra)),
            out_specs=[vmem] * len(shapes),
            compiler_params=LIMIT,
            name="place",
        )(*blocks, *extra)

    def share_out(part, owner):
        dt, dr = owner
        if not (dt or dr):
            return part
        route = [
            (t * cores + r, (t + dt) % tilts * cores + (r + dr) % cores)
            for t in range(tilts)
            for r in range(cores)
        ]
        return lax.ppermute(part, ("tilt", "rep"), route)

    joined = []
    for k in range(far):
        joined += join(first[k], slice(k, k + 1 if k + 1 < far else sources))
    second = [send(block, k) if k else block for block, k in zip(joined, shifts)]
    *parts, marks = place(first, [], 0)
    extra = [share_out(part, owner) for part, owner in zip(parts, owners)]
    held = [part for part, (dt, dr) in zip(extra, owners) if dr and not dt]
    late = place(second, [marks, *held], 1)
    extra += [share_out(part, owner) for part, owner in zip(late, owners)]
    return pl.pallas_call(
        functools.partial(sum_kernel, owners),
        out_shape=jax.ShapeDtypeStruct((each, cores, block_rows, block_cols), f32),
        in_specs=[vmem] * len(extra),
        out_specs=vmem,
        compiler_params=LIMIT,
        name="total",
    )(*extra)


def solution(mesh):
    in_specs = (
        P(("groups", "tilt"), None, None, "slab", None),
        P(),
        P(),
        P(("groups", "tilt"), ("slab", "rep"), None, None, None),
        P(("groups", "tilt"), ("slab", "rep")),
        P(None, ("groups", "tilt"), "slab", None, None),
        P(("groups", "tilt"), "slab", None),
        P(),
        P(),
    )
    out_specs = P(("groups", "slab", "tilt", "rep"), None, None, None)
    return jax.shard_map(
        on_device, mesh=mesh, in_specs=in_specs, out_specs=out_specs, check_vma=False
    )
```

```python
import functools
import math

import jax
import jax.numpy as jnp
import numpy as np
from jax import lax
from jax.experimental import pallas as pl
from jax.experimental.pallas import tpu as pltpu
from jax.sharding import PartitionSpec as P

VB_DEV = 64
REACH = 3
CHUNKS = 2
CHUNK_ROWS = 8
BATCH = 8
HIGH = lax.Precision.HIGHEST
SMEM = pltpu.SMEM
VMEM = pltpu.VMEM
LIMIT = pltpu.CompilerParams(vmem_limit_bytes=40 * 1024 * 1024)


def dot(left, right, precision=None):
    return jnp.dot(left, right, precision=precision, preferred_element_type=jnp.float32)


def slab_steps(peers):
    if peers <= REACH + 1:
        return tuple(sorted(range(peers), key=lambda k: (k == 0, k < peers // 2, k)))
    ring = [s for k in range(REACH, 0, -1) for s in (peers - k, k)]
    return (*ring, 0)


def partner(slab, step, peers):
    if peers <= REACH + 1 and peers & (peers - 1) == 0:
        return slab ^ step
    return (slab + step) % peers


def angle_table(length):
    grid = np.arange(length)
    angles = (grid[:, None] * grid[None, :] % length) * (2.0 * math.pi / length)
    return np.concatenate([np.cos(angles), np.sin(angles)], axis=1).astype(np.float32)


def propagator_blocks(phases, table):
    length = phases.shape[-1]
    row = lax.broadcasted_iota(jnp.int32, (8, length), 0)
    waves = jnp.where(row == 0, jnp.cos(phases), jnp.sin(phases))
    sums = dot(waves, table, HIGH) * (1.0 / length)
    cc, cs = sums[0:1, :length], sums[0:1, length:]
    sc, ss = sums[1:2, :length], sums[1:2, length:]

    def circulant(line):
        wide = jnp.broadcast_to(line, (length, length))
        return pltpu.roll(wide, 0, 1, stride=1, stride_axis=0)

    kr, ki = circulant(cc + ss), circulant(sc - cs)
    krt, kit = circulant(cc - ss), circulant(sc + cs)
    whole = jnp.concatenate(
        [jnp.concatenate([kr, -ki], 1), jnp.concatenate([ki, kr], 1)], 0
    ).astype(jnp.bfloat16)
    turned = jnp.concatenate(
        [jnp.concatenate([krt, kit], 1), jnp.concatenate([-kit, krt], 1)], 0
    ).astype(jnp.bfloat16)
    return whole, turned


def mix_blocks(shifts, which, index_ref, count_ref, band, col_bf, row_scr, put):
    me, core = lax.axis_index("slab"), lax.axis_index("rep")
    peers = lax.axis_size("slab")
    f32, bf16 = jnp.float32, jnp.bfloat16
    capacity = index_ref.shape[-1]
    block_rows, block_cols = band.shape[-2:]
    wide = BATCH * block_rows
    strip = lax.div(lax.broadcasted_iota(jnp.int32, (block_rows, wide), 1), block_rows)
    half = block_rows // CHUNKS
    mark_down = lax.broadcasted_iota(jnp.int32, (half, capacity * half), 0)
    mark_along = lax.broadcasted_iota(jnp.int32, (half, capacity * half), 1)
    mark_slot = jnp.where(lax.rem(mark_along, half) == mark_down, lax.div(mark_along, half), -1)
    for k in which:
        dest = partner(me, shifts[k], peers)
        live = count_ref[0, 0, dest]
        marks = jnp.full(mark_slot.shape, VB_DEV, jnp.int32)
        for first in range(0, capacity, BATCH):
            inner, picks = [], []
            for slot in range(first, first + BATCH, 2):
                pairs, factors = [], []
                for one in (slot, slot + 1):
                    block = index_ref[0, 0, 0, dest, one]
                    target = index_ref[1, 0, 0, dest, one]
                    t = index_ref[2, 0, 0, dest, one]
                    target = jnp.where(one < live, target, VB_DEV)
                    marks = jnp.where(mark_slot == one, target, marks)
                    pairs += [band[core, block], band[1 - core, block]]
                    factors.append(col_bf[t])
                    picked = jnp.where(strip == one - first, row_scr[t], 0.0)
                    picks.append(picked.astype(bf16))
                mixed = dot(jnp.concatenate(pairs, 0), jnp.concatenate(factors, 1)).astype(bf16)
                for n in (0, 1):
                    lanes = slice(n * block_cols, (n + 1) * block_cols)
                    top = 2 * n * block_rows
                    inner.append(
                        jnp.concatenate(
                            [
                                mixed[top : top + block_rows, lanes],
                                mixed[top + block_rows : top + 2 * block_rows, lanes],
                            ],
                            1,
                        )
                    )
            result = dot(jnp.concatenate(picks, 0), jnp.concatenate(inner, 0))
            for h in range(CHUNKS):
                for slot in range(first, first + BATCH):
                    top = (slot - first) * block_rows + h * half
                    put(k, h, slot * half, result[top : top + half])
        marks = marks.astype(f32)
        put(k, 0, capacity * half, jnp.concatenate([marks, jnp.zeros_like(marks)], 1))


def near_kernel(shifts, index_ref, count_ref, band, col_bf, row_scr, spare, *refs):
    mine, other = refs[:-1], refs[-1]
    far, near = len(shifts) - 2, 2
    half, cols = CHUNK_ROWS, band.shape[-1]
    lines = index_ref.shape[-1] * half
    late = near * (lines + half)
    other[late : late + far * lines] = spare[...]

    def put(k, h, row, value):
        base = late + k * lines if h else (k - far) * (lines + half)
        mine[h * near + k - far][row : row + half] = value[:, :cols]
        other[base + row : base + row + half] = value[:, cols:]

    mix_blocks(shifts, range(far, far + near), index_ref, count_ref, band, col_bf, row_scr, put)


def frame_kernel(
    shifts,
    pos_hbm,
    index_hbm,
    count_hbm,
    phase_hbm,
    table_hbm,
    obj_hbm,
    probe_hbm,
    cot_hbm,
    row_hbm,
    col_hbm,
    *rest,
):
    far = len(shifts) - 2
    mine, swaps = rest[: 2 * far], rest[2 * far : 2 * far + 2]
    band, col_bf, row_scr, index_out, count_out = rest[2 * far + 2 : 2 * far + 7]
    scratch = rest[2 * far + 7 :]
    pos_ref, index_ref, count_ref = scratch[0:3]
    phase_ref, table_ref, obj_ref, probe_ref, cot_ref, row_ref, col_ref = scratch[3:10]
    sems, window = scratch[10:]
    slices = obj_ref.shape[2]
    copies = [
        pltpu.make_async_copy(src, dst, sems.at[i])
        for i, (src, dst) in enumerate(
            [
                (phase_hbm, phase_ref),
                (table_hbm, table_ref),
                (pos_hbm, pos_ref),
                (probe_hbm, probe_ref),
                (index_hbm, index_ref),
                (count_hbm, count_ref),
                (row_hbm, row_ref),
            ]
        )
    ]
    got_phase, got_table, got_pos, got_probe, got_index, got_count, got_row = copies
    got_obj = [
        pltpu.make_async_copy(obj_hbm.at[0, :, s], obj_ref.at[0, :, s], sems.at[len(copies) + s])
        for s in range(slices)
    ]
    got_cot = pltpu.make_async_copy(cot_hbm, cot_ref, sems.at[len(copies) + slices])
    got_col = pltpu.make_async_copy(col_hbm, col_ref, sems.at[len(copies) + slices + 1])
    got_lists = [
        pltpu.make_async_copy(index_hbm, index_out, sems.at[len(copies) + slices + 2]),
        pltpu.make_async_copy(count_hbm, count_out, sems.at[len(copies) + slices + 3]),
    ]
    order = [s for i in range((slices + 1) // 2) for s in sorted({i, slices - 1 - i})]
    for copy in (got_pos, got_phase, got_table, *[got_obj[s] for s in order], got_probe, got_cot):
        copy.start()
    for copy in (got_index, got_count, got_row, got_col, *got_lists):
        copy.start()

    size = probe_ref.shape[-1]
    rows, cols = obj_ref.shape[3:]
    count = cot_ref.shape[1]
    group = 2 if count % 2 == 0 else 1
    f32, bf16 = jnp.float32, jnp.bfloat16

    got_pos.wait()
    got_phase.wait()
    got_table.wait()
    col_down = lax.broadcasted_iota(jnp.int32, (cols, size), 0)
    lane = lax.broadcasted_iota(jnp.int32, (cols, size), 1)
    cut = jnp.concatenate(
        [(col_down == lane + pos_ref[0, w]).astype(bf16) for w in range(count)], 1
    )
    whole, turned = propagator_blocks(phase_ref[...], table_ref[...])

    for copy in got_obj:
        copy.wait()
    got_probe.wait()
    got_cot.wait()
    got_row.wait()
    got_col.wait()
    got_index.wait()
    got_count.wait()
    for copy in got_lists:
        copy.wait()
    for s in order:
        source = jnp.concatenate([obj_ref[0, 0, s], obj_ref[0, 1, s]], 0)
        window[s] = dot(source, cut).astype(bf16)

    def tile(s, c, w):
        return window[s, c * rows : (c + 1) * rows, w * size : (w + 1) * size]

    def left(fields, matrix):
        parts = []
        for g in range(0, count, group):
            stack = jnp.concatenate(
                [jnp.concatenate([fields[w][c] for w in range(g, g + group)], 1) for c in (0, 1)], 0
            )
            parts.append(dot(matrix, stack).astype(bf16))
        return parts

    def right(parts, matrix):
        result = []
        for part in parts:
            stack = jnp.concatenate(
                [
                    jnp.concatenate(
                        [
                            part[c * size : (c + 1) * size, k * size : (k + 1) * size]
                            for c in (0, 1)
                        ],
                        1,
                    )
                    for k in range(group)
                ],
                0,
            )
            done = dot(stack, matrix).astype(bf16)
            for k in range(group):
                lines = done[k * size : (k + 1) * size]
                result.append((lines[:, :size], lines[:, size:]))
        return result

    def product(one, two, conjugate):
        a_re, a_im = one[0].astype(f32), one[1].astype(f32)
        b_re, b_im = two[0].astype(f32), two[1].astype(f32)
        if conjugate:
            a_im = -a_im
        return (
            (a_re * b_re - a_im * b_im).astype(bf16),
            (a_re * b_im + a_im * b_re).astype(bf16),
        )

    block_rows, block_cols = row_ref.shape[-1], col_ref.shape[-1]
    across = cols // block_cols
    psi, chi = {}, {}
    now = [(probe_ref[0], probe_ref[1])] * count
    back = [(cot_ref[0, w, 0], cot_ref[0, w, 1]) for w in range(count)]
    lane_down = lax.broadcasted_iota(jnp.int32, (size, cols), 0)
    col = lax.broadcasted_iota(jnp.int32, (size, cols), 1)
    paste = jnp.concatenate(
        [(col == lane_down + pos_ref[0, w]).astype(bf16) for w in range(count)], 0
    )
    for i in range(slices):
        s, e = i, slices - 1 - i
        psi[s], chi[e] = now, back
        if i + 1 < slices:
            here = [(tile(s, 0, w), tile(s, 1, w)) for w in range(count)]
            there = [(tile(e, 0, w), tile(e, 1, w)) for w in range(count)]
            passed = [product(here[w], now[w], False) for w in range(count)]
            rho = [product(there[w], back[w], True) for w in range(count)]
            now, back = left(passed, whole), left(rho, turned)
            now, back = right(now, turned), right(back, whole)
        for t in sorted({s, e}):
            if t not in psi or t not in chi or max(t, slices - 1 - t) != i:
                continue
            grads = [product(psi[t][w], chi[t][w], True) for w in range(count)]
            stack = jnp.concatenate(
                [jnp.concatenate([grads[w][c] for w in range(count)], 1) for c in (0, 1)], 0
            )
            spread = dot(stack, paste).astype(bf16)
            for c in (0, 1):
                for k in range(rows // block_rows):
                    top = c * rows + k * block_rows
                    for j in range(across):
                        band[c, (t * (rows // block_rows) + k) * across + j] = spread[
                            top : top + block_rows, j * block_cols : (j + 1) * block_cols
                        ]

    tiles = row_ref.shape[0]
    wide = BATCH * block_rows
    col_bf[...] = col_ref[...].astype(bf16)
    down = lax.broadcasted_iota(jnp.int32, (block_rows, wide), 0)
    along = lax.broadcasted_iota(jnp.int32, (block_rows, wide), 1)
    repeat = (lax.rem(along, block_rows) == down).astype(bf16)
    row_wide = dot(row_ref[...].reshape(tiles * block_rows, block_rows).astype(bf16), repeat)
    row_scr[...] = row_wide.reshape(tiles, block_rows, wide)
    half = block_rows // CHUNKS

    def put(k, h, row, value):
        base = k * mine[h * far].shape[0] + row
        mine[h * far + k][row : row + half] = value[:, :block_cols]
        swaps[h][base : base + half] = value[:, block_cols:]

    mix_blocks(shifts, range(far), index_ref, count_ref, band, col_bf, row_scr, put)


def keep_until(value, after):
    anywhere = pl.BlockSpec(memory_space=pl.ANY)

    def kernel(value_ref, after_ref, out_ref):
        pass

    return pl.pallas_call(
        kernel,
        out_shape=jax.ShapeDtypeStruct(value.shape, value.dtype),
        in_specs=[anywhere] * 2,
        out_specs=anywhere,
        input_output_aliases={0: 0},
        compiler_params=LIMIT,
        name="keep",
    )(value, after)


def join_kernel(base, first_ref, got_ref, *refs):
    count = len(refs) // 2
    for part, out in zip(refs[:count], refs[count:]):
        tall = part.shape[0]
        out[...] = part[...] + got_ref[base : base + tall]
        base += tall


def place_kernel(sources, owners, first, *refs):
    tilt, core = lax.axis_index("tilt"), lax.axis_index("rep")
    tilts, cores = lax.axis_size("tilt"), lax.axis_size("rep")
    each = VB_DEV // (tilts * cores)
    blocks = refs[:sources]
    half, lanes = CHUNK_ROWS, blocks[0].shape[-1]
    size = each * half
    if first:
        outs, mark_ref = refs[sources:-1], refs[-1]
        for k, block in enumerate(blocks):
            mark_ref[k] = block[lanes:]
    else:
        mark_ref, outs = refs[sources], refs[sources + cores :]
    data = jnp.concatenate([block[:lanes].astype(jnp.bfloat16) for block in blocks], 0)
    volume = lax.broadcasted_iota(jnp.int32, (each, half, lanes), 0).astype(jnp.float32)
    for out, (dt, dr) in zip(outs, owners):
        owner = lax.rem(tilt + dt, tilts) * cores + lax.rem(core + dr, cores)
        base = (owner * each).astype(jnp.float32)
        hot = []
        for k in range(sources):
            mark = mark_ref[k] - base
            hit = jnp.where(volume == mark[None], 1.0, 0.0)
            hot.append(hit.reshape(size, lanes).astype(jnp.bfloat16))
        out[:size] = dot(jnp.concatenate(hot, 1), data)
        if out.shape[0] > size:
            out[size:] = jnp.zeros((out.shape[0] - size, out.shape[1]), jnp.float32)


def sum_kernel(owners, *refs):
    out_ref = refs[-1]
    core, cores = lax.axis_index("rep"), lax.axis_size("rep")
    each, cols = out_ref.shape[0], out_ref.shape[-1]
    size = each * CHUNK_ROWS
    for h in range(CHUNKS):
        parts = refs[h * len(owners) : (h + 1) * len(owners)]
        for dr in range(cores):
            values = [ref[:size] for ref, (_, r) in zip(parts, owners) if r == dr]
            total = functools.reduce(jnp.add, values).reshape(each, CHUNK_ROWS, cols)
            out_ref[:, lax.rem(core + dr, cores), pl.ds(h * CHUNK_ROWS, CHUNK_ROWS)] = total


def on_device(
    object_slab,
    probe_field,
    phases,
    cotangent,
    positions,
    pair_index,
    pair_counts,
    row_interp,
    col_interp,
):
    peers = lax.axis_size("slab")
    tilts, cores = lax.axis_size("tilt"), lax.axis_size("rep")
    shifts = slab_steps(peers)
    capacity = pair_index.shape[-1]
    block_rows, block_cols = row_interp.shape[-1], col_interp.shape[-1]
    _, _, slices, rows, cols = object_slab.shape
    windows, size = cotangent.shape[1], cotangent.shape[-1]
    f32, bf16 = jnp.float32, jnp.bfloat16
    hbm, vmem = pl.BlockSpec(memory_space=pltpu.HBM), pl.BlockSpec(memory_space=VMEM)
    sources = len(shifts)
    lanes = capacity * CHUNK_ROWS

    phase_line = phases.reshape(1, -1)
    table = jnp.asarray(angle_table(size))
    frames = (slices * (rows // block_rows) * (cols // block_cols), block_rows, block_cols)
    far = sources - 2
    tall = lanes + CHUNK_ROWS
    heights = [tall] * sources + [lanes] * sources
    swapped = [far * tall, (sources - far) * tall + sources * lanes]
    shapes = [jax.ShapeDtypeStruct((tall, block_cols), f32) for tall in heights + swapped]
    fetched = [
        (phase_line, VMEM),
        (table, VMEM),
        (object_slab, VMEM),
        (probe_field, VMEM),
        (cotangent, VMEM),
        (row_interp, VMEM),
        (col_interp, VMEM),
    ]
    scalars = [positions, pair_index, pair_counts]
    in_hbm = functools.partial(pltpu.with_memory_space_constraint, memory_space=pltpu.HBM)
    passed = [
        jax.ShapeDtypeStruct((2,) + frames, bf16),
        jax.ShapeDtypeStruct(col_interp.shape, bf16),
        jax.ShapeDtypeStruct((row_interp.shape[0], block_rows, BATCH * block_rows), f32),
        jax.ShapeDtypeStruct(pair_index.shape, pair_index.dtype),
        jax.ShapeDtypeStruct(pair_counts.shape, pair_counts.dtype),
    ]
    spare = jax.ShapeDtypeStruct((far * lanes, block_cols), f32)
    outs = shapes[:far] + shapes[sources : sources + far] + [shapes[-2], spare] + passed
    *held, other, spare, band, col_bf, row_wide, index_near, count_near = pl.pallas_call(
        functools.partial(frame_kernel, shifts),
        out_shape=outs,
        in_specs=[hbm] * 10,
        out_specs=[vmem] * len(outs),
        scratch_shapes=[SMEM(x.shape, x.dtype) for x in scalars]
        + [space(x.shape, x.dtype) for x, space in fetched]
        + [
            pltpu.SemaphoreType.DMA((11 + slices,)),
            VMEM((slices, 2 * rows, windows * size), bf16),
        ],
        compiler_params=LIMIT,
        name="frame",
    )(*[in_hbm(x) for x in scalars + [x for x, _ in fetched]])
    outs = shapes[far:sources] + shapes[sources + far : 2 * sources] + [shapes[-1]]
    *near, rest = pl.pallas_call(
        functools.partial(near_kernel, shifts),
        out_shape=outs,
        in_specs=[pl.BlockSpec(memory_space=SMEM)] * 2 + [vmem] * 4,
        out_specs=[vmem] * len(outs),
        compiler_params=LIMIT,
        name="near",
    )(index_near, count_near, band, col_bf, row_wide, spare)
    mine = held[:far] + near[:2] + held[far:] + near[2:]

    swap = [(r, (r + 1) % cores) for r in range(cores)]
    owners = sorted(
        ((dt, dr) for dt in range(tilts) for dr in range(cores)), key=lambda o: (o[0] == 0, o)
    )
    each = VB_DEV // len(owners)
    share = jax.ShapeDtypeStruct((each * CHUNK_ROWS, block_cols), f32)
    mark = jax.ShapeDtypeStruct((sources, CHUNK_ROWS, block_cols), f32)
    padded = jax.ShapeDtypeStruct(((each + 1) * CHUNK_ROWS, block_cols), f32)
    got = [lax.ppermute(other, "rep", swap)]
    got.append(lax.ppermute(keep_until(rest, got[0]), "rep", swap))

    def send(block, step):
        ring = [(p, partner(p, step, peers)) for p in range(peers)]
        return lax.ppermute(block, "slab", ring)

    first = []
    for k in range(sources):
        h, at = (0, k * tall) if k < far else (1, (k - far) * tall)
        block = mine[k] + got[h][at : at + tall]
        first.append(send(block, shifts[k]) if shifts[k] else block)
    def join(after, part):
        late = mine[sources:][part]
        return pl.pallas_call(
            functools.partial(join_kernel, (sources - far) * tall + part.start * lanes),
            out_shape=shapes[sources : 2 * sources][part],
            in_specs=[vmem] * (len(late) + 2),
            out_specs=[vmem] * len(late),
            compiler_params=LIMIT,
            name="join",
        )(after, got[1], *late)

    def place(blocks, extra, h):
        shapes = [padded if dt else share for dt, dr in owners] + [mark]
        if h:
            shapes = [share] * len(owners)
        return pl.pallas_call(
            functools.partial(place_kernel, sources, owners, h == 0),
            out_shape=shapes,
            in_specs=[vmem] * (sources + len(extra)),
            out_specs=[vmem] * len(shapes),
            compiler_params=LIMIT,
            name="place",
        )(*blocks, *extra)

    def share_out(part, owner):
        dt, dr = owner
        if not (dt or dr):
            return part
        route = [
            (t * cores + r, (t + dt) % tilts * cores + (r + dr) % cores)
            for t in range(tilts)
            for r in range(cores)
        ]
        return lax.ppermute(part, ("tilt", "rep"), route)

    joined = []
    for k in range(far):
        joined += join(first[k], slice(k, k + 1 if k + 1 < far else sources))
    second = [send(block, k) if k else block for block, k in zip(joined, shifts)]
    *parts, marks = place(first, [], 0)
    extra = [share_out(part, owner) for part, owner in zip(parts, owners)]
    held = [part for part, (dt, dr) in zip(extra, owners) if dr and not dt]
    late = place(second, [marks, *held], 1)
    extra += [share_out(part, owner) for part, owner in zip(late, owners)]
    return pl.pallas_call(
        functools.partial(sum_kernel, owners),
        out_shape=jax.ShapeDtypeStruct((each, cores, block_rows, block_cols), f32),
        in_specs=[vmem] * len(extra),
        out_specs=vmem,
        compiler_params=LIMIT,
        name="total",
    )(*extra)


def solution(mesh):
    in_specs = (
        P(("groups", "tilt"), None, None, "slab", None),
        P(),
        P(),
        P(("groups", "tilt"), ("slab", "rep"), None, None, None),
        P(("groups", "tilt"), ("slab", "rep")),
        P(None, ("groups", "tilt"), "slab", None, None),
        P(("groups", "tilt"), "slab", None),
        P(),
        P(),
    )
    out_specs = P(("groups", "slab", "tilt", "rep"), None, None, None)
    return jax.shard_map(
        on_device, mesh=mesh, in_specs=in_specs, out_specs=out_specs, check_vma=False
    )
```

```python
import functools
import math

import jax
import jax.numpy as jnp
import numpy as np
from jax import lax
from jax.experimental import pallas as pl
from jax.experimental.pallas import tpu as pltpu
from jax.sharding import PartitionSpec as P

VB_DEV = 64
REACH = 3
CHUNKS = 2
CHUNK_ROWS = 8
BATCH = 8
HIGH = lax.Precision.HIGHEST
SMEM = pltpu.SMEM
VMEM = pltpu.VMEM
LIMIT = pltpu.CompilerParams(vmem_limit_bytes=40 * 1024 * 1024)


def dot(left, right, precision=None):
    return jnp.dot(left, right, precision=precision, preferred_element_type=jnp.float32)


def slab_steps(peers):
    if peers <= REACH + 1:
        return tuple(sorted(range(peers), key=lambda k: (k == 0, k < peers // 2, k)))
    ring = [s for k in range(REACH, 0, -1) for s in (peers - k, k)]
    return (*ring, 0)


def partner(slab, step, peers):
    if peers <= REACH + 1 and peers & (peers - 1) == 0:
        return slab ^ step
    return (slab + step) % peers


def angle_table(length):
    grid = np.arange(length)
    angles = (grid[:, None] * grid[None, :] % length) * (2.0 * math.pi / length)
    return np.concatenate([np.cos(angles), np.sin(angles)], axis=1).astype(np.float32)


def propagator_blocks(phases, table):
    length = phases.shape[-1]
    row = lax.broadcasted_iota(jnp.int32, (8, length), 0)
    waves = jnp.where(row == 0, jnp.cos(phases), jnp.sin(phases))
    sums = dot(waves, table, HIGH) * (1.0 / length)
    cc, cs = sums[0:1, :length], sums[0:1, length:]
    sc, ss = sums[1:2, :length], sums[1:2, length:]

    def circulant(line):
        wide = jnp.broadcast_to(line, (length, length))
        return pltpu.roll(wide, 0, 1, stride=1, stride_axis=0)

    kr, ki = circulant(cc + ss), circulant(sc - cs)
    krt, kit = circulant(cc - ss), circulant(sc + cs)
    whole = jnp.concatenate(
        [jnp.concatenate([kr, -ki], 1), jnp.concatenate([ki, kr], 1)], 0
    ).astype(jnp.bfloat16)
    turned = jnp.concatenate(
        [jnp.concatenate([krt, kit], 1), jnp.concatenate([-kit, krt], 1)], 0
    ).astype(jnp.bfloat16)
    return whole, turned


def mix_blocks(shifts, which, index_ref, count_ref, band, col_bf, row_scr, put):
    me, core = lax.axis_index("slab"), lax.axis_index("rep")
    peers = lax.axis_size("slab")
    f32, bf16 = jnp.float32, jnp.bfloat16
    capacity = index_ref.shape[-1]
    block_rows, block_cols = band.shape[-2:]
    wide = BATCH * block_rows
    strip = lax.div(lax.broadcasted_iota(jnp.int32, (block_rows, wide), 1), block_rows)
    half = block_rows // CHUNKS
    mark_down = lax.broadcasted_iota(jnp.int32, (half, capacity * half), 0)
    mark_along = lax.broadcasted_iota(jnp.int32, (half, capacity * half), 1)
    mark_slot = jnp.where(lax.rem(mark_along, half) == mark_down, lax.div(mark_along, half), -1)
    for k in which:
        dest = partner(me, shifts[k], peers)
        live = count_ref[0, 0, dest]
        marks = jnp.full(mark_slot.shape, VB_DEV, jnp.int32)
        for first in range(0, capacity, BATCH):
            inner, picks = [], []
            for slot in range(first, first + BATCH, 2):
                pairs, factors = [], []
                for one in (slot, slot + 1):
                    block = index_ref[0, 0, 0, dest, one]
                    target = index_ref[1, 0, 0, dest, one]
                    t = index_ref[2, 0, 0, dest, one]
                    target = jnp.where(one < live, target, VB_DEV)
                    marks = jnp.where(mark_slot == one, target, marks)
                    pairs += [band[core, block], band[1 - core, block]]
                    factors.append(col_bf[t])
                    picked = jnp.where(strip == one - first, row_scr[t], 0.0)
                    picks.append(picked.astype(bf16))
                mixed = dot(jnp.concatenate(pairs, 0), jnp.concatenate(factors, 1)).astype(bf16)
                for n in (0, 1):
                    lanes = slice(n * block_cols, (n + 1) * block_cols)
                    top = 2 * n * block_rows
                    inner.append(
                        jnp.concatenate(
                            [
                                mixed[top : top + block_rows, lanes],
                                mixed[top + block_rows : top + 2 * block_rows, lanes],
                            ],
                            1,
                        )
                    )
            result = dot(jnp.concatenate(picks, 0), jnp.concatenate(inner, 0))
            for h in range(CHUNKS):
                for slot in range(first, first + BATCH):
                    top = (slot - first) * block_rows + h * half
                    put(k, h, slot * half, result[top : top + half])
        marks = marks.astype(f32)
        put(k, 0, capacity * half, jnp.concatenate([marks, jnp.zeros_like(marks)], 1))


def own_kernel(shifts, index_ref, count_ref, band, col_bf, row_scr, spare, *refs):
    mine, other = refs[:CHUNKS], refs[CHUNKS]
    last = len(shifts) - 1
    half, cols = CHUNK_ROWS, band.shape[-1]
    lines = index_ref.shape[-1] * half
    tall = lines + half
    other[:tall] = spare[:tall]
    other[2 * tall : 2 * tall + last * lines] = spare[tall:]

    def put(k, h, row, value):
        base = (2 * tall + last * lines if h else tall) + row
        mine[h][row : row + half] = value[:, :cols]
        other[base : base + half] = value[:, cols:]

    mix_blocks(shifts, [last], index_ref, count_ref, band, col_bf, row_scr, put)


def frame_kernel(
    shifts,
    pos_hbm,
    index_hbm,
    count_hbm,
    phase_hbm,
    table_hbm,
    obj_hbm,
    probe_hbm,
    cot_hbm,
    row_hbm,
    col_hbm,
    *rest,
):
    far = len(shifts) - 2
    sent = far + 1
    mine, (other, spare) = rest[: 2 * sent], rest[2 * sent : 2 * sent + 2]
    band, col_bf, row_scr, index_out, count_out = rest[2 * sent + 2 : 2 * sent + 7]
    scratch = rest[2 * sent + 7 :]
    pos_ref, index_ref, count_ref = scratch[0:3]
    phase_ref, table_ref, obj_ref, probe_ref, cot_ref, row_ref, col_ref = scratch[3:10]
    sems, window = scratch[10:]
    slices = obj_ref.shape[2]
    copies = [
        pltpu.make_async_copy(src, dst, sems.at[i])
        for i, (src, dst) in enumerate(
            [
                (phase_hbm, phase_ref),
                (table_hbm, table_ref),
                (pos_hbm, pos_ref),
                (probe_hbm, probe_ref),
                (index_hbm, index_ref),
                (count_hbm, count_ref),
                (row_hbm, row_ref),
            ]
        )
    ]
    got_phase, got_table, got_pos, got_probe, got_index, got_count, got_row = copies
    got_obj = [
        pltpu.make_async_copy(obj_hbm.at[0, :, s], obj_ref.at[0, :, s], sems.at[len(copies) + s])
        for s in range(slices)
    ]
    got_cot = pltpu.make_async_copy(cot_hbm, cot_ref, sems.at[len(copies) + slices])
    got_col = pltpu.make_async_copy(col_hbm, col_ref, sems.at[len(copies) + slices + 1])
    got_lists = [
        pltpu.make_async_copy(index_hbm, index_out, sems.at[len(copies) + slices + 2]),
        pltpu.make_async_copy(count_hbm, count_out, sems.at[len(copies) + slices + 3]),
    ]
    order = [s for i in range((slices + 1) // 2) for s in sorted({i, slices - 1 - i})]
    for copy in (got_pos, got_phase, got_table, *[got_obj[s] for s in order], got_probe, got_cot):
        copy.start()
    for copy in (got_index, got_count, got_row, got_col, *got_lists):
        copy.start()

    size = probe_ref.shape[-1]
    rows, cols = obj_ref.shape[3:]
    count = cot_ref.shape[1]
    group = 2 if count % 2 == 0 else 1
    f32, bf16 = jnp.float32, jnp.bfloat16

    got_pos.wait()
    got_phase.wait()
    got_table.wait()
    col_down = lax.broadcasted_iota(jnp.int32, (cols, size), 0)
    lane = lax.broadcasted_iota(jnp.int32, (cols, size), 1)
    cut = jnp.concatenate(
        [(col_down == lane + pos_ref[0, w]).astype(bf16) for w in range(count)], 1
    )
    whole, turned = propagator_blocks(phase_ref[...], table_ref[...])

    for copy in got_obj:
        copy.wait()
    got_probe.wait()
    got_cot.wait()
    got_row.wait()
    got_col.wait()
    got_index.wait()
    got_count.wait()
    for copy in got_lists:
        copy.wait()
    for s in order:
        source = jnp.concatenate([obj_ref[0, 0, s], obj_ref[0, 1, s]], 0)
        window[s] = dot(source, cut).astype(bf16)

    def tile(s, c, w):
        return window[s, c * rows : (c + 1) * rows, w * size : (w + 1) * size]

    def left(fields, matrix):
        parts = []
        for g in range(0, count, group):
            stack = jnp.concatenate(
                [jnp.concatenate([fields[w][c] for w in range(g, g + group)], 1) for c in (0, 1)], 0
            )
            parts.append(dot(matrix, stack).astype(bf16))
        return parts

    def right(parts, matrix):
        result = []
        for part in parts:
            stack = jnp.concatenate(
                [
                    jnp.concatenate(
                        [
                            part[c * size : (c + 1) * size, k * size : (k + 1) * size]
                            for c in (0, 1)
                        ],
                        1,
                    )
                    for k in range(group)
                ],
                0,
            )
            done = dot(stack, matrix).astype(bf16)
            for k in range(group):
                lines = done[k * size : (k + 1) * size]
                result.append((lines[:, :size], lines[:, size:]))
        return result

    def product(one, two, conjugate):
        a_re, a_im = one[0].astype(f32), one[1].astype(f32)
        b_re, b_im = two[0].astype(f32), two[1].astype(f32)
        if conjugate:
            a_im = -a_im
        return (
            (a_re * b_re - a_im * b_im).astype(bf16),
            (a_re * b_im + a_im * b_re).astype(bf16),
        )

    block_rows, block_cols = row_ref.shape[-1], col_ref.shape[-1]
    across = cols // block_cols
    psi, chi = {}, {}
    now = [(probe_ref[0], probe_ref[1])] * count
    back = [(cot_ref[0, w, 0], cot_ref[0, w, 1]) for w in range(count)]
    lane_down = lax.broadcasted_iota(jnp.int32, (size, cols), 0)
    col = lax.broadcasted_iota(jnp.int32, (size, cols), 1)
    paste = jnp.concatenate(
        [(col == lane_down + pos_ref[0, w]).astype(bf16) for w in range(count)], 0
    )
    for i in range(slices):
        s, e = i, slices - 1 - i
        psi[s], chi[e] = now, back
        if i + 1 < slices:
            here = [(tile(s, 0, w), tile(s, 1, w)) for w in range(count)]
            there = [(tile(e, 0, w), tile(e, 1, w)) for w in range(count)]
            passed = [product(here[w], now[w], False) for w in range(count)]
            rho = [product(there[w], back[w], True) for w in range(count)]
            now, back = left(passed, whole), left(rho, turned)
            now, back = right(now, turned), right(back, whole)
        for t in sorted({s, e}):
            if t not in psi or t not in chi or max(t, slices - 1 - t) != i:
                continue
            grads = [product(psi[t][w], chi[t][w], True) for w in range(count)]
            stack = jnp.concatenate(
                [jnp.concatenate([grads[w][c] for w in range(count)], 1) for c in (0, 1)], 0
            )
            spread = dot(stack, paste).astype(bf16)
            for c in (0, 1):
                for k in range(rows // block_rows):
                    top = c * rows + k * block_rows
                    for j in range(across):
                        band[c, (t * (rows // block_rows) + k) * across + j] = spread[
                            top : top + block_rows, j * block_cols : (j + 1) * block_cols
                        ]

    tiles = row_ref.shape[0]
    wide = BATCH * block_rows
    col_bf[...] = col_ref[...].astype(bf16)
    down = lax.broadcasted_iota(jnp.int32, (block_rows, wide), 0)
    along = lax.broadcasted_iota(jnp.int32, (block_rows, wide), 1)
    repeat = (lax.rem(along, block_rows) == down).astype(bf16)
    row_wide = dot(row_ref[...].reshape(tiles * block_rows, block_rows).astype(bf16), repeat)
    row_scr[...] = row_wide.reshape(tiles, block_rows, wide)
    half = block_rows // CHUNKS

    def put(k, h, row, value):
        tall, lines = mine[0].shape[0], mine[sent].shape[0]
        if h:
            swap, base = spare, tall + k * lines + row
        else:
            swap, base = (other, k * tall + row) if k < far else (spare, row)
        mine[h * sent + k][row : row + half] = value[:, :block_cols]
        swap[base : base + half] = value[:, block_cols:]

    mix_blocks(shifts, range(sent), index_ref, count_ref, band, col_bf, row_scr, put)


def keep_until(value, after):
    anywhere = pl.BlockSpec(memory_space=pl.ANY)

    def kernel(value_ref, after_ref, out_ref):
        pass

    return pl.pallas_call(
        kernel,
        out_shape=jax.ShapeDtypeStruct(value.shape, value.dtype),
        in_specs=[anywhere] * 2,
        out_specs=anywhere,
        input_output_aliases={0: 0},
        compiler_params=LIMIT,
        name="keep",
    )(value, after)


def join_kernel(base, first_ref, got_ref, *refs):
    count = len(refs) // 2
    for part, out in zip(refs[:count], refs[count:]):
        tall = part.shape[0]
        out[...] = part[...] + got_ref[base : base + tall]
        base += tall


def place_kernel(sources, owners, first, *refs):
    tilt, core = lax.axis_index("tilt"), lax.axis_index("rep")
    tilts, cores = lax.axis_size("tilt"), lax.axis_size("rep")
    each = VB_DEV // (tilts * cores)
    blocks = refs[:sources]
    half, lanes = CHUNK_ROWS, blocks[0].shape[-1]
    size = each * half
    if first:
        outs, mark_ref = refs[sources:-1], refs[-1]
        for k, block in enumerate(blocks):
            mark_ref[k] = block[lanes:]
    else:
        mark_ref, outs = refs[sources], refs[sources + cores :]
    data = jnp.concatenate([block[:lanes].astype(jnp.bfloat16) for block in blocks], 0)
    volume = lax.broadcasted_iota(jnp.int32, (each, half, lanes), 0).astype(jnp.float32)
    for out, (dt, dr) in zip(outs, owners):
        owner = lax.rem(tilt + dt, tilts) * cores + lax.rem(core + dr, cores)
        base = (owner * each).astype(jnp.float32)
        hot = []
        for k in range(sources):
            mark = mark_ref[k] - base
            hit = jnp.where(volume == mark[None], 1.0, 0.0)
            hot.append(hit.reshape(size, lanes).astype(jnp.bfloat16))
        out[:size] = dot(jnp.concatenate(hot, 1), data)
        if out.shape[0] > size:
            out[size:] = jnp.zeros((out.shape[0] - size, out.shape[1]), jnp.float32)


def sum_kernel(owners, *refs):
    out_ref = refs[-1]
    core, cores = lax.axis_index("rep"), lax.axis_size("rep")
    each, cols = out_ref.shape[0], out_ref.shape[-1]
    size = each * CHUNK_ROWS
    for h in range(CHUNKS):
        parts = refs[h * len(owners) : (h + 1) * len(owners)]
        for dr in range(cores):
            values = [ref[:size] for ref, (_, r) in zip(parts, owners) if r == dr]
            total = functools.reduce(jnp.add, values).reshape(each, CHUNK_ROWS, cols)
            out_ref[:, lax.rem(core + dr, cores), pl.ds(h * CHUNK_ROWS, CHUNK_ROWS)] = total


def on_device(
    object_slab,
    probe_field,
    phases,
    cotangent,
    positions,
    pair_index,
    pair_counts,
    row_interp,
    col_interp,
):
    peers = lax.axis_size("slab")
    tilts, cores = lax.axis_size("tilt"), lax.axis_size("rep")
    shifts = slab_steps(peers)
    capacity = pair_index.shape[-1]
    block_rows, block_cols = row_interp.shape[-1], col_interp.shape[-1]
    _, _, slices, rows, cols = object_slab.shape
    windows, size = cotangent.shape[1], cotangent.shape[-1]
    f32, bf16 = jnp.float32, jnp.bfloat16
    hbm, vmem = pl.BlockSpec(memory_space=pltpu.HBM), pl.BlockSpec(memory_space=VMEM)
    sources = len(shifts)
    lanes = capacity * CHUNK_ROWS

    phase_line = phases.reshape(1, -1)
    table = jnp.asarray(angle_table(size))
    frames = (slices * (rows // block_rows) * (cols // block_cols), block_rows, block_cols)
    far = sources - 2
    tall = lanes + CHUNK_ROWS
    heights = [tall] * sources + [lanes] * sources
    swapped = [far * tall, (sources - far) * tall + sources * lanes]
    shapes = [jax.ShapeDtypeStruct((tall, block_cols), f32) for tall in heights + swapped]
    fetched = [
        (phase_line, VMEM),
        (table, VMEM),
        (object_slab, VMEM),
        (probe_field, VMEM),
        (cotangent, VMEM),
        (row_interp, VMEM),
        (col_interp, VMEM),
    ]
    scalars = [positions, pair_index, pair_counts]
    in_hbm = functools.partial(pltpu.with_memory_space_constraint, memory_space=pltpu.HBM)
    passed = [
        jax.ShapeDtypeStruct((2,) + frames, bf16),
        jax.ShapeDtypeStruct(col_interp.shape, bf16),
        jax.ShapeDtypeStruct((row_interp.shape[0], block_rows, BATCH * block_rows), f32),
        jax.ShapeDtypeStruct(pair_index.shape, pair_index.dtype),
        jax.ShapeDtypeStruct(pair_counts.shape, pair_counts.dtype),
    ]
    sent = far + 1
    spare = jax.ShapeDtypeStruct((tall + sent * lanes, block_cols), f32)
    outs = shapes[:sent] + shapes[sources : sources + sent] + [shapes[-2], spare] + passed
    *held, other, spare, band, col_bf, row_wide, index_near, count_near = pl.pallas_call(
        functools.partial(frame_kernel, shifts),
        out_shape=outs,
        in_specs=[hbm] * 10,
        out_specs=[vmem] * len(outs),
        scratch_shapes=[SMEM(x.shape, x.dtype) for x in scalars]
        + [space(x.shape, x.dtype) for x, space in fetched]
        + [
            pltpu.SemaphoreType.DMA((11 + slices,)),
            VMEM((slices, 2 * rows, windows * size), bf16),
        ],
        compiler_params=LIMIT,
        name="frame",
    )(*[in_hbm(x) for x in scalars + [x for x, _ in fetched]])
    outs = [shapes[sent], shapes[sources + sent], shapes[-1]]
    *own, rest = pl.pallas_call(
        functools.partial(own_kernel, shifts),
        out_shape=outs,
        in_specs=[pl.BlockSpec(memory_space=SMEM)] * 2 + [vmem] * 4,
        out_specs=[vmem] * len(outs),
        compiler_params=LIMIT,
        name="own",
    )(index_near, count_near, band, col_bf, row_wide, spare)
    mine = held[:sent] + own[:1] + held[sent:] + own[1:]

    swap = [(r, (r + 1) % cores) for r in range(cores)]
    owners = sorted(
        ((dt, dr) for dt in range(tilts) for dr in range(cores)), key=lambda o: (o[0] == 0, o)
    )
    each = VB_DEV // len(owners)
    share = jax.ShapeDtypeStruct((each * CHUNK_ROWS, block_cols), f32)
    mark = jax.ShapeDtypeStruct((sources, CHUNK_ROWS, block_cols), f32)
    padded = jax.ShapeDtypeStruct(((each + 1) * CHUNK_ROWS, block_cols), f32)
    got = [lax.ppermute(other, "rep", swap)]
    got.append(lax.ppermute(keep_until(rest, got[0]), "rep", swap))

    def send(block, step):
        ring = [(p, partner(p, step, peers)) for p in range(peers)]
        return lax.ppermute(block, "slab", ring)

    first = []
    for k in range(sources):
        h, at = (0, k * tall) if k < far else (1, (k - far) * tall)
        block = mine[k] + got[h][at : at + tall]
        first.append(send(block, shifts[k]) if shifts[k] else block)
    def join(after, part):
        late = mine[sources:][part]
        return pl.pallas_call(
            functools.partial(join_kernel, (sources - far) * tall + part.start * lanes),
            out_shape=shapes[sources : 2 * sources][part],
            in_specs=[vmem] * (len(late) + 2),
            out_specs=[vmem] * len(late),
            compiler_params=LIMIT,
            name="join",
        )(after, got[1], *late)

    def place(blocks, extra, h):
        shapes = [padded if dt else share for dt, dr in owners] + [mark]
        if h:
            shapes = [share] * len(owners)
        return pl.pallas_call(
            functools.partial(place_kernel, sources, owners, h == 0),
            out_shape=shapes,
            in_specs=[vmem] * (sources + len(extra)),
            out_specs=[vmem] * len(shapes),
            compiler_params=LIMIT,
            name="place",
        )(*blocks, *extra)

    def share_out(part, owner):
        dt, dr = owner
        if not (dt or dr):
            return part
        route = [
            (t * cores + r, (t + dt) % tilts * cores + (r + dr) % cores)
            for t in range(tilts)
            for r in range(cores)
        ]
        return lax.ppermute(part, ("tilt", "rep"), route)

    joined = []
    for k in range(far):
        joined += join(first[k], slice(k, k + 1 if k + 1 < far else sources))
    second = [send(block, k) if k else block for block, k in zip(joined, shifts)]
    *parts, marks = place(first, [], 0)
    extra = [share_out(part, owner) for part, owner in zip(parts, owners)]
    held = [part for part, (dt, dr) in zip(extra, owners) if dr and not dt]
    late = place(second, [marks, *held], 1)
    extra += [share_out(part, owner) for part, owner in zip(late, owners)]
    return pl.pallas_call(
        functools.partial(sum_kernel, owners),
        out_shape=jax.ShapeDtypeStruct((each, cores, block_rows, block_cols), f32),
        in_specs=[vmem] * len(extra),
        out_specs=vmem,
        compiler_params=LIMIT,
        name="total",
    )(*extra)


def solution(mesh):
    in_specs = (
        P(("groups", "tilt"), None, None, "slab", None),
        P(),
        P(),
        P(("groups", "tilt"), ("slab", "rep"), None, None, None),
        P(("groups", "tilt"), ("slab", "rep")),
        P(None, ("groups", "tilt"), "slab", None, None),
        P(("groups", "tilt"), "slab", None),
        P(),
        P(),
    )
    out_specs = P(("groups", "slab", "tilt", "rep"), None, None, None)
    return jax.shard_map(
        on_device, mesh=mesh, in_specs=in_specs, out_specs=out_specs, check_vma=False
    )
```

```python
import functools
import math

import jax
import jax.numpy as jnp
import numpy as np
from jax import lax
from jax.experimental import pallas as pl
from jax.experimental.pallas import tpu as pltpu
from jax.sharding import PartitionSpec as P

VB_DEV = 64
REACH = 3
CHUNKS = 2
CHUNK_ROWS = 8
HIGH = lax.Precision.HIGHEST
SMEM = pltpu.SMEM
VMEM = pltpu.VMEM
LIMIT = pltpu.CompilerParams(vmem_limit_bytes=40 * 1024 * 1024)


def dot(left, right, precision=None):
    return jnp.dot(left, right, precision=precision, preferred_element_type=jnp.float32)


def slab_steps(peers):
    if peers <= REACH + 1:
        return tuple(sorted(range(peers), key=lambda k: (k == 0, k < peers // 2, k)))
    ring = [s for k in range(REACH, 0, -1) for s in (peers - k, k)]
    return (*ring, 0)


def partner(slab, step, peers):
    if peers <= REACH + 1 and peers & (peers - 1) == 0:
        return slab ^ step
    return (slab + step) % peers


def angle_table(length):
    grid = np.arange(length)
    angles = (grid[:, None] * grid[None, :] % length) * (2.0 * math.pi / length)
    return np.concatenate([np.cos(angles), np.sin(angles)], axis=1).astype(np.float32)


def propagator_blocks(phases, table):
    length = phases.shape[-1]
    row = lax.broadcasted_iota(jnp.int32, (8, length), 0)
    waves = jnp.where(row == 0, jnp.cos(phases), jnp.sin(phases))
    sums = dot(waves, table, HIGH) * (1.0 / length)
    cc, cs = sums[0:1, :length], sums[0:1, length:]
    sc, ss = sums[1:2, :length], sums[1:2, length:]

    def circulant(line):
        wide = jnp.broadcast_to(line, (length, length))
        return pltpu.roll(wide, 0, 1, stride=1, stride_axis=0)

    kr, ki = circulant(cc + ss), circulant(sc - cs)
    krt, kit = circulant(cc - ss), circulant(sc + cs)
    whole = jnp.concatenate(
        [jnp.concatenate([kr, -ki], 1), jnp.concatenate([ki, kr], 1)], 0
    ).astype(jnp.bfloat16)
    turned = jnp.concatenate(
        [jnp.concatenate([krt, kit], 1), jnp.concatenate([-kit, krt], 1)], 0
    ).astype(jnp.bfloat16)
    return whole, turned


def frame_kernel(
    shifts,
    pos_hbm,
    index_hbm,
    count_hbm,
    phase_hbm,
    table_hbm,
    obj_hbm,
    probe_hbm,
    cot_hbm,
    row_hbm,
    col_hbm,
    *rest,
):
    far, steps = len(shifts) - 2, len(shifts)
    mine, other, scratch = rest[: 2 * steps], rest[2 * steps : 2 * steps + 2], rest[2 * steps + 2 :]
    pos_ref, index_ref, count_ref = scratch[0:3]
    phase_ref, table_ref, obj_ref, probe_ref, cot_ref, row_ref, col_ref = scratch[3:10]
    sems, band, window, col_bf, row_scr = scratch[10:]
    slices = obj_ref.shape[2]
    copies = [
        pltpu.make_async_copy(src, dst, sems.at[i])
        for i, (src, dst) in enumerate(
            [
                (phase_hbm, phase_ref),
                (table_hbm, table_ref),
                (pos_hbm, pos_ref),
                (probe_hbm, probe_ref),
                (index_hbm, index_ref),
                (count_hbm, count_ref),
                (row_hbm, row_ref),
            ]
        )
    ]
    got_phase, got_table, got_pos, got_probe, got_index, got_count, got_row = copies
    got_obj = [
        pltpu.make_async_copy(obj_hbm.at[0, :, s], obj_ref.at[0, :, s], sems.at[len(copies) + s])
        for s in range(slices)
    ]
    got_cot = pltpu.make_async_copy(cot_hbm, cot_ref, sems.at[len(copies) + slices])
    got_col = pltpu.make_async_copy(col_hbm, col_ref, sems.at[len(copies) + slices + 1])
    order = [s for i in range((slices + 1) // 2) for s in sorted({i, slices - 1 - i})]
    for copy in (got_pos, got_phase, got_table, *[got_obj[s] for s in order], got_probe, got_cot):
        copy.start()
    for copy in (got_index, got_count, got_row, got_col):
        copy.start()

    me, core = lax.axis_index("slab"), lax.axis_index("rep")
    peers = lax.axis_size("slab")
    capacity = index_ref.shape[-1]
    size = probe_ref.shape[-1]
    rows, cols = obj_ref.shape[3:]
    count = cot_ref.shape[1]
    group = 2 if count % 2 == 0 else 1
    f32, bf16 = jnp.float32, jnp.bfloat16

    got_pos.wait()
    got_phase.wait()
    got_table.wait()
    col_down = lax.broadcasted_iota(jnp.int32, (cols, size), 0)
    lane = lax.broadcasted_iota(jnp.int32, (cols, size), 1)
    cut = jnp.concatenate(
        [(col_down == lane + pos_ref[0, w]).astype(bf16) for w in range(count)], 1
    )
    whole, turned = propagator_blocks(phase_ref[...], table_ref[...])

    for copy in got_obj:
        copy.wait()
    got_probe.wait()
    got_cot.wait()
    got_row.wait()
    got_col.wait()
    got_index.wait()
    got_count.wait()
    for s in order:
        source = jnp.concatenate([obj_ref[0, 0, s], obj_ref[0, 1, s]], 0)
        window[s] = dot(source, cut).astype(bf16)

    def tile(s, c, w):
        return window[s, c * rows : (c + 1) * rows, w * size : (w + 1) * size]

    def left(fields, matrix):
        parts = []
        for g in range(0, count, group):
            stack = jnp.concatenate(
                [jnp.concatenate([fields[w][c] for w in range(g, g + group)], 1) for c in (0, 1)], 0
            )
            parts.append(dot(matrix, stack).astype(bf16))
        return parts

    def right(parts, matrix):
        result = []
        for part in parts:
            stack = jnp.concatenate(
                [
                    jnp.concatenate(
                        [
                            part[c * size : (c + 1) * size, k * size : (k + 1) * size]
                            for c in (0, 1)
                        ],
                        1,
                    )
                    for k in range(group)
                ],
                0,
            )
            done = dot(stack, matrix).astype(bf16)
            for k in range(group):
                lines = done[k * size : (k + 1) * size]
                result.append((lines[:, :size], lines[:, size:]))
        return result

    def product(one, two, conjugate):
        a_re, a_im = one[0].astype(f32), one[1].astype(f32)
        b_re, b_im = two[0].astype(f32), two[1].astype(f32)
        if conjugate:
            a_im = -a_im
        return (
            (a_re * b_re - a_im * b_im).astype(bf16),
            (a_re * b_im + a_im * b_re).astype(bf16),
        )

    block_rows, block_cols = row_ref.shape[-1], col_ref.shape[-1]
    across = cols // block_cols
    psi, chi = {}, {}
    now = [(probe_ref[0], probe_ref[1])] * count
    back = [(cot_ref[0, w, 0], cot_ref[0, w, 1]) for w in range(count)]
    lane_down = lax.broadcasted_iota(jnp.int32, (size, cols), 0)
    col = lax.broadcasted_iota(jnp.int32, (size, cols), 1)
    paste = jnp.concatenate(
        [(col == lane_down + pos_ref[0, w]).astype(bf16) for w in range(count)], 0
    )
    for i in range(slices):
        s, e = i, slices - 1 - i
        psi[s], chi[e] = now, back
        if i + 1 < slices:
            here = [(tile(s, 0, w), tile(s, 1, w)) for w in range(count)]
            there = [(tile(e, 0, w), tile(e, 1, w)) for w in range(count)]
            passed = [product(here[w], now[w], False) for w in range(count)]
            rho = [product(there[w], back[w], True) for w in range(count)]
            now, back = left(passed, whole), left(rho, turned)
            now, back = right(now, turned), right(back, whole)
        for t in sorted({s, e}):
            if t not in psi or t not in chi or max(t, slices - 1 - t) != i:
                continue
            grads = [product(psi[t][w], chi[t][w], True) for w in range(count)]
            stack = jnp.concatenate(
                [jnp.concatenate([grads[w][c] for w in range(count)], 1) for c in (0, 1)], 0
            )
            spread = dot(stack, paste).astype(bf16)
            for c in (0, 1):
                for k in range(rows // block_rows):
                    top = c * rows + k * block_rows
                    for j in range(across):
                        band[c, (t * (rows // block_rows) + k) * across + j] = spread[
                            top : top + block_rows, j * block_cols : (j + 1) * block_cols
                        ]

    tiles = row_ref.shape[0]
    batch = 8
    wide = batch * block_rows
    col_bf[...] = col_ref[...].astype(bf16)
    down = lax.broadcasted_iota(jnp.int32, (block_rows, wide), 0)
    along = lax.broadcasted_iota(jnp.int32, (block_rows, wide), 1)
    repeat = (lax.rem(along, block_rows) == down).astype(bf16)
    row_wide = dot(row_ref[...].reshape(tiles * block_rows, block_rows).astype(bf16), repeat)
    row_scr[...] = row_wide.reshape(tiles, block_rows, wide)
    strip = lax.div(along, block_rows)
    half = block_rows // CHUNKS
    mark_down = lax.broadcasted_iota(jnp.int32, (half, capacity * half), 0)
    mark_along = lax.broadcasted_iota(jnp.int32, (half, capacity * half), 1)
    mark_slot = jnp.where(lax.rem(mark_along, half) == mark_down, lax.div(mark_along, half), -1)
    lines = capacity * half
    late = (steps - far) * (lines + half)

    def put(k, h, slot, value):
        at = slot * half
        if h:
            swap, base = other[1], late + k * lines
        elif k < far:
            swap, base = other[0], k * (lines + half)
        else:
            swap, base = other[1], (k - far) * (lines + half)
        mine[h * steps + k][at : at + half] = value[:, :block_cols]
        swap[base + at : base + at + half] = value[:, block_cols:]

    for k, shift in enumerate(shifts):
        dest = partner(me, shift, peers)
        live = count_ref[0, 0, dest]
        marks = jnp.full(mark_slot.shape, VB_DEV, jnp.int32)
        for first in range(0, capacity, batch):
            inner, picks = [], []
            for slot in range(first, first + batch, 2):
                pairs, factors = [], []
                for one in (slot, slot + 1):
                    block = index_ref[0, 0, 0, dest, one]
                    target = index_ref[1, 0, 0, dest, one]
                    t = index_ref[2, 0, 0, dest, one]
                    target = jnp.where(one < live, target, VB_DEV)
                    marks = jnp.where(mark_slot == one, target, marks)
                    pairs += [band[core, block], band[1 - core, block]]
                    factors.append(col_bf[t])
                    picked = jnp.where(strip == one - first, row_scr[t], 0.0)
                    picks.append(picked.astype(bf16))
                mixed = dot(jnp.concatenate(pairs, 0), jnp.concatenate(factors, 1)).astype(bf16)
                for n in (0, 1):
                    lanes = slice(n * block_cols, (n + 1) * block_cols)
                    top = 2 * n * block_rows
                    inner.append(
                        jnp.concatenate(
                            [
                                mixed[top : top + block_rows, lanes],
                                mixed[top + block_rows : top + 2 * block_rows, lanes],
                            ],
                            1,
                        )
                    )
            result = dot(jnp.concatenate(picks, 0), jnp.concatenate(inner, 0))
            for slot in range(first, first + batch):
                for h in range(CHUNKS):
                    top = (slot - first) * block_rows + h * half
                    put(k, h, slot, result[top : top + half])
        marks = marks.astype(f32)
        put(k, 0, capacity, jnp.concatenate([marks, jnp.zeros_like(marks)], 1))


def keep_until(value, after):
    anywhere = pl.BlockSpec(memory_space=pl.ANY)

    def kernel(value_ref, after_ref, out_ref):
        pass

    return pl.pallas_call(
        kernel,
        out_shape=jax.ShapeDtypeStruct(value.shape, value.dtype),
        in_specs=[anywhere] * 2,
        out_specs=anywhere,
        input_output_aliases={0: 0},
        compiler_params=LIMIT,
        name="keep",
    )(value, after)


def join_kernel(base, first_ref, got_ref, *refs):
    count = len(refs) // 2
    for part, out in zip(refs[:count], refs[count:]):
        tall = part.shape[0]
        out[...] = part[...] + got_ref[base : base + tall]
        base += tall


def place_kernel(sources, owners, first, *refs):
    tilt, core = lax.axis_index("tilt"), lax.axis_index("rep")
    tilts, cores = lax.axis_size("tilt"), lax.axis_size("rep")
    each = VB_DEV // (tilts * cores)
    blocks = refs[:sources]
    half, lanes = CHUNK_ROWS, blocks[0].shape[-1]
    size = each * half
    if first:
        outs, mark_ref = refs[sources:-1], refs[-1]
        for k, block in enumerate(blocks):
            mark_ref[k] = block[lanes:]
    else:
        mark_ref, outs = refs[sources], refs[sources + cores :]
    data = jnp.concatenate([block[:lanes].astype(jnp.bfloat16) for block in blocks], 0)
    volume = lax.broadcasted_iota(jnp.int32, (each, half, lanes), 0).astype(jnp.float32)
    for out, (dt, dr) in zip(outs, owners):
        owner = lax.rem(tilt + dt, tilts) * cores + lax.rem(core + dr, cores)
        base = (owner * each).astype(jnp.float32)
        hot = []
        for k in range(sources):
            mark = mark_ref[k] - base
            hit = jnp.where(volume == mark[None], 1.0, 0.0)
            hot.append(hit.reshape(size, lanes).astype(jnp.bfloat16))
        out[:size] = dot(jnp.concatenate(hot, 1), data)
        if out.shape[0] > size:
            out[size:] = jnp.zeros((out.shape[0] - size, out.shape[1]), jnp.float32)


def sum_kernel(owners, *refs):
    out_ref = refs[-1]
    core, cores = lax.axis_index("rep"), lax.axis_size("rep")
    each, cols = out_ref.shape[0], out_ref.shape[-1]
    size = each * CHUNK_ROWS
    for h in range(CHUNKS):
        parts = refs[h * len(owners) : (h + 1) * len(owners)]
        for dr in range(cores):
            values = [ref[:size] for ref, (_, r) in zip(parts, owners) if r == dr]
            total = functools.reduce(jnp.add, values).reshape(each, CHUNK_ROWS, cols)
            out_ref[:, lax.rem(core + dr, cores), pl.ds(h * CHUNK_ROWS, CHUNK_ROWS)] = total


def on_device(
    object_slab,
    probe_field,
    phases,
    cotangent,
    positions,
    pair_index,
    pair_counts,
    row_interp,
    col_interp,
):
    peers = lax.axis_size("slab")
    tilts, cores = lax.axis_size("tilt"), lax.axis_size("rep")
    shifts = slab_steps(peers)
    capacity = pair_index.shape[-1]
    block_rows, block_cols = row_interp.shape[-1], col_interp.shape[-1]
    _, _, slices, rows, cols = object_slab.shape
    windows, size = cotangent.shape[1], cotangent.shape[-1]
    f32, bf16 = jnp.float32, jnp.bfloat16
    hbm, vmem = pl.BlockSpec(memory_space=pltpu.HBM), pl.BlockSpec(memory_space=VMEM)
    sources = len(shifts)
    lanes = capacity * CHUNK_ROWS

    phase_line = phases.reshape(1, -1)
    table = jnp.asarray(angle_table(size))
    frames = (slices * (rows // block_rows) * (cols // block_cols), block_rows, block_cols)
    far = sources - 2
    tall = lanes + CHUNK_ROWS
    heights = [tall] * sources + [lanes] * sources
    swapped = [far * tall, (sources - far) * tall + sources * lanes]
    shapes = [jax.ShapeDtypeStruct((tall, block_cols), f32) for tall in heights + swapped]
    fetched = [
        (phase_line, VMEM),
        (table, VMEM),
        (object_slab, VMEM),
        (probe_field, VMEM),
        (cotangent, VMEM),
        (row_interp, VMEM),
        (col_interp, VMEM),
    ]
    scalars = [positions, pair_index, pair_counts]
    held = pl.pallas_call(
        functools.partial(frame_kernel, shifts),
        out_shape=shapes,
        in_specs=[hbm] * 10,
        out_specs=[vmem] * len(shapes),
        scratch_shapes=[SMEM(x.shape, x.dtype) for x in scalars]
        + [space(x.shape, x.dtype) for x, space in fetched]
        + [
            pltpu.SemaphoreType.DMA((9 + slices,)),
            VMEM((2,) + frames, bf16),
            VMEM((slices, 2 * rows, windows * size), bf16),
            VMEM(col_interp.shape, bf16),
            VMEM((row_interp.shape[0], block_rows, 8 * block_rows), f32),
        ],
        compiler_params=LIMIT,
        name="frame",
    )(*[pltpu.with_memory_space_constraint(x, pltpu.HBM) for x in scalars + [x for x, _ in fetched]])

    swap = [(r, (r + 1) % cores) for r in range(cores)]
    owners = sorted(
        ((dt, dr) for dt in range(tilts) for dr in range(cores)), key=lambda o: (o[0] == 0, o)
    )
    each = VB_DEV // len(owners)
    share = jax.ShapeDtypeStruct((each * CHUNK_ROWS, block_cols), f32)
    mark = jax.ShapeDtypeStruct((sources, CHUNK_ROWS, block_cols), f32)
    padded = jax.ShapeDtypeStruct(((each + 1) * CHUNK_ROWS, block_cols), f32)
    mine, other = held[: len(heights)], held[len(heights) :]
    got = [lax.ppermute(other[0], "rep", swap)]
    got.append(lax.ppermute(keep_until(other[1], got[0]), "rep", swap))

    def send(block, step):
        ring = [(p, partner(p, step, peers)) for p in range(peers)]
        return lax.ppermute(block, "slab", ring)

    first = []
    for k in range(sources):
        h, at = (0, k * tall) if k < far else (1, (k - far) * tall)
        block = mine[k] + got[h][at : at + tall]
        first.append(send(block, shifts[k]) if shifts[k] else block)
    def join(after, part):
        late = mine[sources:][part]
        return pl.pallas_call(
            functools.partial(join_kernel, (sources - far) * tall + part.start * lanes),
            out_shape=shapes[sources : 2 * sources][part],
            in_specs=[vmem] * (len(late) + 2),
            out_specs=[vmem] * len(late),
            compiler_params=LIMIT,
            name="join",
        )(after, got[1], *late)

    def place(blocks, extra, h):
        shapes = [padded if dt else share for dt, dr in owners] + [mark]
        if h:
            shapes = [share] * len(owners)
        return pl.pallas_call(
            functools.partial(place_kernel, sources, owners, h == 0),
            out_shape=shapes,
            in_specs=[vmem] * (sources + len(extra)),
            out_specs=[vmem] * len(shapes),
            compiler_params=LIMIT,
            name="place",
        )(*blocks, *extra)

    def share_out(part, owner):
        dt, dr = owner
        if not (dt or dr):
            return part
        route = [
            (t * cores + r, (t + dt) % tilts * cores + (r + dr) % cores)
            for t in range(tilts)
            for r in range(cores)
        ]
        return lax.ppermute(part, ("tilt", "rep"), route)

    joined = []
    for k in range(far):
        joined += join(first[k], slice(k, k + 1))
    joined += join(first[0], slice(far, sources))
    second = [send(block, k) if k else block for block, k in zip(joined, shifts)]
    *parts, marks = place(first, [], 0)
    extra = [share_out(part, owner) for part, owner in zip(parts, owners)]
    held = [part for part, (dt, dr) in zip(extra, owners) if dr and not dt]
    late = place(second, [marks, *held], 1)
    extra += [share_out(part, owner) for part, owner in zip(late, owners)]
    return pl.pallas_call(
        functools.partial(sum_kernel, owners),
        out_shape=jax.ShapeDtypeStruct((each, cores, block_rows, block_cols), f32),
        in_specs=[vmem] * len(extra),
        out_specs=vmem,
        compiler_params=LIMIT,
        name="total",
    )(*extra)


def solution(mesh):
    in_specs = (
        P(("groups", "tilt"), None, None, "slab", None),
        P(),
        P(),
        P(("groups", "tilt"), ("slab", "rep"), None, None, None),
        P(("groups", "tilt"), ("slab", "rep")),
        P(None, ("groups", "tilt"), "slab", None, None),
        P(("groups", "tilt"), "slab", None),
        P(),
        P(),
    )
    out_specs = P(("groups", "slab", "tilt", "rep"), None, None, None)
    return jax.shard_map(
        on_device, mesh=mesh, in_specs=in_specs, out_specs=out_specs, check_vma=False
    )
```
